128 devices in a mesh: gx: 8 (over z, x_hi), gy: 16 (over x_lo, y, core).
Axes of the slice: x: 4 (x_hi: 2, x_lo: 2; x = x_hi * 2 + x_lo), y: 4, z: 4, core: 2. Of those that a mesh axis runs over, the one named last changes fastest.
Arguments:
- source_now: float32 [256, 128, 128], P('gx', 'gy'), may hold values from -6 to 6
- source_next: float32 [256, 128, 128], P('gx', 'gy'), may hold values from -6 to 6
- receiver_now: float32 [256, 128, 128], P('gx', 'gy'), may hold values from -1.5 to 1.5
- receiver_next: float32 [256, 128, 128], P('gx', 'gy'), may hold values from -1.5 to 1.5
- courant: float32 [256, 128, 128], P('gx', 'gy'), may hold values from 0.05 to 0.25
- source_cell: int32 [1], replicated, may hold values from 0 to 4194303
- wavelet: float32 [2], replicated, may hold values from -24 to 24
- receiver_cells: int32 [32768], P(('gx', 'gy')), may hold values from 0 to 4194303
- receiver_traces: float32 [2, 32768], P(None, ('gx', 'gy')), may hold values from -80 to 80
- strip_depth: int32 [128, 256], P('gy', 'gx'), may hold values from 0 to 124
- strip_values: float32 [2, 4, 128, 256], P(None, None, 'gy', 'gx'), may hold values from -6 to 6
Outputs:
- source_field: float32 [256, 128, 128], P('gx', 'gy')
- receiver_field: float32 [256, 128, 128], P('gx', 'gy')
- angle_image: float32 [32, 64, 1024], P('gy', 'gx')
The draws below stay inside these ranges and needn't reach their ends.
All inputs are finite; a program needn't handle non-finite values.
Results may differ from the reference program's by a relative error of at most 0.00011.
Values sent between devices are 32-bit elements; how exact they have to be, the bound alone decides.
No kernel may reach another device: no remote copies, remote signals or barrier semaphores. Data moves between devices by JAX's collectives and lax.ppermute only.
A program may use at most 128 MiB of HBM per device.

```python
import math
import jax
import jax.numpy as jnp
from jax import lax

STEPS = 2
NX = 256
NY = 128
NZ = 128
NXI = 64
NYI = 32
NZI = 32
NREC = 32768


def place_ends(entries, own_key, least, largest):
    spot = [jax.random.randint(jax.random.fold_in(own_key, axis), (), 0, length) for axis, length in enumerate(entries.shape)]
    widest = entries.shape.index(max(entries.shape))
    next_to = spot[:widest] + [(spot[widest] + 1) % entries.shape[widest]] + spot[widest + 1:]
    return entries.at[tuple(spot)].set(least).at[tuple(next_to)].set(largest)


def level_of(stream_key, shape, pieces, low, top_value):
    level, own = 1.0, jax.random.fold_in(stream_key, 6)
    for dim, shards_of in pieces:
        draws = jnp.exp(jax.random.uniform(jax.random.fold_in(own, dim), (shards_of,), jnp.float32, low / len(pieces), top_value / len(pieces)))
        level = level * jnp.repeat(draws, shape[dim] // shards_of).reshape([-1 if axis == dim else 1 for axis in range(len(shape))])
    return level


def normal_values(rng, dims, deviation, bound, pieces=(), kind=jnp.bfloat16):
    array = jax.random.normal(rng, dims, jnp.float32) * deviation
    if len(pieces) > 0:
        array = level_of(rng, dims, pieces, -0.22, 0.18) * array
    return jnp.clip(array, min=-bound, max=bound).astype(kind)


def setup_inputs(seed: int = 0) -> dict:
    streams_of = jax.random.split(jax.random.key(seed), 12)
    return {
        "source_now": normal_values(streams_of[0], (NX, NY, NZ), 1.0, 6.0, ((0, 8), (1, 16)), jnp.float32),
        "source_next": normal_values(streams_of[1], (NX, NY, NZ), 1.0, 6.0, ((0, 8), (1, 16)), jnp.float32),
        "receiver_now": normal_values(streams_of[2], (NX, NY, NZ), 0.25, 1.5, ((0, 8), (1, 16)), jnp.float32),
        "receiver_next": normal_values(streams_of[3], (NX, NY, NZ), 0.25, 1.5, ((0, 8), (1, 16)), jnp.float32),
        "courant": jnp.clip(jnp.exp(math.log(0.25) - 1.609438 * jax.random.uniform(streams_of[4], (NX, NY, NZ), jnp.float32) ** level_of(streams_of[4], (NX, NY, NZ), ((0, 8), (1, 16)), -0.2, 0.2)), 0.05, 0.25),
        "source_cell": jax.random.randint(streams_of[5], (1,), 0, NX * NY * NZ).astype(jnp.int32),
        "wavelet": normal_values(streams_of[6], (STEPS,), 8.0, 24.0, (), jnp.float32),
        "receiver_cells": place_ends(jax.random.randint(streams_of[7], (NREC,), 0, NX * NY * NZ), jax.random.fold_in(streams_of[7], 1), 0, (NX * NY * NZ) - 1).astype(jnp.int32),
        "receiver_traces": normal_values(streams_of[8], (STEPS, NREC), 20.0, 80.0, ((1, 128),), jnp.float32),
        "strip_depth": place_ends(jax.random.randint(streams_of[9], (NY, NX), 0, NZ - 3), jax.random.fold_in(streams_of[9], 1), 0, (NZ - 3) - 1).astype(jnp.int32),
        "strip_values": normal_values(streams_of[10], (STEPS, 4, NY, NX), 1.0, 6.0, ((2, 16), (3, 8)), jnp.float32),
    }


COEFS = (-205.0 / 72.0, 8.0 / 5.0, -1.0 / 5.0, 8.0 / 315.0, -1.0 / 560.0)
SLOPES = [math.tan(math.pi * (-60.0 + 120.0 * (angle + 0.5) / 32.0) / 180.0) for angle in range(32)]


def laplacian(padded):
    size_x = padded.shape[-3] - 8
    size_y = padded.shape[-2] - 8
    size_z = padded.shape[-1] - 8
    core = padded[..., 4:4 + size_x, 4:4 + size_y, 4:4 + size_z]
    total = 3.0 * COEFS[0] * core
    for reach in range(1, 5):
        pairs = padded[..., 4 + reach:4 + reach + size_x, 4:4 + size_y, 4:4 + size_z] + padded[..., 4 - reach:4 - reach + size_x, 4:4 + size_y, 4:4 + size_z]
        pairs = pairs + padded[..., 4:4 + size_x, 4 + reach:4 + reach + size_y, 4:4 + size_z] + padded[..., 4:4 + size_x, 4 - reach:4 - reach + size_y, 4:4 + size_z]
        pairs = pairs + padded[..., 4:4 + size_x, 4:4 + size_y, 4 + reach:4 + reach + size_z] + padded[..., 4:4 + size_x, 4:4 + size_y, 4 - reach:4 - reach + size_z]
        total = total + COEFS[reach] * pairs
    return total


def slant_table(depth_points):
    offsets = jnp.arange(33, dtype=jnp.int32).astype(jnp.float32) - 16.0
    slopes = jnp.asarray(SLOPES, dtype=jnp.float32)
    depths = jnp.arange(depth_points, dtype=jnp.int32).astype(jnp.float32)
    where_at = depths[None, None, :] + offsets[:, None, None] * slopes[None, :, None] / 4.0
    lower = jnp.floor(where_at)
    frac = where_at - lower
    lower_index = lower.astype(jnp.int32)
    rows = jnp.arange(depth_points, dtype=jnp.int32)[None, :, None, None]
    low_hit = rows == lower_index[:, None, :, :]
    high_hit = rows == (lower_index + 1)[:, None, :, :]
    zero = jnp.zeros((), jnp.float32)
    table = jnp.where(low_hit, (1.0 - frac)[:, None, :, :], zero) + jnp.where(high_hit, frac[:, None, :, :], zero)
    return table.astype(jnp.float32).reshape(33 * depth_points, 32 * depth_points)


def correlate(fields):
    count_x = fields.shape[1] - 32
    terms = []
    for offset in range(-16, 17):
        left = fields[0, 16 - offset:16 - offset + count_x:4]
        right = fields[1, 16 + offset:16 + offset + count_x:4]
        terms.append(left * right)
    return jnp.stack(terms, axis=2)


def reference(source_now, source_next, receiver_now, receiver_next, courant, source_cell, wavelet, receiver_cells, receiver_traces, strip_depth, strip_values):
    shape = source_now.shape
    courant_flat = courant.reshape(-1)
    depth_index = jnp.arange(NZ, dtype=jnp.int32)
    relative = depth_index[None, None, :] - jnp.transpose(strip_depth)[:, :, None]
    inside = (relative >= 0) & (relative < 4)
    lag_image = jnp.zeros((NXI, NYI, 33, NZI), source_now.dtype)
    for step in range(STEPS):
        fields = jnp.stack([source_now, receiver_now])
        curvature = laplacian(jnp.pad(fields, ((0, 0), (4, 4), (4, 4), (4, 4))))
        source_new = 2.0 * source_now - source_next + courant * curvature[0]
        source_new = source_new.reshape(-1).at[source_cell].add(-courant_flat[source_cell] * wavelet[step]).reshape(shape)
        strip = strip_values[step]
        filled = jnp.zeros_like(source_new)
        for layer in range(4):
            filled = filled + jnp.where(relative == layer, jnp.transpose(strip[layer])[:, :, None], 0.0)
        source_new = jnp.where(inside, filled, source_new)
        receiver_new = 2.0 * receiver_now - receiver_next + courant * curvature[1]
        receiver_new = receiver_new.reshape(-1).at[receiver_cells].add(courant_flat[receiver_cells] * receiver_traces[step]).reshape(shape)
        sampled = jnp.stack([source_new, receiver_new])[:, :, ::4, ::4]
        widened = jnp.pad(sampled, ((0, 0), (16, 16), (0, 0), (0, 0)))
        lag_image = lag_image + correlate(widened)
        source_next, source_now = source_now, source_new
        receiver_next, receiver_now = receiver_now, receiver_new
    table = slant_table(NZI).astype(lag_image.dtype)
    angles = jnp.dot(lag_image.reshape(NXI * NYI, 33 * NZI), table, precision=lax.Precision.HIGHEST, preferred_element_type=lag_image.dtype)
    angles = jnp.transpose(angles.reshape(NXI, NYI, 32, NZI), (2, 0, 1, 3)).reshape(32, NXI, NYI * NZI)
    return source_now, receiver_now, angles
```

```python
import math

import jax
import jax.numpy as jnp
import numpy as np
from jax import lax
from jax.experimental import pallas as pl
from jax.experimental.pallas import tpu as pltpu
from jax.sharding import PartitionSpec as P

COEFS = (-205.0 / 72.0, 8.0 / 5.0, -1.0 / 5.0, 8.0 / 315.0, -1.0 / 560.0)
SLOPES = np.array(
    [math.tan(math.pi * (-60.0 + 120.0 * (angle + 0.5) / 32.0) / 180.0) for angle in range(32)],
    dtype=np.float32,
)
GX, GY = 8, 16
TX, TY, TZ = 32, 8, 128
DEVICES = GX * GY
RECEIVERS = 256
SLOTS = 16
F32, BF16, I32 = jnp.float32, jnp.bfloat16, jnp.int32
VMEM_LIMIT = 24 * 1024 * 1024


def iota(shape, dim):
    return lax.broadcasted_iota(I32, shape, dim)


def halves(value):
    high = value.astype(BF16)
    return high, (value - high.astype(F32)).astype(BF16)


def dot_nt(left, right):
    return lax.dot_general(left, right, (((1,), (1,)), ((), ())), preferred_element_type=F32)


def routed(cells, traces, first_slot):
    x, y, z = cells >> 14, (cells >> 7) & 127, cells & 127
    tile_x, tile_y, in_x, in_y = x >> 5, y >> 3, x & 31, y & 7
    beside_y = jnp.where(in_y < 4, tile_y - 1, tile_y + 1)
    beside_x = jnp.where(in_x < 4, tile_x - 1, jnp.where(in_x >= 28, tile_x + 1, -1))
    to_y = jnp.where((beside_y >= 0) & (beside_y < GY), tile_x * GY + beside_y, -1)
    to_x = jnp.where((beside_x >= 0) & (beside_x < GX), beside_x * GY + tile_y, -1)
    rim_x = jnp.where(in_x < 4, in_x + 4, in_x - 28)
    classes = (
        (tile_x * GY + tile_y, (in_x * 8 + in_y) * 128 + z, 2),
        (to_y, (in_x * 8 + (in_y ^ 4)) * 128 + z, 1),
        (to_x, (rim_x * 8 + in_y) * 128 + z, 1),
    )
    earlier = jnp.where(
        iota((RECEIVERS, RECEIVERS), 0) < iota((RECEIVERS, RECEIVERS), 1), 1.0, 0.0
    ).astype(BF16)
    device = iota((DEVICES, RECEIVERS), 0)
    slot = iota((SLOTS, RECEIVERS), 0).astype(F32) + first_slot.astype(F32)
    hits, kept, last_rank, row = [], [], None, 0
    for target, place, steps in classes:
        hit = jnp.where(device == target, 1.0, 0.0)
        before = jnp.dot(hit.astype(BF16), earlier, preferred_element_type=F32)
        rank = jnp.sum(hit * before, axis=0, keepdims=True)
        last_rank = rank if last_rank is None else jnp.maximum(last_rank, rank)
        mine = slot == rank
        rows = [jnp.where(mine, place.astype(F32), 0.0)]
        rows += [jnp.where(mine, traces[s : s + 1], 0.0) for s in range(steps)]
        size = SLOTS * len(rows)
        above = [jnp.zeros((row, RECEIVERS), F32)] if row else []
        below = [jnp.zeros((128 - row - size, RECEIVERS), F32)]
        kept.append(jnp.concatenate(above + rows + below, axis=0))
        hits.append(hit.astype(BF16))
        row += size
    hits = jnp.concatenate(hits, axis=1)
    high, low = halves(jnp.concatenate(kept, axis=1))
    sent = dot_nt(hits, high) + dot_nt(hits, low)
    rounds = (jnp.max(last_rank, axis=1, keepdims=True).astype(I32) // SLOTS + 1).astype(F32)
    return jnp.where(iota((DEVICES, 128), 1) >= row, rounds, sent)


def route_kernel(first_ref, cells_ref, traces_ref, sent_ref):
    sent_ref[:, 0, :] = routed(cells_ref[...], traces_ref[...], first_ref[0])


def collected(got):
    rows = got.T
    sums, row = [], 0
    for columns, steps in ((TX * 8, 2), (TX * 8, 1), (64, 1)):
        cell = rows[row : row + SLOTS].astype(I32)
        column, depth = cell >> 7, cell & 127
        at = iota((columns, DEVICES), 0)
        down = iota((TZ, DEVICES), 0)
        one, parts = [], [[] for _ in range(2 * steps)]
        for k in range(SLOTS):
            one.append(jnp.where(at == column[k : k + 1], 1.0, 0.0).astype(BF16))
            same = down == depth[k : k + 1]
            for s in range(steps):
                value = rows[row + (s + 1) * SLOTS + k : row + (s + 1) * SLOTS + k + 1]
                high = value.astype(BF16).astype(F32)
                parts[2 * s].append(jnp.where(same, high, 0.0).astype(BF16))
                parts[2 * s + 1].append(jnp.where(same, value - high, 0.0).astype(BF16))
        one = jnp.concatenate(one, axis=1)
        for s in range(steps):
            high = jnp.concatenate(parts[2 * s], axis=1)
            low = jnp.concatenate(parts[2 * s + 1], axis=1)
            sums.append(dot_nt(one, high) + dot_nt(one, low))
        row += SLOTS * (steps + 1)
    return sums


def collect_kernel(got_ref, own_ref, rim_y_ref, rim_x_ref, rounds_ref):
    got = got_ref[:, 0, :]
    own_0, own_1, rim_y, rim_x = collected(got)
    own_ref[0] = own_0.reshape(TX, 8, 128)
    own_ref[1] = own_1.reshape(TX, 8, 128)
    rim_y_ref[...] = rim_y.reshape(TX, 8, 128)
    rim_x_ref[...] = rim_x.reshape(8, 8, 128)
    rounds_ref[0] = jnp.max(got[:, 112:128]).astype(I32)


def collect_more_kernel(got_ref, own_in, rim_y_in, rim_x_in, own_ref, rim_y_ref, rim_x_ref):
    own_0, own_1, rim_y, rim_x = collected(got_ref[:, 0, :])
    own_ref[0] = own_in[0] + own_0.reshape(TX, 8, 128)
    own_ref[1] = own_in[1] + own_1.reshape(TX, 8, 128)
    rim_y_ref[...] = rim_y_in[...] + rim_y.reshape(TX, 8, 128)
    rim_x_ref[...] = rim_x_in[...] + rim_x.reshape(8, 8, 128)


def strip_values_tile(values, step, rows):
    return jnp.concatenate([values[step, layer][rows] for layer in range(4)], axis=1)


def wide(depth):
    return jnp.concatenate([depth, jnp.zeros((depth.shape[0], 96), depth.dtype)], axis=1)


def pack_y_kernel(
    cells_ref, traces_ref, s0, r0, sm, rm, c, depth, values, sent_ref, up_ref, down_ref
):
    for ref, rows in ((up_ref, slice(4, 8)), (down_ref, slice(0, 4))):
        ref[0:32] = s0[...]
        ref[32:64] = r0[...]
        ref[64:96, 0:4] = sm[:, rows]
        ref[64:96, 4:8] = rm[:, rows]
        ref[96:112, 0:4] = c[0:16, rows]
        ref[96:112, 4:8] = c[16:32, rows]
        ref[112, 0:4] = strip_values_tile(values, 0, rows)
        ref[112, 4:8] = wide(depth[rows].astype(F32))
    sent_ref[:, 0, :] = routed(cells_ref[...], traces_ref[...], jnp.int32(0))


def pack_x_kernel(
    place, s0, r0, sm, rm, c, depth, values, before, after, up_ref, down_ref
):
    keep_before = jnp.where(place[1] > 0, 1.0, 0.0)
    keep_after = jnp.where(place[1] < GY - 1, 1.0, 0.0)
    near = strip_values_tile(values, 0, slice(0, 8))
    depths = wide(depth[...].astype(F32))
    for ref, deep, rim in ((up_ref, 24, 28), (down_ref, 0, 0)):
        for f, field in ((0, s0), (1, r0)):
            ref[8 * f : 8 * f + 8] = field[deep : deep + 8]
            start = 16 + 4 * f
            ref[start : start + 4, 0:4] = before[32 * f + rim : 32 * f + rim + 4, 4:8] * keep_before
            ref[start : start + 4, 4:8] = after[32 * f + rim : 32 * f + rim + 4, 0:4] * keep_after
        ref[24:28] = sm[rim : rim + 4]
        ref[28:32] = rm[rim : rim + 4]
        ref[32:36] = c[rim : rim + 4]
        ref[36] = near
        ref[37] = depths


def depth_pairs(tile, reach):
    lane = iota((8, 128), 1)
    below = jnp.where(lane < 128 - reach, pltpu.roll(tile, 128 - reach, 1), 0.0)
    above = jnp.where(lane >= reach, pltpu.roll(tile, reach, 1), 0.0)
    return below + above


def curvature(ref, f, x, row):
    tile = ref[f, x, row : row + 8]
    total = (3.0 * COEFS[0]) * tile
    for reach in range(1, 5):
        pairs = ref[f, x + reach, row : row + 8] + ref[f, x - reach, row : row + 8]
        pairs = pairs + ref[f, x, row + reach : row + reach + 8]
        pairs = pairs + ref[f, x, row - reach : row - reach + 8]
        pairs = pairs + depth_pairs(tile, reach)
        total = total + COEFS[reach] * pairs
    return tile, total


def overwritten(tile, depths, values, lane_start):
    lane = iota((8, 128), 1)
    column = jnp.full((8, 128), lane_start, I32)
    relative = lane - jnp.take_along_axis(depths, column, axis=1)
    fill = jnp.take_along_axis(values, (relative & 3) * 32 + column, axis=1)
    return jnp.where((relative >= 0) & (relative < 4), fill, tile)


def steps_kernel(
    place, source_cell, wavelet,
    s0, r0, sm, rm, c, depth, values, before, after, left, right, own, rim_y, rim_x,
    s_out, r_out, near_ref, up_ref, down_ref,
    e_ref, m_ref, o_ref, d_ref, v_ref, sub_ref,
):
    keep_before = jnp.where(place[1] > 0, 1.0, 0.0)
    keep_after = jnp.where(place[1] < GY - 1, 1.0, 0.0)
    keep_left = jnp.where(place[0] > 0, 1.0, 0.0)
    keep_right = jnp.where(place[0] < GX - 1, 1.0, 0.0)
    for f, field in ((0, s0), (1, r0)):
        e_ref[f, 8:40, 12:20] = field[...]
        e_ref[f, 8:40, 4:12] = before[32 * f : 32 * f + 32] * keep_before
        e_ref[f, 8:40, 20:28] = after[32 * f : 32 * f + 32] * keep_after
        for ref, keep, deep, rim in ((left, keep_left, 0, 4), (right, keep_right, 40, 40)):
            e_ref[f, deep : deep + 8, 12:20] = ref[8 * f : 8 * f + 8] * keep
            corner = 16 + 4 * f
            e_ref[f, rim : rim + 4, 8:12] = ref[corner : corner + 4, 0:4] * keep
            e_ref[f, rim : rim + 4, 20:24] = ref[corner : corner + 4, 4:8] * keep
    for k, field in ((0, sm), (1, rm), (2, c)):
        m_ref[k, 4:36, 4:12] = field[...]
        m_ref[k, 0:4, 4:12] = left[24 + 4 * k : 28 + 4 * k] * keep_left
        m_ref[k, 36:40, 4:12] = right[24 + 4 * k : 28 + 4 * k] * keep_right
    for ref, keep, rows in ((before, keep_before, slice(0, 4)), (after, keep_after, slice(12, 16))):
        m_ref[0, 4:36, rows] = ref[64:96, 0:4] * keep
        m_ref[1, 4:36, rows] = ref[64:96, 4:8] * keep
        m_ref[2, 4:20, rows] = ref[96:112, 0:4] * keep
        m_ref[2, 20:36, rows] = ref[96:112, 4:8] * keep
    m_ref[3, 4:36, 4:12] = own[0]
    m_ref[3, 4:36, 0:4] = rim_y[:, 0:4]
    m_ref[3, 4:36, 12:16] = rim_y[:, 4:8]
    m_ref[3, 0:4, 4:12] = rim_x[0:4]
    m_ref[3, 36:40, 4:12] = rim_x[4:8]
    near_values = strip_values_tile(values, 0, slice(0, 8))
    near_depth = wide(depth[...])
    v_ref[1, 4:12] = near_values
    d_ref[1, 4:12] = near_depth
    for ref, keep, rows in ((before, keep_before, slice(0, 4)), (after, keep_after, slice(12, 16))):
        v_ref[1, rows] = ref[112, 0:4] * keep
        d_ref[1, rows] = (ref[112, 4:8] * keep).astype(I32)
    for k, ref, keep in ((0, left, keep_left), (2, right, keep_right)):
        v_ref[k] = jnp.zeros((16, 128), F32)
        d_ref[k] = jnp.zeros((16, 128), I32)
        v_ref[k, 4:12] = ref[36] * keep
        d_ref[k, 4:12] = (ref[37] * keep).astype(I32)
    cell = source_cell[0]
    source_x = (cell >> 14) - place[0] * TX
    source_y = ((cell >> 7) & 127) - place[1] * TY
    source_z = cell & 127
    lane, sublane = iota((8, 128), 1), iota((8, 128), 0)

    def first(i, carry):
        part = jnp.where(i >= 4, 1, 0) + jnp.where(i >= 36, 1, 0)
        column = jnp.where(i < 4, i + 28, jnp.where(i < 36, i - 4, i - 36))
        amount = jnp.where(i - 4 == source_x, wavelet[0], 0.0)
        for t in range(2):
            rows = slice(8 * t, 8 * t + 8)
            at_source = (lane == source_z) & (sublane + (8 * t - 4) == source_y)
            courant = m_ref[2, i, rows]
            now, total = curvature(e_ref, 0, i + 4, 8 + 8 * t)
            total = total - jnp.where(at_source, amount, 0.0)
            new = 2.0 * now - m_ref[0, i, rows] + courant * total
            new = overwritten(new, d_ref[part, rows], v_ref[part, rows], column)
            o_ref[0, i, 4 + 8 * t : 12 + 8 * t] = new
            sub_ref[0, t, pl.ds(i, 1)] = new[4 - 4 * t : 5 - 4 * t]
            now, total = curvature(e_ref, 1, i + 4, 8 + 8 * t)
            new = 2.0 * now - m_ref[1, i, rows] + courant * (total + m_ref[3, i, rows])
            o_ref[1, i, 4 + 8 * t : 12 + 8 * t] = new
            sub_ref[2, t, pl.ds(i, 1)] = new[4 - 4 * t : 5 - 4 * t]
        return carry

    lax.fori_loop(0, 40, first, 0)
    late_values = strip_values_tile(values, 1, slice(0, 8))
    at_source = (lane == source_z) & (sublane == source_y)

    def second(x, carry):
        amount = jnp.where(x == source_x, wavelet[1], 0.0)
        now, total = curvature(o_ref, 0, x + 4, 8)
        total = total - jnp.where(at_source, amount, 0.0)
        new = 2.0 * now - s0[x] + c[x] * total
        new = overwritten(new, near_depth, late_values, x)
        s_out[x] = new
        for j in range(2):
            sub_ref[1, j, pl.ds(x + 4, 1)] = new[4 * j : 4 * j + 1]
        now, total = curvature(o_ref, 1, x + 4, 8)
        new = 2.0 * now - r0[x] + c[x] * (total + own[1, x])
        r_out[x] = new
        for j in range(2):
            sub_ref[3, j, pl.ds(x + 4, 1)] = new[4 * j : 4 * j + 1]
        return carry

    lax.fori_loop(0, 32, second, 0)
    z, to = iota((TZ, 128), 0), iota((TZ, 128), 1)
    for k in range(4):
        total = None
        for j in range(2):
            pick = jnp.where((z & 3 == 0) & (to == (z >> 2) + (16 + 64 * j)), 1.0, 0.0)
            part = jnp.dot(
                sub_ref[k, j, 4:36], pick, precision=lax.Precision.HIGHEST, preferred_element_type=F32
            )
            total = part if total is None else total + part
        near_ref[k] = total
        up_ref[k] = total[16:32]
        down_ref[k] = total[0:16]


def angles_kernel(place, near, left, right, out_ref, g_ref):
    keep_left = jnp.where(place[0] > 0, 1.0, 0.0)
    keep_right = jnp.where(place[0] < GX - 1, 1.0, 0.0)
    for k in range(4):
        g_ref[k, 0:16] = left[k] * keep_left
        g_ref[k, 16:48] = near[k]
        g_ref[k, 48:64] = right[k] * keep_right
    sums = [None] * 32
    for lag in range(-16, 17):
        product = None
        for step in range(2):
            source = g_ref[step, pl.ds(16 - lag, 8, stride=4)]
            receiver = g_ref[2 + step, pl.ds(16 + lag, 8, stride=4)]
            part = source * receiver
            product = part if product is None else product + part
        shifted = {}

        def shift(amount):
            if amount not in shifted:
                shifted[amount] = product if amount == 0 else pltpu.roll(product, -amount % 128, 1)
            return shifted[amount]

        for a in range(32):
            move = np.float32(lag) * SLOPES[a] / np.float32(4.0)
            low = np.floor(move)
            frac = float(move - low)
            term = shift(int(low)) * (1.0 - frac)
            if frac != 0.0:
                term = term + shift(int(low) + 1) * frac
            sums[a] = term if sums[a] is None else sums[a] + term
    lane = iota((8, 128), 1)
    for b in range(16):
        first, second = sums[2 * b], sums[2 * b + 1]
        packed = jnp.where(lane < 32, pltpu.roll(first, 112, 1), pltpu.roll(first, 80, 1))
        other = jnp.where(lane < 96, pltpu.roll(second, 48, 1), pltpu.roll(second, 16, 1))
        out_ref[b] = jnp.where(lane < 64, packed, other)


def arrange_kernel(got, out_ref):
    lane = iota((8, 128), 1)
    for t in range(8):
        even, odd = got[2 * t], got[2 * t + 1]
        out_ref[0, :, 128 * t : 128 * t + 128] = jnp.where(lane < 64, even, pltpu.roll(odd, 64, 1))
        out_ref[1, :, 128 * t : 128 * t + 128] = jnp.where(lane < 64, pltpu.roll(even, 64, 1), odd)


def call(kernel, outs, scalars, arrays, out_scalars=0, scratch=(), cost=None):
    smem, vmem = pl.BlockSpec(memory_space=pltpu.SMEM), pl.BlockSpec(memory_space=pltpu.VMEM)
    return pl.pallas_call(
        kernel,
        out_shape=[jax.ShapeDtypeStruct(shape, kind) for shape, kind in outs],
        in_specs=[smem] * len(scalars) + [vmem] * len(arrays),
        out_specs=[vmem] * (len(outs) - out_scalars) + [smem] * out_scalars,
        scratch_shapes=list(scratch),
        compiler_params=pltpu.CompilerParams(vmem_limit_bytes=VMEM_LIMIT),
        cost_estimate=cost,
    )(*scalars, *arrays)


def both_ways(to_next, to_last, axis):
    size = lax.axis_size(axis)
    from_last = lax.ppermute(to_next, axis, [(i, (i + 1) % size) for i in range(size)])
    from_next = lax.ppermute(to_last, axis, [((i + 1) % size, i) for i in range(size)])
    return from_last, from_next


def body(
    source_now,
    source_next,
    receiver_now,
    receiver_next,
    courant,
    source_cell,
    wavelet,
    receiver_cells,
    receiver_traces,
    strip_depth,
    strip_values,
):
    place = jnp.stack([lax.axis_index("gx"), lax.axis_index("gy")]).astype(I32)
    cells = receiver_cells.reshape(1, RECEIVERS)
    tile = (TX, TY, TZ)
    fields = (source_now, receiver_now, source_next, receiver_next, courant, strip_depth, strip_values)
    sent, up_y, down_y = call(
        pack_y_kernel,
        [((DEVICES, 1, 128), F32), ((113, 8, 128), F32), ((113, 8, 128), F32)],
        [], [cells, receiver_traces, *fields],
    )
    before, after = both_ways(up_y, down_y, "gy")
    got = lax.all_to_all(sent, ("gx", "gy"), 0, 0, tiled=True)
    up_x, down_x = call(
        pack_x_kernel, [((38, 8, 128), F32)] * 2, [place], [*fields, before, after]
    )
    left, right = both_ways(up_x, down_x, "gx")
    sums = [((2, *tile), F32), (tile, F32), ((8, 8, 128), F32)]
    own, rim_y, rim_x, rounds = call(
        collect_kernel, [*sums, ((1,), I32)], [], [got], out_scalars=1
    )

    def another(state):
        turn, *partial = state
        (more,) = call(
            route_kernel,
            [((DEVICES, 1, 128), F32)],
            [(turn * SLOTS).reshape(1)], [cells, receiver_traces],
        )
        more = lax.all_to_all(more, ("gx", "gy"), 0, 0, tiled=True)
        return (turn + 1, *call(collect_more_kernel, sums, [], [more, *partial]))

    _, own, rim_y, rim_x = lax.while_loop(
        lambda state: state[0] < rounds[0], another, (jnp.int32(1), own, rim_y, rim_x)
    )
    source_field, receiver_field, near, up, down = call(
        steps_kernel,
        [(tile, F32), (tile, F32), ((4, 32, 128), F32), ((4, 16, 128), F32), ((4, 16, 128), F32)],
        [place, source_cell, wavelet],
        [*fields, before, after, left, right, own, rim_y, rim_x],
        scratch=[
            pltpu.VMEM((2, 48, 32, 128), F32),
            pltpu.VMEM((4, 40, 16, 128), F32),
            pltpu.VMEM((2, 40, 24, 128), F32),
            pltpu.VMEM((3, 16, 128), I32),
            pltpu.VMEM((3, 16, 128), F32),
            pltpu.VMEM((4, 2, 40, 128), F32),
        ],
    )
    near_left, near_right = both_ways(up, down, "gx")
    (angles,) = call(
        angles_kernel, [((16, 8, 128), F32)], [place], [near, near_left, near_right],
        scratch=[pltpu.VMEM((4, 64, 128), F32)],
    )
    angles = lax.all_to_all(angles, "gy", 0, 0, tiled=True)
    (image,) = call(arrange_kernel, [((2, 8, 1024), F32)], [], [angles])
    return source_field, receiver_field, image


def solution(mesh):
    return jax.shard_map(
        body,
        mesh=mesh,
        in_specs=(
            P("gx", "gy", None),
            P("gx", "gy", None),
            P("gx", "gy", None),
            P("gx", "gy", None),
            P("gx", "gy", None),
            P(),
            P(),
            P(("gx", "gy")),
            P(None, ("gx", "gy")),
            P("gy", "gx"),
            P(None, None, "gy", "gx"),
        ),
        out_specs=(P("gx", "gy", None), P("gx", "gy", None), P("gy", "gx", None)),
        check_vma=False,
    )
```

```python
import math

import jax
import jax.numpy as jnp
import numpy as np
from jax import lax
from jax.experimental import pallas as pl
from jax.experimental.pallas import tpu as pltpu
from jax.sharding import PartitionSpec as P

COEFS = (-205.0 / 72.0, 8.0 / 5.0, -1.0 / 5.0, 8.0 / 315.0, -1.0 / 560.0)
SLOPES = np.array(
    [math.tan(math.pi * (-60.0 + 120.0 * (angle + 0.5) / 32.0) / 180.0) for angle in range(32)],
    dtype=np.float32,
)
GX, GY = 8, 16
TX, TY, TZ = 32, 8, 128
DEVICES = GX * GY
RECEIVERS = 256
SLOTS = 16
UNROLL = (10, 16)
F32, BF16, I32 = jnp.float32, jnp.bfloat16, jnp.int32
VMEM_LIMIT = 24 * 1024 * 1024


def iota(shape, dim):
    return lax.broadcasted_iota(I32, shape, dim)


def halves(value):
    high = value.astype(BF16)
    return high, (value - high.astype(F32)).astype(BF16)


def dot_nt(left, right):
    return lax.dot_general(left, right, (((1,), (1,)), ((), ())), preferred_element_type=F32)


def routed(cells, traces, first_slot):
    x, y, z = cells >> 14, (cells >> 7) & 127, cells & 127
    tile_x, tile_y, in_x, in_y = x >> 5, y >> 3, x & 31, y & 7
    beside_y = jnp.where(in_y < 4, tile_y - 1, tile_y + 1)
    beside_x = jnp.where(in_x < 4, tile_x - 1, jnp.where(in_x >= 28, tile_x + 1, -1))
    to_y = jnp.where((beside_y >= 0) & (beside_y < GY), tile_x * GY + beside_y, -1)
    to_x = jnp.where((beside_x >= 0) & (beside_x < GX), beside_x * GY + tile_y, -1)
    rim_x = jnp.where(in_x < 4, in_x + 4, in_x - 28)
    classes = (
        (tile_x * GY + tile_y, (in_x * 8 + in_y) * 128 + z, 2),
        (to_y, (in_x * 8 + (in_y ^ 4)) * 128 + z, 1),
        (to_x, (rim_x * 8 + in_y) * 128 + z, 1),
    )
    earlier = jnp.where(
        iota((RECEIVERS, RECEIVERS), 0) < iota((RECEIVERS, RECEIVERS), 1), 1.0, 0.0
    ).astype(BF16)
    device = iota((DEVICES, RECEIVERS), 0)
    slot = iota((SLOTS, RECEIVERS), 0).astype(F32) + first_slot.astype(F32)
    hits, kept, last_rank, row = [], [], None, 0
    for target, place, steps in classes:
        hit = jnp.where(device == target, 1.0, 0.0)
        before = jnp.dot(hit.astype(BF16), earlier, preferred_element_type=F32)
        rank = jnp.sum(hit * before, axis=0, keepdims=True)
        last_rank = rank if last_rank is None else jnp.maximum(last_rank, rank)
        mine = slot == rank
        rows = [jnp.where(mine, place.astype(F32), 0.0)]
        rows += [jnp.where(mine, traces[s : s + 1], 0.0) for s in range(steps)]
        size = SLOTS * len(rows)
        above = [jnp.zeros((row, RECEIVERS), F32)] if row else []
        below = [jnp.zeros((128 - row - size, RECEIVERS), F32)]
        kept.append(jnp.concatenate(above + rows + below, axis=0))
        hits.append(hit.astype(BF16))
        row += size
    hits = jnp.concatenate(hits, axis=1)
    high, low = halves(jnp.concatenate(kept, axis=1))
    sent = dot_nt(hits, high) + dot_nt(hits, low)
    rounds = (jnp.max(last_rank, axis=1, keepdims=True).astype(I32) // SLOTS + 1).astype(F32)
    return jnp.where(iota((DEVICES, 128), 1) >= row, rounds, sent)


def route_kernel(cells_ref, traces_ref, sent_ref):
    sent_ref[:, 0, :] = routed(cells_ref[...], traces_ref[...], jnp.int32(0))


def route_more_kernel(first_ref, cells, traces, sent_ref, cells_v, traces_v, sems):
    for copy in started([(cells, cells_v), (traces, traces_v)], sems):
        copy.wait()
    sent_ref[:, 0, :] = routed(cells_v[...], traces_v[...], first_ref[0])


def collected(got):
    rows = got.T
    sums, row = [], 0
    for columns, steps in ((TX * 8, 2), (TX * 8, 1), (64, 1)):
        cell = rows[row : row + SLOTS].astype(I32)
        column, depth = cell >> 7, cell & 127
        at = iota((columns, DEVICES), 0)
        down = iota((TZ, DEVICES), 0)
        one, parts = [], [[] for _ in range(2 * steps)]
        for k in range(SLOTS):
            one.append(jnp.where(at == column[k : k + 1], 1.0, 0.0).astype(BF16))
            same = down == depth[k : k + 1]
            for s in range(steps):
                value = rows[row + (s + 1) * SLOTS + k : row + (s + 1) * SLOTS + k + 1]
                high = value.astype(BF16).astype(F32)
                parts[2 * s].append(jnp.where(same, high, 0.0).astype(BF16))
                parts[2 * s + 1].append(jnp.where(same, value - high, 0.0).astype(BF16))
        one = jnp.concatenate(one, axis=1)
        for s in range(steps):
            high = jnp.concatenate(parts[2 * s], axis=1)
            low = jnp.concatenate(parts[2 * s + 1], axis=1)
            sums.append(dot_nt(one, high) + dot_nt(one, low))
        row += SLOTS * (steps + 1)
    return sums


def collect_kernel(got_ref, own_ref, rim_y_ref, rim_x_ref, rounds_ref):
    got = got_ref[:, 0, :]
    own_0, own_1, rim_y, rim_x = collected(got)
    own_ref[0] = own_0.reshape(TX, 8, 128)
    own_ref[1] = own_1.reshape(TX, 8, 128)
    rim_y_ref[...] = rim_y.reshape(TX, 8, 128)
    rim_x_ref[...] = rim_x.reshape(8, 8, 128)
    rounds_ref[0] = jnp.max(got[:, 112:128]).astype(I32)


def collect_more_kernel(got_ref, own_in, rim_y_in, rim_x_in, own_ref, rim_y_ref, rim_x_ref):
    own_0, own_1, rim_y, rim_x = collected(got_ref[:, 0, :])
    own_ref[0] = own_in[0] + own_0.reshape(TX, 8, 128)
    own_ref[1] = own_in[1] + own_1.reshape(TX, 8, 128)
    rim_y_ref[...] = rim_y_in[...] + rim_y.reshape(TX, 8, 128)
    rim_x_ref[...] = rim_x_in[...] + rim_x.reshape(8, 8, 128)


def strip_values_tile(values, step, rows):
    return jnp.concatenate([values[step, layer][rows] for layer in range(4)], axis=1)


def wide(depth):
    return jnp.concatenate([depth, jnp.zeros((depth.shape[0], 96), depth.dtype)], axis=1)


def started(copies, sems):
    copies = [pltpu.make_async_copy(*ends, sems.at[k]) for k, ends in enumerate(copies)]
    for copy in copies:
        copy.start()
    return copies


def pack_y_kernel(
    cells, traces, s0, r0, sm, rm, c, depth, values,
    up_ref, down_ref, cells_ref, traces_ref, sm_v, rm_v, c_v, depth_v, values_v, sems,
):
    copies = started(
        [
            (sm, sm_v), (rm, rm_v), (c, c_v), (depth, depth_v), (values, values_v),
            (s0, up_ref.at[0:32]), (r0, up_ref.at[32:64]), (s0, down_ref.at[0:32]), (r0, down_ref.at[32:64]),
            (cells, cells_ref), (traces, traces_ref),
        ],
        sems,
    )
    for copy in copies[:5]:
        copy.wait()
    for ref, rows in ((up_ref, slice(4, 8)), (down_ref, slice(0, 4))):
        ref[64:96, 0:4] = sm_v[:, rows]
        ref[64:96, 4:8] = rm_v[:, rows]
        ref[96:112, 0:4] = c_v[0:16, rows]
        ref[96:112, 4:8] = c_v[16:32, rows]
        ref[112, 0:4] = strip_values_tile(values_v, 0, rows)
        ref[112, 4:8] = wide(depth_v[rows].astype(F32))
    for copy in copies[5:]:
        copy.wait()


def own_place():
    return lax.axis_index("gx"), lax.axis_index("gy")


def pack_x_kernel(s0, r0, sm, rm, c, depth, values, before, after, got, up_ref, down_ref):
    place = own_place()
    keep_before = jnp.where(place[1] > 0, 1.0, 0.0)
    keep_after = jnp.where(place[1] < GY - 1, 1.0, 0.0)
    near = strip_values_tile(values, 0, slice(0, 8))
    depths = wide(depth[...].astype(F32))
    for ref, deep, rim in ((up_ref, 24, 28), (down_ref, 0, 0)):
        for f, field in ((0, s0), (1, r0)):
            ref[8 * f : 8 * f + 8] = field[deep : deep + 8]
            start = 16 + 4 * f
            ref[start : start + 4, 0:4] = before[32 * f + rim : 32 * f + rim + 4, 4:8] * keep_before
            ref[start : start + 4, 4:8] = after[32 * f + rim : 32 * f + rim + 4, 0:4] * keep_after
        ref[24:28] = sm[rim : rim + 4]
        ref[28:32] = rm[rim : rim + 4]
        ref[32:36] = c[rim : rim + 4]
        ref[36] = near
        ref[37] = depths


def depth_matrix():
    apart = jnp.abs(iota((TZ, TZ), 0) - iota((TZ, TZ), 1))
    weights = jnp.zeros((TZ, TZ), F32)
    for reach in range(1, 5):
        weights = jnp.where(apart == reach, COEFS[reach], weights)
    high, low = halves(weights)
    top = jnp.concatenate([high, low], axis=1)
    return jnp.concatenate([top, jnp.concatenate([high, jnp.zeros_like(low)], axis=1)], axis=0)


def depth_sums(rows, matrix):
    both = jnp.dot(jnp.concatenate(halves(rows), axis=1), matrix, preferred_element_type=F32)
    return both[:, :128] + both[:, 128:]


def curvature(ref, f, x, row, depth_sum):
    tile = ref[f, x, row : row + 8]
    total = (3.0 * COEFS[0]) * tile + depth_sum
    for reach in range(1, 5):
        pairs = ref[f, x + reach, row : row + 8] + ref[f, x - reach, row : row + 8]
        pairs = pairs + ref[f, x, row + reach : row + reach + 8]
        pairs = pairs + ref[f, x, row - reach : row - reach + 8]
        total = total + COEFS[reach] * pairs
    return tile, total


def overwritten(tile, depths, values, lane_start):
    lane = iota((8, 128), 1)
    column = jnp.full((8, 128), lane_start, I32)
    relative = lane - jnp.take_along_axis(depths, column, axis=1)
    fill = jnp.take_along_axis(values, (relative & 3) * 32 + column, axis=1)
    return jnp.where((relative >= 0) & (relative < 4), fill, tile)


def steps_kernel(
    source_cell, wavelet,
    s0, r0, sm, rm, c, depth, values, before, after, left, right, own, rim_y, rim_x,
    s_out, r_out, near_ref, up_ref, down_ref,
    e_ref, m_ref, o_ref, z_ref, d_ref, v_ref, sub_ref, cell_s, wavelet_s, sems,
):
    place = own_place()
    copies = started([(source_cell, cell_s), (wavelet, wavelet_s)], sems)
    keep_before = jnp.where(place[1] > 0, 1.0, 0.0)
    keep_after = jnp.where(place[1] < GY - 1, 1.0, 0.0)
    keep_left = jnp.where(place[0] > 0, 1.0, 0.0)
    keep_right = jnp.where(place[0] < GX - 1, 1.0, 0.0)
    for f, field in ((0, s0), (1, r0)):
        e_ref[f, 8:40, 12:20] = field[...]
        e_ref[f, 8:40, 4:12] = before[32 * f : 32 * f + 32] * keep_before
        e_ref[f, 8:40, 20:28] = after[32 * f : 32 * f + 32] * keep_after
        for ref, keep, deep, rim in ((left, keep_left, 0, 4), (right, keep_right, 40, 40)):
            e_ref[f, deep : deep + 8, 12:20] = ref[8 * f : 8 * f + 8] * keep
            corner = 16 + 4 * f
            e_ref[f, rim : rim + 4, 8:12] = ref[corner : corner + 4, 0:4] * keep
            e_ref[f, rim : rim + 4, 20:24] = ref[corner : corner + 4, 4:8] * keep
    for k, field in ((0, sm), (1, rm), (2, c)):
        m_ref[k, 4:36, 4:12] = field[...]
        m_ref[k, 0:4, 4:12] = left[24 + 4 * k : 28 + 4 * k] * keep_left
        m_ref[k, 36:40, 4:12] = right[24 + 4 * k : 28 + 4 * k] * keep_right
    for ref, keep, rows in ((before, keep_before, slice(0, 4)), (after, keep_after, slice(12, 16))):
        m_ref[0, 4:36, rows] = ref[64:96, 0:4] * keep
        m_ref[1, 4:36, rows] = ref[64:96, 4:8] * keep
        m_ref[2, 4:20, rows] = ref[96:112, 0:4] * keep
        m_ref[2, 20:36, rows] = ref[96:112, 4:8] * keep
    m_ref[3, 4:36, 4:12] = own[0]
    m_ref[3, 4:36, 0:4] = rim_y[:, 0:4]
    m_ref[3, 4:36, 12:16] = rim_y[:, 4:8]
    m_ref[3, 0:4, 4:12] = rim_x[0:4]
    m_ref[3, 36:40, 4:12] = rim_x[4:8]
    near_values = strip_values_tile(values, 0, slice(0, 8))
    near_depth = wide(depth[...])
    v_ref[1, 4:12] = near_values
    d_ref[1, 4:12] = near_depth
    for ref, keep, rows in ((before, keep_before, slice(0, 4)), (after, keep_after, slice(12, 16))):
        v_ref[1, rows] = ref[112, 0:4] * keep
        d_ref[1, rows] = (ref[112, 4:8] * keep).astype(I32)
    for k, ref, keep in ((0, left, keep_left), (2, right, keep_right)):
        v_ref[k] = jnp.zeros((16, 128), F32)
        d_ref[k] = jnp.zeros((16, 128), I32)
        v_ref[k, 4:12] = ref[36] * keep
        d_ref[k, 4:12] = (ref[37] * keep).astype(I32)
    for copy in copies:
        copy.wait()
    cell = cell_s[0]
    source_x = (cell >> 14) - place[0] * TX
    source_y = ((cell >> 7) & 127) - place[1] * TY
    source_z = cell & 127
    lane, sublane = iota((8, 128), 1), iota((8, 128), 0)

    matrix = depth_matrix()
    for f in range(2):
        rows = e_ref[f, 4:44, 8:24].reshape(640, 128)
        z_ref[f] = depth_sums(rows, matrix).reshape(40, 16, 128)

    def first(i, carry):
        part = jnp.where(i >= 4, 1, 0) + jnp.where(i >= 36, 1, 0)
        column = jnp.where(i < 4, i + 28, jnp.where(i < 36, i - 4, i - 36))
        amount = jnp.where(i - 4 == source_x, wavelet_s[0], 0.0)
        for t in range(2):
            rows = slice(8 * t, 8 * t + 8)
            at_source = (lane == source_z) & (sublane + (8 * t - 4) == source_y)
            courant = m_ref[2, i, rows]
            now, total = curvature(e_ref, 0, i + 4, 8 + 8 * t, z_ref[0, i, rows])
            total = total - jnp.where(at_source, amount, 0.0)
            new = 2.0 * now - m_ref[0, i, rows] + courant * total
            new = overwritten(new, d_ref[part, rows], v_ref[part, rows], column)
            o_ref[0, i, 4 + 8 * t : 12 + 8 * t] = new
            sub_ref[0, t, pl.ds(i, 1)] = new[4 - 4 * t : 5 - 4 * t]
            now, total = curvature(e_ref, 1, i + 4, 8 + 8 * t, z_ref[1, i, rows])
            new = 2.0 * now - m_ref[1, i, rows] + courant * (total + m_ref[3, i, rows])
            o_ref[1, i, 4 + 8 * t : 12 + 8 * t] = new
            sub_ref[2, t, pl.ds(i, 1)] = new[4 - 4 * t : 5 - 4 * t]
        return carry

    lax.fori_loop(0, 40, first, 0, unroll=UNROLL[0])
    for f in range(2):
        rows = o_ref[f, 4:36, 8:16].reshape(256, 128)
        z_ref[f, 0:32, 0:8] = depth_sums(rows, matrix).reshape(32, 8, 128)
    late_values = strip_values_tile(values, 1, slice(0, 8))
    at_source = (lane == source_z) & (sublane == source_y)

    def second(x, carry):
        amount = jnp.where(x == source_x, wavelet_s[1], 0.0)
        now, total = curvature(o_ref, 0, x + 4, 8, z_ref[0, x, 0:8])
        total = total - jnp.where(at_source, amount, 0.0)
        new = 2.0 * now - s0[x] + c[x] * total
        new = overwritten(new, near_depth, late_values, x)
        s_out[x] = new
        for j in range(2):
            sub_ref[1, j, pl.ds(x + 4, 1)] = new[4 * j : 4 * j + 1]
        now, total = curvature(o_ref, 1, x + 4, 8, z_ref[1, x, 0:8])
        new = 2.0 * now - r0[x] + c[x] * (total + own[1, x])
        r_out[x] = new
        for j in range(2):
            sub_ref[3, j, pl.ds(x + 4, 1)] = new[4 * j : 4 * j + 1]
        return carry

    lax.fori_loop(0, 32, second, 0, unroll=UNROLL[1])
    z, to = iota((TZ, 128), 0), iota((TZ, 128), 1)
    for k in range(4):
        total = None
        for j in range(2):
            pick = jnp.where((z & 3 == 0) & (to == (z >> 2) + (16 + 64 * j)), 1.0, 0.0)
            part = jnp.dot(
                sub_ref[k, j, 4:36], pick, precision=lax.Precision.HIGHEST, preferred_element_type=F32
            )
            total = part if total is None else total + part
        near_ref[k] = total
        up_ref[k] = total[16:32]
        down_ref[k] = total[0:16]


def angles_kernel(near, left, right, out_ref, g_ref):
    place = own_place()
    keep_left = jnp.where(place[0] > 0, 1.0, 0.0)
    keep_right = jnp.where(place[0] < GX - 1, 1.0, 0.0)
    for k in range(4):
        g_ref[k, 0:16] = left[k] * keep_left
        g_ref[k, 16:48] = near[k]
        g_ref[k, 48:64] = right[k] * keep_right
    sums = [None] * 32
    for lag in range(-16, 17):
        product = None
        for step in range(2):
            source = g_ref[step, pl.ds(16 - lag, 8, stride=4)]
            receiver = g_ref[2 + step, pl.ds(16 + lag, 8, stride=4)]
            part = source * receiver
            product = part if product is None else product + part
        shifted = {}

        def shift(amount):
            if amount not in shifted:
                shifted[amount] = product if amount == 0 else pltpu.roll(product, -amount % 128, 1)
            return shifted[amount]

        for a in range(32):
            move = np.float32(lag) * SLOPES[a] / np.float32(4.0)
            low = np.floor(move)
            frac = float(move - low)
            term = shift(int(low)) * (1.0 - frac)
            if frac != 0.0:
                term = term + shift(int(low) + 1) * frac
            sums[a] = term if sums[a] is None else sums[a] + term
    lane = iota((8, 128), 1)
    for b in range(16):
        first, second = sums[2 * b], sums[2 * b + 1]
        packed = jnp.where(lane < 32, pltpu.roll(first, 112, 1), pltpu.roll(first, 80, 1))
        other = jnp.where(lane < 96, pltpu.roll(second, 48, 1), pltpu.roll(second, 16, 1))
        out_ref[b] = jnp.where(lane < 64, packed, other)


def arrange_kernel(got, out_ref):
    lane = iota((8, 128), 1)
    for t in range(8):
        even, odd = got[2 * t], got[2 * t + 1]
        out_ref[0, :, 128 * t : 128 * t + 128] = jnp.where(lane < 64, even, pltpu.roll(odd, 64, 1))
        out_ref[1, :, 128 * t : 128 * t + 128] = jnp.where(lane < 64, pltpu.roll(even, 64, 1), odd)


def call(kernel, outs, arrays, scalars=(), hbm=(), out_scalars=0, scratch=(), weight=0):
    smem, vmem = pl.BlockSpec(memory_space=pltpu.SMEM), pl.BlockSpec(memory_space=pltpu.VMEM)
    far = pl.BlockSpec(memory_space=pltpu.HBM)
    hbm = [
        pltpu.with_memory_space_constraint(array, pltpu.HBM) if array.size > 2 else array for array in hbm
    ]
    return pl.pallas_call(
        kernel,
        out_shape=[jax.ShapeDtypeStruct(shape, kind) for shape, kind in outs],
        in_specs=[smem] * len(scalars) + [far] * len(hbm) + [vmem] * len(arrays),
        out_specs=[vmem] * (len(outs) - out_scalars) + [smem] * out_scalars,
        scratch_shapes=list(scratch),
        compiler_params=pltpu.CompilerParams(vmem_limit_bytes=VMEM_LIMIT),
        cost_estimate=pl.CostEstimate(flops=0, bytes_accessed=weight, transcendentals=0) if weight else None,
    )(*scalars, *hbm, *arrays)


def both_ways(to_next, to_last, axis):
    size = lax.axis_size(axis)
    from_last = lax.ppermute(to_next, axis, [(i, (i + 1) % size) for i in range(size)])
    from_next = lax.ppermute(to_last, axis, [((i + 1) % size, i) for i in range(size)])
    return from_last, from_next


def body(
    source_now,
    source_next,
    receiver_now,
    receiver_next,
    courant,
    source_cell,
    wavelet,
    receiver_cells,
    receiver_traces,
    strip_depth,
    strip_values,
):
    cells = receiver_cells.reshape(1, RECEIVERS)
    tile, sent_shape = (TX, TY, TZ), ((DEVICES, 1, 128), F32)
    listed = [((1, RECEIVERS), I32), ((2, RECEIVERS), F32)]
    fields = (source_now, receiver_now, source_next, receiver_next, courant, strip_depth, strip_values)
    up_y, down_y, near_cells, near_traces = call(
        pack_y_kernel,
        [((113, 8, 128), F32), ((113, 8, 128), F32), *listed],
        [],
        hbm=[cells, receiver_traces, *fields],
        scratch=[pltpu.VMEM(tile, F32)] * 3
        + [pltpu.VMEM((8, 32), I32), pltpu.VMEM((2, 4, 8, 32), F32), pltpu.SemaphoreType.DMA((11,))],
    )
    before, after = both_ways(up_y, down_y, "gy")
    (sent,) = call(route_kernel, [sent_shape], [near_cells, near_traces], weight=20_000_000)
    got = lax.all_to_all(sent, ("gx", "gy"), 0, 0, tiled=True)
    up_x, down_x = call(pack_x_kernel, [((38, 8, 128), F32)] * 2, [*fields, before, after, got])
    left, right = both_ways(up_x, down_x, "gx")
    sums = [((2, *tile), F32), (tile, F32), ((8, 8, 128), F32)]
    own, rim_y, rim_x, rounds = call(collect_kernel, [*sums, ((1,), I32)], [got], out_scalars=1, weight=40_000_000)

    def another(state):
        turn, *partial = state
        (more,) = call(
            route_more_kernel,
            [sent_shape],
            [],
            scalars=[(turn * SLOTS).reshape(1)],
            hbm=[cells, receiver_traces],
            scratch=[pltpu.VMEM(*shape) for shape in listed] + [pltpu.SemaphoreType.DMA((2,))],
        )
        more = lax.all_to_all(more, ("gx", "gy"), 0, 0, tiled=True)
        return (turn + 1, *call(collect_more_kernel, sums, [more, *partial]))

    _, own, rim_y, rim_x = lax.while_loop(
        lambda state: state[0] < rounds[0], another, (jnp.int32(1), own, rim_y, rim_x)
    )
    source_field, receiver_field, near, up, down = call(
        steps_kernel,
        [(tile, F32), (tile, F32), ((4, 32, 128), F32), ((4, 16, 128), F32), ((4, 16, 128), F32)],
        [*fields, before, after, left, right, own, rim_y, rim_x],
        hbm=[source_cell, wavelet],
        scratch=[
            pltpu.VMEM((2, 48, 32, 128), F32),
            pltpu.VMEM((4, 40, 16, 128), F32),
            pltpu.VMEM((2, 40, 24, 128), F32),
            pltpu.VMEM((2, 40, 16, 128), F32),
            pltpu.VMEM((3, 16, 128), I32),
            pltpu.VMEM((3, 16, 128), F32),
            pltpu.VMEM((4, 2, 40, 128), F32),
            pltpu.SMEM((1,), I32),
            pltpu.SMEM((2,), F32),
            pltpu.SemaphoreType.DMA((2,)),
        ],
    )
    near_left, near_right = both_ways(up, down, "gx")
    (angles,) = call(
        angles_kernel, [((16, 8, 128), F32)], [near, near_left, near_right],
        scratch=[pltpu.VMEM((4, 64, 128), F32)],
    )
    angles = lax.all_to_all(angles, "gy", 0, 0, tiled=True)
    (image,) = call(arrange_kernel, [((2, 8, 1024), F32)], [angles])
    return source_field, receiver_field, image


def solution(mesh):
    return jax.shard_map(
        body,
        mesh=mesh,
        in_specs=(
            P("gx", "gy", None),
            P("gx", "gy", None),
            P("gx", "gy", None),
            P("gx", "gy", None),
            P("gx", "gy", None),
            P(),
            P(),
            P(("gx", "gy")),
            P(None, ("gx", "gy")),
            P("gy", "gx"),
            P(None, None, "gy", "gx"),
        ),
        out_specs=(P("gx", "gy", None), P("gx", "gy", None), P("gy", "gx", None)),
        check_vma=False,
    )
```

```python
import math

import jax
import jax.numpy as jnp
import numpy as np
from jax import lax
from jax.experimental import pallas as pl
from jax.experimental.pallas import tpu as pltpu
from jax.sharding import PartitionSpec as P

COEFS = (-205.0 / 72.0, 8.0 / 5.0, -1.0 / 5.0, 8.0 / 315.0, -1.0 / 560.0)
SLOPES = np.array(
    [math.tan(math.pi * (-60.0 + 120.0 * (angle + 0.5) / 32.0) / 180.0) for angle in range(32)],
    dtype=np.float32,
)
GX, GY = 8, 16
TX, TY, TZ = 32, 8, 128
DEVICES = GX * GY
RECEIVERS = 256
SLOTS = 16
F32, BF16, I32 = jnp.float32, jnp.bfloat16, jnp.int32
VMEM_LIMIT = 24 * 1024 * 1024


def iota(shape, dim):
    return lax.broadcasted_iota(I32, shape, dim)


def halves(value):
    high = value.astype(BF16)
    return high, (value - high.astype(F32)).astype(BF16)


def dot_nt(left, right):
    return lax.dot_general(left, right, (((1,), (1,)), ((), ())), preferred_element_type=F32)


def routed(cells, traces, first_slot):
    x, y, z = cells >> 14, (cells >> 7) & 127, cells & 127
    tile_x, tile_y, in_x, in_y = x >> 5, y >> 3, x & 31, y & 7
    beside_y = jnp.where(in_y < 4, tile_y - 1, tile_y + 1)
    beside_x = jnp.where(in_x < 4, tile_x - 1, jnp.where(in_x >= 28, tile_x + 1, -1))
    to_y = jnp.where((beside_y >= 0) & (beside_y < GY), tile_x * GY + beside_y, -1)
    to_x = jnp.where((beside_x >= 0) & (beside_x < GX), beside_x * GY + tile_y, -1)
    rim_x = jnp.where(in_x < 4, in_x + 4, in_x - 28)
    classes = (
        (tile_x * GY + tile_y, (in_x * 8 + in_y) * 128 + z, 2),
        (to_y, (in_x * 8 + (in_y ^ 4)) * 128 + z, 1),
        (to_x, (rim_x * 8 + in_y) * 128 + z, 1),
    )
    earlier = jnp.where(
        iota((RECEIVERS, RECEIVERS), 0) < iota((RECEIVERS, RECEIVERS), 1), 1.0, 0.0
    ).astype(BF16)
    device = iota((DEVICES, RECEIVERS), 0)
    slot = iota((SLOTS, RECEIVERS), 0).astype(F32) + first_slot.astype(F32)
    hits, kept, last_rank, row = [], [], None, 0
    for target, place, steps in classes:
        hit = jnp.where(device == target, 1.0, 0.0)
        before = jnp.dot(hit.astype(BF16), earlier, preferred_element_type=F32)
        rank = jnp.sum(hit * before, axis=0, keepdims=True)
        last_rank = rank if last_rank is None else jnp.maximum(last_rank, rank)
        mine = slot == rank
        rows = [jnp.where(mine, place.astype(F32), 0.0)]
        rows += [jnp.where(mine, traces[s : s + 1], 0.0) for s in range(steps)]
        size = SLOTS * len(rows)
        above = [jnp.zeros((row, RECEIVERS), F32)] if row else []
        below = [jnp.zeros((128 - row - size, RECEIVERS), F32)]
        kept.append(jnp.concatenate(above + rows + below, axis=0))
        hits.append(hit.astype(BF16))
        row += size
    hits = jnp.concatenate(hits, axis=1)
    high, low = halves(jnp.concatenate(kept, axis=1))
    sent = dot_nt(hits, high) + dot_nt(hits, low)
    rounds = (jnp.max(last_rank, axis=1, keepdims=True).astype(I32) // SLOTS + 1).astype(F32)
    return jnp.where(iota((DEVICES, 128), 1) >= row, rounds, sent)


def route_kernel(cells_ref, traces_ref, sent_ref):
    sent_ref[:, 0, :] = routed(cells_ref[...], traces_ref[...], jnp.int32(0))


def route_more_kernel(first_ref, cells, traces, sent_ref, cells_v, traces_v, sems):
    for copy in started([(cells, cells_v), (traces, traces_v)], sems):
        copy.wait()
    sent_ref[:, 0, :] = routed(cells_v[...], traces_v[...], first_ref[0])


def collected(got):
    rows = got.T
    sums, row = [], 0
    for columns, steps in ((TX * 8, 2), (TX * 8, 1), (64, 1)):
        cell = rows[row : row + SLOTS].astype(I32)
        column, depth = cell >> 7, cell & 127
        at = iota((columns, DEVICES), 0)
        down = iota((TZ, DEVICES), 0)
        one, parts = [], [[] for _ in range(2 * steps)]
        for k in range(SLOTS):
            one.append(jnp.where(at == column[k : k + 1], 1.0, 0.0).astype(BF16))
            same = down == depth[k : k + 1]
            for s in range(steps):
                value = rows[row + (s + 1) * SLOTS + k : row + (s + 1) * SLOTS + k + 1]
                high = value.astype(BF16).astype(F32)
                parts[2 * s].append(jnp.where(same, high, 0.0).astype(BF16))
                parts[2 * s + 1].append(jnp.where(same, value - high, 0.0).astype(BF16))
        one = jnp.concatenate(one, axis=1)
        for s in range(steps):
            high = jnp.concatenate(parts[2 * s], axis=1)
            low = jnp.concatenate(parts[2 * s + 1], axis=1)
            sums.append(dot_nt(one, high) + dot_nt(one, low))
        row += SLOTS * (steps + 1)
    return sums


def collect_kernel(got_ref, own_ref, rim_y_ref, rim_x_ref, rounds_ref):
    got = got_ref[...]
    own_0, own_1, rim_y, rim_x = collected(got)
    own_ref[0] = own_0.reshape(TX, 8, 128)
    own_ref[1] = own_1.reshape(TX, 8, 128)
    rim_y_ref[...] = rim_y.reshape(TX, 8, 128)
    rim_x_ref[...] = rim_x.reshape(8, 8, 128)
    rounds_ref[0] = jnp.max(got[:, 112:128]).astype(I32)


def collect_more_kernel(got_ref, own_in, rim_y_in, rim_x_in, own_ref, rim_y_ref, rim_x_ref):
    own_0, own_1, rim_y, rim_x = collected(got_ref[:, 0, :])
    own_ref[0] = own_in[0] + own_0.reshape(TX, 8, 128)
    own_ref[1] = own_in[1] + own_1.reshape(TX, 8, 128)
    rim_y_ref[...] = rim_y_in[...] + rim_y.reshape(TX, 8, 128)
    rim_x_ref[...] = rim_x_in[...] + rim_x.reshape(8, 8, 128)


def strip_values_tile(values, step, rows):
    return jnp.concatenate([values[step, layer][rows] for layer in range(4)], axis=1)


def wide(depth):
    return jnp.concatenate([depth, jnp.zeros((depth.shape[0], 96), depth.dtype)], axis=1)


def started(copies, sems):
    copies = [pltpu.make_async_copy(*ends, sems.at[k]) for k, ends in enumerate(copies)]
    for copy in copies:
        copy.start()
    return copies


def pack_kernel(
    cells, traces, wavelet, s0, r0, sm, rm, c, depth, values,
    up_y, down_y, cells_ref, traces_ref, wavelet_ref, sm_v, rm_v, c_v, depth_v, values_v, sems,
):
    copies = started(
        [
            (sm, sm_v), (rm, rm_v), (c, c_v), (depth, depth_v), (values, values_v),
            (s0, up_y.at[0:32]), (r0, up_y.at[32:64]), (s0, down_y.at[0:32]), (r0, down_y.at[32:64]),
            (cells, cells_ref), (traces, traces_ref), (wavelet, wavelet_ref),
        ],
        sems,
    )
    for copy in copies[:5]:
        copy.wait()
    for ref, rows in ((up_y, slice(4, 8)), (down_y, slice(0, 4))):
        ref[64:96, 0:4] = sm_v[:, rows]
        ref[64:96, 4:8] = rm_v[:, rows]
        ref[96:112, 0:4] = c_v[0:16, rows]
        ref[96:112, 4:8] = c_v[16:32, rows]
        ref[112, 0:4] = strip_values_tile(values_v, 0, rows)
        ref[112, 4:8] = wide(depth_v[rows].astype(F32))
    for copy in copies[5:]:
        copy.wait()


def pack_x_kernel(s0, r0, sm, rm, c, depth, values, before, after, up_ref, down_ref):
    keep_before, keep_after = keeps("gy", GY)
    near = strip_values_tile(values, 0, slice(0, 8))
    depths = wide(depth[...].astype(F32))
    for ref, deep, rim in ((up_ref, 24, 28), (down_ref, 0, 0)):
        for f, field in ((0, s0), (1, r0)):
            ref[8 * f : 8 * f + 8] = field[deep : deep + 8]
            start = 16 + 4 * f
            ref[start : start + 4, 0:4] = before[32 * f + rim : 32 * f + rim + 4, 4:8] * keep_before
            ref[start : start + 4, 4:8] = after[32 * f + rim : 32 * f + rim + 4, 0:4] * keep_after
        ref[24:28] = sm[rim : rim + 4]
        ref[28:32] = rm[rim : rim + 4]
        ref[32:36] = c[rim : rim + 4]
        ref[36] = near
        ref[37] = depths


def depth_matrix():
    apart = jnp.abs(iota((TZ, TZ), 0) - iota((TZ, TZ), 1))
    weights = jnp.zeros((TZ, TZ), F32)
    for reach in range(1, 5):
        weights = jnp.where(apart == reach, COEFS[reach], weights)
    high, low = halves(weights)
    top = jnp.concatenate([high, low], axis=1)
    return jnp.concatenate([top, jnp.concatenate([high, jnp.zeros_like(low)], axis=1)], axis=0)


def depth_sums(rows, matrix):
    both = jnp.dot(jnp.concatenate(halves(rows), axis=1), matrix, preferred_element_type=F32)
    return both[:, :128] + both[:, 128:]


def curvature(ref, f, x, row, depth_sum):
    tile = ref[f, x, row : row + 8]
    total = (3.0 * COEFS[0]) * tile + depth_sum
    for reach in range(1, 5):
        pairs = ref[f, x + reach, row : row + 8] + ref[f, x - reach, row : row + 8]
        pairs = pairs + ref[f, x, row + reach : row + reach + 8]
        pairs = pairs + ref[f, x, row - reach : row - reach + 8]
        total = total + COEFS[reach] * pairs
    return tile, total


def overwritten(tile, depths, values, lane_start):
    lane = iota((8, 128), 1)
    column = jnp.full((8, 128), lane_start, I32)
    relative = lane - jnp.take_along_axis(depths, column, axis=1)
    fill = jnp.take_along_axis(values, (relative & 3) * 32 + column, axis=1)
    return jnp.where((relative >= 0) & (relative < 4), fill, tile)


def keeps(axis, size):
    at = lax.axis_index(axis)
    return jnp.where(at > 0, 1.0, 0.0), jnp.where(at < size - 1, 1.0, 0.0)


def pulse(source_cell, wavelet, step, row):
    cell = source_cell[0]
    lane, sublane = iota((8, 128), 1), iota((8, 128), 0)
    at_row = sublane + (row + lax.axis_index("gy") * TY) == (cell >> 7) & 127
    return jnp.where((lane == cell & 127) & at_row, wavelet[0:1, step : step + 1], 0.0)


def source_layer(source_cell):
    return (source_cell[0] >> 14) - lax.axis_index("gx") * TX


def near_strips(depth, values, before, after, keep_before, keep_after, d_ref, v_ref):
    v_ref[4:12] = strip_values_tile(values, 0, slice(0, 8))
    d_ref[4:12] = wide(depth[...])
    for ref, keep, rows in ((before, keep_before, slice(0, 4)), (after, keep_after, slice(12, 16))):
        v_ref[rows] = ref[112, 0:4] * keep
        d_ref[rows] = (ref[112, 4:8] * keep).astype(I32)


def beside_rows(ref, before, after, keep_before, keep_after, to, first, last):
    size = last - first
    for part, keep, rows in ((before, keep_before, slice(0, 4)), (after, keep_after, slice(12, 16))):
        ref[0, to : to + size, rows] = part[64 + first : 64 + last, 0:4] * keep
        ref[1, to : to + size, rows] = part[64 + first : 64 + last, 4:8] * keep
        for half in range(2):
            low, high = max(first, 16 * half), min(last, 16 * half + 16)
            if low < high:
                at = to + low - first
                start = 96 + low - 16 * half
                ref[2, at : at + high - low, rows] = (
                    part[start : start + high - low, 4 * half : 4 * half + 4] * keep
                )


def inner_kernel(
    source_cell,
    wavelet, s0, r0, sm, rm, c, depth, values, before, after,
    new_ref, courant_ref,
    e_ref, m_ref, z_ref, d_ref, v_ref,
):
    keep_before, keep_after = keeps("gy", GY)
    for f, field in ((0, s0), (1, r0)):
        e_ref[f, :, 12:20] = field[...]
        e_ref[f, :, 4:12] = before[32 * f : 32 * f + 32] * keep_before
        e_ref[f, :, 20:28] = after[32 * f : 32 * f + 32] * keep_after
    for k, field in ((0, sm), (1, rm), (2, c)):
        m_ref[k, :, 4:12] = field[4:28]
    beside_rows(m_ref, before, after, keep_before, keep_after, 0, 4, 28)
    near_strips(depth, values, before, after, keep_before, keep_after, d_ref, v_ref)
    pulses = [pulse(source_cell, wavelet, 0, 8 * t - 4) for t in range(2)]
    source_x = source_layer(source_cell)
    matrix = depth_matrix()
    for f in range(2):
        rows = e_ref[f, 4:28, 8:24].reshape(384, 128)
        z_ref[f] = depth_sums(rows, matrix).reshape(24, 16, 128)

    def layer(i, carry):
        for t in range(2):
            rows = slice(8 * t, 8 * t + 8)
            courant = m_ref[2, i, rows]
            courant_ref[i, rows] = courant
            now, total = curvature(e_ref, 0, i + 4, 8 + 8 * t, z_ref[0, i, rows])
            total = total - jnp.where(i + 4 == source_x, pulses[t], 0.0)
            new = 2.0 * now - m_ref[0, i, rows] + courant * total
            new_ref[0, i, rows] = overwritten(new, d_ref[rows], v_ref[rows], i + 4)
            now, total = curvature(e_ref, 1, i + 4, 8 + 8 * t, z_ref[1, i, rows])
            new_ref[1, i, rows] = 2.0 * now - m_ref[1, i, rows] + courant * total
        return carry

    lax.fori_loop(0, 24, layer, 0, unroll=8)


def steps_kernel(
    source_cell,
    wavelet, s0, r0, sm, rm, c, depth, values, before, after, left, right, inner, inner_courant,
    own, rim_y, rim_x,
    s_out, r_out, near_ref, up_ref, down_ref,
    e_ref, m_ref, o_ref, z_ref, d_ref, v_ref, sub_ref,
):
    keep_before, keep_after = keeps("gy", GY)
    keep_left, keep_right = keeps("gx", GX)
    sides = ((0, left, keep_left), (1, right, keep_right))
    for f, field in ((0, s0), (1, r0)):
        for side, ref, keep in sides:
            near, far, rim, first = ((8, 0, 4, 0), (16, 24, 24, 24))[side]
            e_ref[f, near : near + 8, 12:20] = field[first : first + 8]
            start = 32 * f + first
            e_ref[f, near : near + 8, 4:12] = before[start : start + 8] * keep_before
            e_ref[f, near : near + 8, 20:28] = after[start : start + 8] * keep_after
            e_ref[f, far : far + 8, 12:20] = ref[8 * f : 8 * f + 8] * keep
            corner = 16 + 4 * f
            e_ref[f, rim : rim + 4, 8:12] = ref[corner : corner + 4, 0:4] * keep
            e_ref[f, rim : rim + 4, 20:24] = ref[corner : corner + 4, 4:8] * keep
    for k, field in ((0, sm), (1, rm), (2, c)):
        m_ref[k, 0:4, 4:12] = left[24 + 4 * k : 28 + 4 * k] * keep_left
        m_ref[k, 4:8, 4:12] = field[0:4]
        m_ref[k, 8:12, 4:12] = field[28:32]
        m_ref[k, 12:16, 4:12] = right[24 + 4 * k : 28 + 4 * k] * keep_right
    beside_rows(m_ref, before, after, keep_before, keep_after, 4, 0, 4)
    beside_rows(m_ref, before, after, keep_before, keep_after, 8, 28, 32)
    m_ref[3, 0:4, 4:12] = rim_x[0:4]
    m_ref[3, 12:16, 4:12] = rim_x[4:8]
    for to, first in ((4, 0), (8, 28)):
        m_ref[3, to : to + 4, 4:12] = own[0, first : first + 4]
        m_ref[3, to : to + 4, 0:4] = rim_y[first : first + 4, 0:4]
        m_ref[3, to : to + 4, 12:16] = rim_y[first : first + 4, 4:8]
    near_strips(depth, values, before, after, keep_before, keep_after, d_ref.at[1], v_ref.at[1])
    for side, ref, keep in sides:
        v_ref[2 * side] = jnp.zeros((16, 128), F32)
        d_ref[2 * side] = jnp.zeros((16, 128), I32)
        v_ref[2 * side, 4:12] = ref[36] * keep
        d_ref[2 * side, 4:12] = (ref[37] * keep).astype(I32)
    o_ref[0, 8:32, 4:20] = inner[0]
    o_ref[1, 8:32, 8:16] = inner[1, :, 4:12] + inner_courant[:, 4:12] * own[0, 4:28]
    o_ref[1, 8:32, 4:8] = inner[1, :, 0:4] + inner_courant[:, 0:4] * rim_y[4:28, 0:4]
    o_ref[1, 8:32, 16:20] = inner[1, :, 12:16] + inner_courant[:, 12:16] * rim_y[4:28, 4:8]
    pulses = [pulse(source_cell, wavelet, 0, 8 * t - 4) for t in range(2)]
    source_x = source_layer(source_cell)
    matrix = depth_matrix()
    for f in range(2):
        for side in range(2):
            rows = e_ref[f, 4 + 16 * side : 12 + 16 * side, 8:24].reshape(128, 128)
            z_ref[f, 8 * side : 8 * side + 8] = depth_sums(rows, matrix).reshape(8, 16, 128)

    def first(j, carry):
        part = jnp.where(j >= 4, 1, 0) + jnp.where(j >= 12, 1, 0)
        low = j < 8
        column = jnp.where(j < 4, j + 28, jnp.where(low, j - 4, jnp.where(j < 12, j + 20, j - 12)))
        at = jnp.where(low, j + 4, j + 12)
        i = jnp.where(low, j, j + 24)
        for t in range(2):
            rows = slice(8 * t, 8 * t + 8)
            courant = m_ref[2, j, rows]
            now, total = curvature(e_ref, 0, at, 8 + 8 * t, z_ref[0, j, rows])
            total = total - jnp.where(i - 4 == source_x, pulses[t], 0.0)
            new = 2.0 * now - m_ref[0, j, rows] + courant * total
            new = overwritten(new, d_ref[part, rows], v_ref[part, rows], column)
            o_ref[0, i, 4 + 8 * t : 12 + 8 * t] = new
            now, total = curvature(e_ref, 1, at, 8 + 8 * t, z_ref[1, j, rows])
            new = 2.0 * now - m_ref[1, j, rows] + courant * (total + m_ref[3, j, rows])
            o_ref[1, i, 4 + 8 * t : 12 + 8 * t] = new
        return carry

    lax.fori_loop(0, 16, first, 0, unroll=8)
    for f in range(2):
        for half in range(2):
            rows = o_ref[f, 4 + 16 * half : 20 + 16 * half, 8:16].reshape(128, 128)
            z_ref[f, :, 8 * half : 8 * half + 8] = depth_sums(rows, matrix).reshape(16, 8, 128)
    late_values = strip_values_tile(values, 1, slice(0, 8))
    near_depth = wide(depth[...])
    late_pulse = pulse(source_cell, wavelet, 1, 0)

    def second(x, half):
        rows = slice(8 * half, 8 * half + 8)
        now, total = curvature(o_ref, 0, x + 4, 8, z_ref[0, x - 16 * half, rows])
        total = total - jnp.where(x == source_x, late_pulse, 0.0)
        new = 2.0 * now - s0[x] + c[x] * total
        new = overwritten(new, near_depth, late_values, x)
        s_out[x] = new
        for j in range(2):
            sub_ref[0, j, pl.ds(x, 1)] = now[4 * j : 4 * j + 1]
            sub_ref[1, j, pl.ds(x, 1)] = new[4 * j : 4 * j + 1]
        now, total = curvature(o_ref, 1, x + 4, 8, z_ref[1, x - 16 * half, rows])
        new = 2.0 * now - r0[x] + c[x] * (total + own[1, x])
        r_out[x] = new
        for j in range(2):
            sub_ref[2, j, pl.ds(x, 1)] = now[4 * j : 4 * j + 1]
            sub_ref[3, j, pl.ds(x, 1)] = new[4 * j : 4 * j + 1]

    for half in range(2):
        lax.fori_loop(
            16 * half, 16 * half + 16, lambda x, carry, half=half: (second(x, half), carry)[1], 0, unroll=16
        )
    z, to = iota((TZ, 128), 0), iota((TZ, 128), 1)
    for k in range(4):
        total = None
        for j in range(2):
            pick = jnp.where((z & 3 == 0) & (to == (z >> 2) + (16 + 64 * j)), 1.0, 0.0)
            part = jnp.dot(
                sub_ref[k, j], pick, precision=lax.Precision.HIGHEST, preferred_element_type=F32
            )
            total = part if total is None else total + part
        near_ref[k] = total
        up_ref[k] = total[16:32]
        down_ref[k] = total[0:16]


def angles_kernel(near, left, right, out_ref, g_ref):
    keep_left, keep_right = keeps("gx", GX)
    for k in range(4):
        g_ref[k, 0:16] = left[k] * keep_left
        g_ref[k, 16:48] = near[k]
        g_ref[k, 48:64] = right[k] * keep_right
    sums = [None] * 32
    for lag in range(-16, 17):
        product = None
        for step in range(2):
            source = g_ref[step, pl.ds(16 - lag, 8, stride=4)]
            receiver = g_ref[2 + step, pl.ds(16 + lag, 8, stride=4)]
            part = source * receiver
            product = part if product is None else product + part
        shifted = {}

        def shift(amount):
            if amount not in shifted:
                shifted[amount] = product if amount == 0 else pltpu.roll(product, -amount % 128, 1)
            return shifted[amount]

        for a in range(32):
            move = np.float32(lag) * SLOPES[a] / np.float32(4.0)
            low = np.floor(move)
            frac = float(move - low)
            term = shift(int(low)) * (1.0 - frac)
            if frac != 0.0:
                term = term + shift(int(low) + 1) * frac
            sums[a] = term if sums[a] is None else sums[a] + term
    lane = iota((8, 128), 1)
    for b in range(16):
        first, second = sums[2 * b], sums[2 * b + 1]
        packed = jnp.where(lane < 32, pltpu.roll(first, 112, 1), pltpu.roll(first, 80, 1))
        other = jnp.where(lane < 96, pltpu.roll(second, 48, 1), pltpu.roll(second, 16, 1))
        out_ref[b] = jnp.where(lane < 64, packed, other)


def arrange_kernel(got, out_ref):
    lane = iota((8, 128), 1)
    for t in range(8):
        even, odd = got[2 * t], got[2 * t + 1]
        out_ref[0, :, 128 * t : 128 * t + 128] = jnp.where(lane < 64, even, pltpu.roll(odd, 64, 1))
        out_ref[1, :, 128 * t : 128 * t + 128] = jnp.where(lane < 64, pltpu.roll(even, 64, 1), odd)


def call(kernel, outs, arrays, scalars=(), hbm=(), out_scalars=0, scratch=(), weight=0):
    smem, vmem = pl.BlockSpec(memory_space=pltpu.SMEM), pl.BlockSpec(memory_space=pltpu.VMEM)
    far = pl.BlockSpec(memory_space=pltpu.HBM)
    hbm = [
        pltpu.with_memory_space_constraint(array, pltpu.HBM) for array in hbm
    ]
    return pl.pallas_call(
        kernel,
        out_shape=[jax.ShapeDtypeStruct(shape, kind) for shape, kind in outs],
        in_specs=[smem] * len(scalars) + [far] * len(hbm) + [vmem] * len(arrays),
        out_specs=[vmem] * (len(outs) - out_scalars) + [smem] * out_scalars,
        scratch_shapes=list(scratch),
        compiler_params=pltpu.CompilerParams(vmem_limit_bytes=VMEM_LIMIT),
        cost_estimate=pl.CostEstimate(flops=0, bytes_accessed=weight, transcendentals=0) if weight else None,
    )(*scalars, *hbm, *arrays)


def both_ways(to_next, to_last, axis):
    size = lax.axis_size(axis)
    from_last = lax.ppermute(to_next, axis, [(i, (i + 1) % size) for i in range(size)])
    from_next = lax.ppermute(to_last, axis, [((i + 1) % size, i) for i in range(size)])
    return from_last, from_next


def body(
    source_now,
    source_next,
    receiver_now,
    receiver_next,
    courant,
    source_cell,
    wavelet,
    receiver_cells,
    receiver_traces,
    strip_depth,
    strip_values,
):
    cells = receiver_cells.reshape(1, RECEIVERS)
    tile, sent_shape = (TX, TY, TZ), ((DEVICES, 1, 128), F32)
    listed = [((1, RECEIVERS), I32), ((2, RECEIVERS), F32)]
    fields = (source_now, receiver_now, source_next, receiver_next, courant, strip_depth, strip_values)
    up_y, down_y, near_cells, near_traces, near_wavelet = call(
        pack_kernel,
        [((113, 8, 128), F32)] * 2 + [*listed, ((1, 2), F32)],
        [],
        hbm=[cells, receiver_traces, wavelet.reshape(1, 2), *fields],
        scratch=[pltpu.VMEM(tile, F32)] * 3
        + [pltpu.VMEM((8, 32), I32), pltpu.VMEM((2, 4, 8, 32), F32), pltpu.SemaphoreType.DMA((12,))],
    )
    before, after = both_ways(up_y, down_y, "gy")
    (sent,) = call(route_kernel, [sent_shape], [near_cells, near_traces], weight=20_000_000)
    got = lax.all_to_all(sent, ("gx", "gy"), 0, 0, tiled=True)
    got = jnp.maximum(got.reshape(DEVICES, 128), -jnp.finfo(F32).max)
    up_x, down_x = call(pack_x_kernel, [((38, 8, 128), F32)] * 2, [*fields, before, after])
    left, right = both_ways(up_x, down_x, "gx")
    inner, inner_courant = call(
        inner_kernel,
        [((2, 24, 16, 128), F32), ((24, 16, 128), F32)],
        [near_wavelet, *fields, before, after],
        scalars=[source_cell],
        scratch=[
            pltpu.VMEM((2, 32, 32, 128), F32),
            pltpu.VMEM((3, 24, 16, 128), F32),
            pltpu.VMEM((2, 24, 16, 128), F32),
            pltpu.VMEM((16, 128), I32),
            pltpu.VMEM((16, 128), F32),
        ],
    )
    sums = [((2, *tile), F32), (tile, F32), ((8, 8, 128), F32)]
    own, rim_y, rim_x, rounds = call(collect_kernel, [*sums, ((1,), I32)], [got], out_scalars=1, weight=1000)

    def another(state):
        turn, *partial = state
        (more,) = call(
            route_more_kernel,
            [sent_shape],
            [],
            scalars=[(turn * SLOTS).reshape(1)],
            hbm=[cells, receiver_traces],
            scratch=[pltpu.VMEM(*shape) for shape in listed] + [pltpu.SemaphoreType.DMA((2,))],
        )
        more = lax.all_to_all(more, ("gx", "gy"), 0, 0, tiled=True)
        return (turn + 1, *call(collect_more_kernel, sums, [more, *partial]))

    _, own, rim_y, rim_x = lax.while_loop(
        lambda state: state[0] < rounds[0], another, (jnp.int32(1), own, rim_y, rim_x)
    )
    source_field, receiver_field, near, up, down = call(
        steps_kernel,
        [(tile, F32), (tile, F32), ((4, 32, 128), F32), ((4, 16, 128), F32), ((4, 16, 128), F32)],
        [near_wavelet, *fields, before, after, left, right, inner, inner_courant, own, rim_y, rim_x],
        scalars=[source_cell],
        scratch=[
            pltpu.VMEM((2, 32, 32, 128), F32),
            pltpu.VMEM((4, 16, 16, 128), F32),
            pltpu.VMEM((2, 40, 24, 128), F32),
            pltpu.VMEM((2, 16, 16, 128), F32),
            pltpu.VMEM((3, 16, 128), I32),
            pltpu.VMEM((3, 16, 128), F32),
            pltpu.VMEM((4, 2, 32, 128), F32),
        ],
    )
    near_left, near_right = both_ways(up, down, "gx")
    (angles,) = call(
        angles_kernel, [((16, 8, 128), F32)], [near, near_left, near_right],
        scratch=[pltpu.VMEM((4, 64, 128), F32)],
    )
    angles = lax.all_to_all(angles, "gy", 0, 0, tiled=True)
    (image,) = call(arrange_kernel, [((2, 8, 1024), F32)], [angles])
    return source_field, receiver_field, image


def solution(mesh):
    return jax.shard_map(
        body,
        mesh=mesh,
        in_specs=(
            P("gx", "gy", None),
            P("gx", "gy", None),
            P("gx", "gy", None),
            P("gx", "gy", None),
            P("gx", "gy", None),
            P(),
            P(),
            P(("gx", "gy")),
            P(None, ("gx", "gy")),
            P("gy", "gx"),
            P(None, None, "gy", "gx"),
        ),
        out_specs=(P("gx", "gy", None), P("gx", "gy", None), P("gy", "gx", None)),
        check_vma=False,
    )
```

```python
import math

import jax
import jax.numpy as jnp
import numpy as np
from jax import lax
from jax.experimental import pallas as pl
from jax.experimental.pallas import tpu as pltpu
from jax.sharding import PartitionSpec as P

COEFS = (-205.0 / 72.0, 8.0 / 5.0, -1.0 / 5.0, 8.0 / 315.0, -1.0 / 560.0)
SLOPES = np.array(
    [math.tan(math.pi * (-60.0 + 120.0 * (angle + 0.5) / 32.0) / 180.0) for angle in range(32)],
    dtype=np.float32,
)
GX, GY = 8, 16
TX, TY, TZ = 32, 8, 128
DEVICES = GX * GY
RECEIVERS = 256
SLOTS = 16
F32, BF16, I32 = jnp.float32, jnp.bfloat16, jnp.int32
VMEM_LIMIT = 24 * 1024 * 1024


def iota(shape, dim):
    return lax.broadcasted_iota(I32, shape, dim)


def halves(value):
    high = value.astype(BF16)
    return high, (value - high.astype(F32)).astype(BF16)


def dot_nt(left, right):
    return lax.dot_general(left, right, (((1,), (1,)), ((), ())), preferred_element_type=F32)


def routed(cells, traces, first_slot):
    x, y, z = cells >> 14, (cells >> 7) & 127, cells & 127
    tile_x, tile_y, in_x, in_y = x >> 5, y >> 3, x & 31, y & 7
    beside_y = jnp.where(in_y < 4, tile_y - 1, tile_y + 1)
    beside_x = jnp.where(in_x < 4, tile_x - 1, jnp.where(in_x >= 28, tile_x + 1, -1))
    to_y = jnp.where((beside_y >= 0) & (beside_y < GY), tile_x * GY + beside_y, -1)
    to_x = jnp.where((beside_x >= 0) & (beside_x < GX), beside_x * GY + tile_y, -1)
    rim_x = jnp.where(in_x < 4, in_x + 4, in_x - 28)
    classes = (
        (tile_x * GY + tile_y, (in_x * 8 + in_y) * 128 + z, 2),
        (to_y, (in_x * 8 + (in_y ^ 4)) * 128 + z, 1),
        (to_x, (rim_x * 8 + in_y) * 128 + z, 1),
    )
    earlier = jnp.where(
        iota((RECEIVERS, RECEIVERS), 0) < iota((RECEIVERS, RECEIVERS), 1), 1.0, 0.0
    ).astype(BF16)
    device = iota((DEVICES, RECEIVERS), 0)
    slot = iota((SLOTS, RECEIVERS), 0).astype(F32) + first_slot.astype(F32)
    hits, kept, last_rank, row = [], [], None, 0
    for target, place, steps in classes:
        hit = jnp.where(device == target, 1.0, 0.0)
        before = jnp.dot(hit.astype(BF16), earlier, preferred_element_type=F32)
        rank = jnp.sum(hit * before, axis=0, keepdims=True)
        last_rank = rank if last_rank is None else jnp.maximum(last_rank, rank)
        mine = slot == rank
        rows = [jnp.where(mine, place.astype(F32), 0.0)]
        rows += [jnp.where(mine, traces[s : s + 1], 0.0) for s in range(steps)]
        size = SLOTS * len(rows)
        above = [jnp.zeros((row, RECEIVERS), F32)] if row else []
        below = [jnp.zeros((128 - row - size, RECEIVERS), F32)]
        kept.append(jnp.concatenate(above + rows + below, axis=0))
        hits.append(hit.astype(BF16))
        row += size
    hits = jnp.concatenate(hits, axis=1)
    high, low = halves(jnp.concatenate(kept, axis=1))
    sent = dot_nt(hits, high) + dot_nt(hits, low)
    rounds = (jnp.max(last_rank, axis=1, keepdims=True).astype(I32) // SLOTS + 1).astype(F32)
    return jnp.where(iota((DEVICES, 128), 1) >= row, rounds, sent)


def route_more_kernel(first_ref, cells, traces, sent_ref, cells_v, traces_v, sems):
    for copy in started([(cells, cells_v), (traces, traces_v)], sems):
        copy.wait()
    sent_ref[:, 0, :] = routed(cells_v[...], traces_v[...], first_ref[0])


def collected(got):
    rows = got.T
    sums, row = [], 0
    down = iota((TZ, DEVICES), 0).astype(F32).astype(BF16)
    unit, zero = jnp.ones((), BF16), jnp.zeros((), BF16)
    for columns, steps in ((TX * 8, 2), (TX * 8, 1), (64, 1)):
        cell = rows[row : row + SLOTS].astype(I32)
        column, depth = (cell >> 7).astype(F32), (cell & 127).astype(F32)
        at = iota((columns, DEVICES), 0).astype(F32).astype(BF16)
        one, parts = [], [[] for _ in range(2 * steps)]
        for k in range(SLOTS):
            one.append(jnp.where(at == column[k : k + 1].astype(BF16), unit, zero))
            same = down == depth[k : k + 1].astype(BF16)
            for s in range(steps):
                value = rows[row + (s + 1) * SLOTS + k : row + (s + 1) * SLOTS + k + 1]
                high, low = halves(value)
                parts[2 * s].append(jnp.where(same, high, zero))
                parts[2 * s + 1].append(jnp.where(same, low, zero))
        one = jnp.concatenate(one, axis=1)
        both = dot_nt(one, jnp.concatenate([jnp.concatenate(part, axis=1) for part in parts], axis=0))
        for s in range(steps):
            sums.append(both[:, 256 * s : 256 * s + 128] + both[:, 256 * s + 128 : 256 * s + 256])
        row += SLOTS * (steps + 1)
    return sums


def collect_kernel(got_ref, inner_courant, own_ref, rim_y_ref, rim_x_ref, rounds_ref):
    got = got_ref[...]
    own_0, own_1, rim_y, rim_x = collected(got)
    own_ref[0] = own_0.reshape(TX, 8, 128)
    own_ref[1] = own_1.reshape(TX, 8, 128)
    rim_y_ref[...] = rim_y.reshape(TX, 8, 128)
    rim_x_ref[...] = rim_x.reshape(8, 8, 128)
    rounds_ref[0] = jnp.max(got[:, 112:128]).astype(I32)


def collect_more_kernel(got_ref, own_in, rim_y_in, rim_x_in, own_ref, rim_y_ref, rim_x_ref):
    own_0, own_1, rim_y, rim_x = collected(got_ref[:, 0, :])
    own_ref[0] = own_in[0] + own_0.reshape(TX, 8, 128)
    own_ref[1] = own_in[1] + own_1.reshape(TX, 8, 128)
    rim_y_ref[...] = rim_y_in[...] + rim_y.reshape(TX, 8, 128)
    rim_x_ref[...] = rim_x_in[...] + rim_x.reshape(8, 8, 128)


def strip_values_tile(values, step, rows):
    return jnp.concatenate([values[step, layer][rows] for layer in range(4)], axis=1)


def wide(depth):
    return jnp.concatenate([depth, jnp.zeros((depth.shape[0], 96), depth.dtype)], axis=1)


def started(copies, sems):
    copies = [pltpu.make_async_copy(*ends, sems.at[k]) for k, ends in enumerate(copies)]
    for copy in copies:
        copy.start()
    return copies


def pack_kernel(
    cells, traces, wavelet, s0, r0, sm, rm, c, depth, values,
    up_y, down_y, wavelet_ref, sm_v, rm_v, c_v, depth_v, values_v, sent_ref,
    sent_v, cells_v, traces_v, sems,
):
    copies = started(
        [
            (cells, cells_v), (traces, traces_v), (depth, depth_v), (values, values_v), (wavelet, wavelet_ref),
            (sm, sm_v), (rm, rm_v), (c, c_v),
            (s0, up_y.at[0:32]), (r0, up_y.at[32:64]), (s0, down_y.at[0:32]), (r0, down_y.at[32:64]),
        ],
        sems,
    )
    for copy in copies[:2]:
        copy.wait()
    sent_v[:, 0, :] = routed(cells_v[...], traces_v[...], jnp.int32(0))
    out = pltpu.make_async_copy(sent_v, sent_ref, sems.at[12])
    out.start()
    for copy in copies[2:8]:
        copy.wait()
    for ref, rows in ((up_y, slice(4, 8)), (down_y, slice(0, 4))):
        ref[64:96, 0:4] = sm_v[:, rows]
        ref[64:96, 4:8] = rm_v[:, rows]
        ref[96:112, 0:4] = c_v[0:16, rows]
        ref[96:112, 4:8] = c_v[16:32, rows]
        ref[112, 0:4] = strip_values_tile(values_v, 0, rows)
        ref[112, 4:8] = wide(depth_v[rows].astype(F32))
    for copy in copies[8:]:
        copy.wait()
    out.wait()


def depth_matrix():
    apart = jnp.abs(iota((TZ, TZ), 0) - iota((TZ, TZ), 1))
    weights = jnp.zeros((TZ, TZ), F32)
    for reach in range(1, 5):
        weights = jnp.where(apart == reach, COEFS[reach], weights)
    high, low = halves(weights)
    top = jnp.concatenate([high, low], axis=1)
    return jnp.concatenate([top, jnp.concatenate([high, jnp.zeros_like(low)], axis=1)], axis=0)


def depth_sums(rows, matrix):
    both = jnp.dot(jnp.concatenate(halves(rows), axis=1), matrix, preferred_element_type=F32)
    return both[:, :128] + both[:, 128:]


def curvature(ref, f, x, row, depth_sum):
    tile = ref[f, x, row : row + 8]
    total = (3.0 * COEFS[0]) * tile + depth_sum
    for reach in range(1, 5):
        pairs = ref[f, x + reach, row : row + 8] + ref[f, x - reach, row : row + 8]
        pairs = pairs + ref[f, x, row + reach : row + reach + 8]
        pairs = pairs + ref[f, x, row - reach : row - reach + 8]
        total = total + COEFS[reach] * pairs
    return tile, total


def overwritten(tile, depths, values, lane_start):
    lane = iota((8, 128), 1)
    column = jnp.full((8, 128), lane_start, I32)
    relative = lane - jnp.take_along_axis(depths, column, axis=1)
    fill = jnp.take_along_axis(values, (relative & 3) * 32 + column, axis=1)
    return jnp.where((relative >= 0) & (relative < 4), fill, tile)


def keeps(axis, size):
    at = lax.axis_index(axis)
    return jnp.where(at > 0, 1.0, 0.0), jnp.where(at < size - 1, 1.0, 0.0)


def pulse(source_cell, wavelet, step, row):
    cell = source_cell[0]
    lane, sublane = iota((8, 128), 1), iota((8, 128), 0)
    at_row = sublane + (row + lax.axis_index("gy") * TY) == (cell >> 7) & 127
    return jnp.where((lane == cell & 127) & at_row, wavelet[0:1, step : step + 1], 0.0)


def source_layer(source_cell):
    return (source_cell[0] >> 14) - lax.axis_index("gx") * TX


def advanced(i, at, x, e_ref, z_ref, m_ref, courant_ref, depth_ref, v_ref, pulses, source_x, new_ref):
    for t in range(2):
        rows = slice(8 * t, 8 * t + 8)
        courant = courant_ref[i, rows]
        now, total = curvature(e_ref, 0, at, 8 + 8 * t, z_ref[0, i, rows])
        if pulses is not None:
            total = total - jnp.where(x == source_x, pulses[t], 0.0)
        new = 2.0 * now - m_ref[0, i, rows] + courant * total
        new_ref[0, i, rows] = overwritten(new, depth_ref[rows], v_ref[rows], x)
        now, total = curvature(e_ref, 1, at, 8 + 8 * t, z_ref[1, i, rows])
        new_ref[1, i, rows] = 2.0 * now - m_ref[1, i, rows] + courant * total


def edge_kernel(
    own_y, sm, rm, c, depth, values, before, after,
    new_ref, courant_ref, depth_ref, v_ref, up_ref, down_ref,
    e_ref, m_ref, z_ref,
):
    keep_before, keep_after = keeps("gy", GY)
    for f in range(2):
        e_ref[f, 0:4, 8:24] = jnp.zeros((4, 16, 128), F32)
        e_ref[f, 20:24, 8:24] = jnp.zeros((4, 16, 128), F32)
        for to, first in ((4, 0), (12, 24)):
            start = 32 * f + first
            e_ref[f, to : to + 8, 12:20] = own_y[start : start + 8]
            e_ref[f, to : to + 8, 4:12] = before[start : start + 8] * keep_before
            e_ref[f, to : to + 8, 20:28] = after[start : start + 8] * keep_after
    v_ref[4:12] = strip_values_tile(values, 0, slice(0, 8))
    depth_ref[4:12] = wide(depth[...])
    for to, first in ((0, 0), (4, 28)):
        layers = slice(to, to + 4)
        m_ref[0, layers, 4:12] = sm[first : first + 4]
        m_ref[1, layers, 4:12] = rm[first : first + 4]
        courant_ref[layers, 4:12] = c[first : first + 4]
    for ref, keep, rows in ((before, keep_before, slice(0, 4)), (after, keep_after, slice(12, 16))):
        for to, first in ((0, 0), (4, 28)):
            layers, half = slice(to, to + 4), first // 16
            m_ref[0, layers, rows] = ref[64 + first : 68 + first, 0:4] * keep
            m_ref[1, layers, rows] = ref[64 + first : 68 + first, 4:8] * keep
            start = 96 + first - 16 * half
            courant_ref[layers, rows] = ref[start : start + 4, 4 * half : 4 * half + 4] * keep
        v_ref[rows] = ref[112, 0:4] * keep
        depth_ref[rows] = (ref[112, 4:8] * keep).astype(I32)
    matrix = depth_matrix()
    for f in range(2):
        for half in range(2):
            rows = e_ref[f, 4 + 12 * half : 8 + 12 * half, 8:24].reshape(64, 128)
            z_ref[f, 4 * half : 4 * half + 4] = depth_sums(rows, matrix).reshape(4, 16, 128)
    for i in range(8):
        at, x = (i + 4, i) if i < 4 else (i + 12, i + 24)
        advanced(
            i, at, x, e_ref, z_ref, m_ref, courant_ref, depth_ref, v_ref, None, None, new_ref
        )
    for ref, to, rim, at in ((up_ref, 4, 28, 16), (down_ref, 0, 0, 4)):
        for f in range(2):
            ref[4 * f : 4 * f + 4] = new_ref[f, to : to + 4, 4:12]
            ref[12 + 4 * f : 16 + 4 * f] = own_y[32 * f + rim : 32 * f + rim + 4]
            ref[20 + 4 * f : 24 + 4 * f, 0:4] = e_ref[f, at : at + 4, 8:12]
            ref[20 + 4 * f : 24 + 4 * f, 4:8] = e_ref[f, at : at + 4, 20:24]
        ref[8:12] = c[rim : rim + 4]
        ref[28] = depth_ref[4:12].astype(F32)


def inner_kernel(
    source_cell,
    wavelet, own_y, sm, rm, c, before, after, depths, values,
    new_ref, courant_ref,
    e_ref, m_ref, z_ref,
):
    keep_before, keep_after = keeps("gy", GY)
    for f in range(2):
        fields = slice(32 * f, 32 * f + 32)
        e_ref[f, :, 12:20] = own_y[fields]
        e_ref[f, :, 4:12] = before[fields] * keep_before
        e_ref[f, :, 20:28] = after[fields] * keep_after
    m_ref[0, :, 4:12] = sm[4:28]
    m_ref[1, :, 4:12] = rm[4:28]
    courant_ref[:, 4:12] = c[4:28]
    for ref, keep, rows in ((before, keep_before, slice(0, 4)), (after, keep_after, slice(12, 16))):
        m_ref[0, :, rows] = ref[68:92, 0:4] * keep
        m_ref[1, :, rows] = ref[68:92, 4:8] * keep
        courant_ref[0:12, rows] = ref[100:112, 0:4] * keep
        courant_ref[12:24, rows] = ref[96:108, 4:8] * keep
    pulses = [pulse(source_cell, wavelet, 0, 8 * t - 4) for t in range(2)]
    source_x = source_layer(source_cell)
    matrix = depth_matrix()
    for f in range(2):
        rows = e_ref[f, 4:28, 8:24].reshape(384, 128)
        z_ref[f] = depth_sums(rows, matrix).reshape(24, 16, 128)

    def layer(i, carry):
        advanced(
            i, i + 4, i + 4, e_ref, z_ref, m_ref, courant_ref, depths, values, pulses, source_x, new_ref
        )
        return carry

    lax.fori_loop(0, 24, layer, 0, unroll=8)


def unless_strip(depths, column, amount):
    relative = iota((8, 128), 1) - depths[:, column : column + 1]
    return jnp.where((relative >= 0) & (relative < 4), 0.0, amount)


def steps_kernel(
    source_cell,
    wavelet, own_y, c, depth, values, left, right, edge, edge_courant, inner, inner_courant, depths,
    own, rim_y, rim_x,
    s_out, r_out, near_ref, up_ref, down_ref,
    o_ref, h_ref, z_ref, sub_ref, s_v, r_v, sems,
):
    keep_left, keep_right = keeps("gx", GX)
    s0, r0 = own_y.at[0:32], own_y.at[32:64]
    for new1, courant, start, first, size in (
        (edge, edge_courant, 0, 0, 4), (inner, inner_courant, 0, 4, 24), (edge, edge_courant, 4, 28, 4)
    ):
        to, part, x = slice(first + 4, first + 4 + size), slice(start, start + size), slice(first, first + size)
        o_ref[0, to, 4:20] = new1[0, part]
        o_ref[1, to, 8:16] = new1[1, part, 4:12] + courant[part, 4:12] * own[0, x]
        o_ref[1, to, 4:8] = new1[1, part, 0:4] + courant[part, 0:4] * rim_y[x, 0:4]
        o_ref[1, to, 16:20] = new1[1, part, 12:16] + courant[part, 12:16] * rim_y[x, 4:8]
    source_x = source_layer(source_cell)
    pulses = [pulse(source_cell, wavelet, 0, row) for row in (-4, 4, 0)]
    for side, ref, keep in ((0, left, keep_left), (1, right, keep_right)):
        beyond_depths = (ref[28] * keep).astype(I32)
        for f in range(2):
            h_ref[f, side, :, 4:12] = ref[12 + 4 * f : 16 + 4 * f] * keep
            h_ref[f, side, :, 0:4] = ref[20 + 4 * f : 24 + 4 * f, 0:4] * keep
            h_ref[f, side, :, 12:16] = ref[20 + 4 * f : 24 + 4 * f, 4:8] * keep
        for n in range(4):
            x = 31 - n if side else n
            for f in range(2):
                for t in range(2):
                    rows = slice(8 * t, 8 * t + 8)
                    amount = None
                    for reach in range(n + 1, 5):
                        away = reach - n
                        term = COEFS[reach] * h_ref[f, side, away - 1 if side else 4 - away, rows]
                        amount = term if amount is None else amount + term
                    if f == 0:
                        amount = amount - jnp.where(x == source_x, pulses[t], 0.0)
                    amount = edge_courant[x - 24 if side else x, rows] * amount
                    if f == 0:
                        amount = unless_strip(depths[rows], x, amount)
                    at = slice(4 + 8 * t, 12 + 8 * t)
                    o_ref[f, x + 4, at] = o_ref[f, x + 4, at] + amount
            k = n if side else 3 - n
            for f, field in ((0, s0), (1, r0)):
                amount = None
                for reach in range(n + 1, 5):
                    inward = reach - n - 1
                    term = COEFS[reach] * field[31 - inward if side else inward]
                    amount = term if amount is None else amount + term
                if f == 0:
                    beyond = 32 + n if side else -1 - n
                    amount = amount - jnp.where(beyond == source_x, pulses[2], 0.0)
                else:
                    amount = amount + rim_x[4 * side + k]
                amount = ref[8 + k] * amount
                if f == 0:
                    amount = unless_strip(beyond_depths, k if side else 28 + k, amount)
                o_ref[f, 36 + n if side else 3 - n, 8:16] = (ref[4 * f + k] + amount) * keep
    matrix = depth_matrix()
    for f in range(2):
        rows = o_ref[f, 4:36, 8:16].reshape(256, 128)
        z_ref[f] = depth_sums(rows, matrix).reshape(32, 8, 128)
    late_values = strip_values_tile(values, 1, slice(0, 8))
    near_depth = wide(depth[...])
    late_pulse = pulse(source_cell, wavelet, 1, 0)

    def second(x, carry):
        now, total = curvature(o_ref, 0, x + 4, 8, z_ref[0, x])
        total = total - jnp.where(x == source_x, late_pulse, 0.0)
        new = 2.0 * now - s0[x] + c[x] * total
        new = overwritten(new, near_depth, late_values, x)
        s_v[x] = new
        for j in range(2):
            sub_ref[0, j, pl.ds(x, 1)] = now[4 * j : 4 * j + 1]
            sub_ref[1, j, pl.ds(x, 1)] = new[4 * j : 4 * j + 1]
        now, total = curvature(o_ref, 1, x + 4, 8, z_ref[1, x])
        new = 2.0 * now - r0[x] + c[x] * (total + own[1, x])
        r_v[x] = new
        for j in range(2):
            sub_ref[2, j, pl.ds(x, 1)] = now[4 * j : 4 * j + 1]
            sub_ref[3, j, pl.ds(x, 1)] = new[4 * j : 4 * j + 1]
        return carry

    lax.fori_loop(0, 32, second, 0, unroll=16)
    copies = started([(s_v, s_out), (r_v, r_out)], sems)
    z, to = iota((TZ, 128), 0), iota((TZ, 128), 1)
    totals = []
    for k in range(4):
        total = None
        for j in range(2):
            pick = jnp.where((z & 3 == 0) & (to == (z >> 2) + (16 + 64 * j)), 1.0, 0.0)
            part = jnp.dot(
                sub_ref[k, j], pick, precision=lax.Precision.HIGHEST, preferred_element_type=F32
            )
            total = part if total is None else total + part
        near_ref[k] = total
        totals.append(total)
    for f in range(2):
        packed = totals[2 * f] + pltpu.roll(totals[2 * f + 1], 32, 1)
        up_ref[f] = packed[16:32]
        down_ref[f] = packed[0:16]
    for copy in copies:
        copy.wait()


def angles_kernel(near, left, right, out_ref, g_ref):
    keep_left, keep_right = keeps("gx", GX)
    lane = iota((16, 128), 1)
    held = ((lane >= 16) & (lane < 48)) | ((lane >= 80) & (lane < 112))
    for f in range(2):
        for ref, keep, rows in ((left, keep_left, slice(0, 16)), (right, keep_right, slice(48, 64))):
            packed = ref[f] * keep
            g_ref[2 * f, rows] = jnp.where(held, packed, 0.0)
            g_ref[2 * f + 1, rows] = jnp.where(held, pltpu.roll(packed, 96, 1), 0.0)
    for k in range(4):
        g_ref[k, 16:48] = near[k]
    sums = [None] * 32
    for lag in range(-16, 17):
        product = None
        for step in range(2):
            source = g_ref[step, pl.ds(16 - lag, 8, stride=4)]
            receiver = g_ref[2 + step, pl.ds(16 + lag, 8, stride=4)]
            part = source * receiver
            product = part if product is None else product + part
        shifted = {}

        def shift(amount):
            if amount not in shifted:
                shifted[amount] = product if amount == 0 else pltpu.roll(product, -amount % 128, 1)
            return shifted[amount]

        for a in range(32):
            move = np.float32(lag) * SLOPES[a] / np.float32(4.0)
            low = np.floor(move)
            frac = float(move - low)
            term = shift(int(low)) * (1.0 - frac)
            if frac != 0.0:
                term = term + shift(int(low) + 1) * frac
            sums[a] = term if sums[a] is None else sums[a] + term
    lane = iota((8, 128), 1)
    for b in range(16):
        first, second = sums[2 * b], sums[2 * b + 1]
        packed = jnp.where(lane < 32, pltpu.roll(first, 112, 1), pltpu.roll(first, 80, 1))
        other = jnp.where(lane < 96, pltpu.roll(second, 48, 1), pltpu.roll(second, 16, 1))
        out_ref[b] = jnp.where(lane < 64, packed, other)


def arrange_kernel(got, out_ref):
    lane = iota((8, 128), 1)
    for t in range(8):
        even, odd = got[2 * t], got[2 * t + 1]
        out_ref[0, :, 128 * t : 128 * t + 128] = jnp.where(lane < 64, even, pltpu.roll(odd, 64, 1))
        out_ref[1, :, 128 * t : 128 * t + 128] = jnp.where(lane < 64, pltpu.roll(even, 64, 1), odd)


def call(kernel, outs, arrays, scalars=(), hbm=(), out_scalars=0, out_hbm=(), scratch=(), weight=0):
    smem, vmem = pl.BlockSpec(memory_space=pltpu.SMEM), pl.BlockSpec(memory_space=pltpu.VMEM)
    far = pl.BlockSpec(memory_space=pltpu.HBM)
    hbm = [
        pltpu.with_memory_space_constraint(array, pltpu.HBM) for array in hbm
    ]
    return pl.pallas_call(
        kernel,
        out_shape=[jax.ShapeDtypeStruct(shape, kind) for shape, kind in outs],
        in_specs=[smem] * len(scalars) + [far] * len(hbm) + [vmem] * len(arrays),
        out_specs=[
            smem if k >= len(outs) - out_scalars else far if k in out_hbm else vmem for k in range(len(outs))
        ],
        scratch_shapes=list(scratch),
        compiler_params=pltpu.CompilerParams(vmem_limit_bytes=VMEM_LIMIT),
        cost_estimate=pl.CostEstimate(flops=0, bytes_accessed=weight, transcendentals=0) if weight else None,
    )(*scalars, *hbm, *arrays)


def both_ways(to_next, to_last, axis):
    size = lax.axis_size(axis)
    from_last = lax.ppermute(to_next, axis, [(i, (i + 1) % size) for i in range(size)])
    from_next = lax.ppermute(to_last, axis, [((i + 1) % size, i) for i in range(size)])
    return from_last, from_next


def body(
    source_now,
    source_next,
    receiver_now,
    receiver_next,
    courant,
    source_cell,
    wavelet,
    receiver_cells,
    receiver_traces,
    strip_depth,
    strip_values,
):
    cells = receiver_cells.reshape(1, RECEIVERS)
    tile, sent_shape = (TX, TY, TZ), ((DEVICES, 1, 128), F32)
    listed = [((1, RECEIVERS), I32), ((2, RECEIVERS), F32)]
    fields = (source_now, receiver_now, source_next, receiver_next, courant, strip_depth, strip_values)
    up_y, down_y, near_wavelet, near_sm, near_rm, near_c, near_depth, near_values, sent = call(
        pack_kernel,
        [((113, 8, 128), F32)] * 2
        + [((1, 2), F32), *[(tile, F32)] * 3, ((8, 32), I32), ((2, 4, 8, 32), F32), sent_shape],
        [],
        hbm=[cells, receiver_traces, wavelet.reshape(1, 2), *fields],
        out_hbm=(8,),
        scratch=[pltpu.VMEM(*shape) for shape in (sent_shape, *listed)] + [pltpu.SemaphoreType.DMA((13,))],
    )
    before, after = both_ways(up_y, down_y, "gy")
    got = lax.all_to_all(sent, ("gx", "gy"), 0, 0, tiled=True)
    got = jnp.maximum(got.reshape(DEVICES, 128), -jnp.finfo(F32).max)
    edge, edge_courant, depths, strips, up_x, down_x = call(
        edge_kernel,
        [((2, 8, 16, 128), F32), ((8, 16, 128), F32), ((16, 128), I32), ((16, 128), F32)]
        + [((29, 8, 128), F32)] * 2,
        [up_y, near_sm, near_rm, near_c, near_depth, near_values, before, after],
        scratch=[
            pltpu.VMEM((2, 24, 32, 128), F32),
            pltpu.VMEM((2, 8, 16, 128), F32),
            pltpu.VMEM((2, 8, 16, 128), F32),
        ],
    )
    left, right = both_ways(up_x, down_x, "gx")
    inner, inner_courant = call(
        inner_kernel,
        [((2, 24, 16, 128), F32), ((24, 16, 128), F32)],
        [near_wavelet, up_y, near_sm, near_rm, near_c, before, after, depths, strips],
        scalars=[source_cell],
        scratch=[
            pltpu.VMEM((2, 32, 32, 128), F32),
            pltpu.VMEM((2, 24, 16, 128), F32),
            pltpu.VMEM((2, 24, 16, 128), F32),
        ],
    )
    sums = [((2, *tile), F32), (tile, F32), ((8, 8, 128), F32)]
    own, rim_y, rim_x, rounds = call(collect_kernel, [*sums, ((1,), I32)], [got, inner_courant], out_scalars=1, weight=1000)

    def another(state):
        turn, *partial = state
        (more,) = call(
            route_more_kernel,
            [sent_shape],
            [],
            scalars=[(turn * SLOTS).reshape(1)],
            hbm=[cells, receiver_traces],
            scratch=[pltpu.VMEM(*shape) for shape in listed] + [pltpu.SemaphoreType.DMA((2,))],
        )
        more = lax.all_to_all(more, ("gx", "gy"), 0, 0, tiled=True)
        return (turn + 1, *call(collect_more_kernel, sums, [more, *partial]))

    _, own, rim_y, rim_x = lax.while_loop(
        lambda state: state[0] < rounds[0], another, (jnp.int32(1), own, rim_y, rim_x)
    )
    source_field, receiver_field, near, up, down = call(
        steps_kernel,
        [(tile, F32), (tile, F32), ((4, 32, 128), F32), ((2, 16, 128), F32), ((2, 16, 128), F32)],
        [
            near_wavelet, up_y, near_c, near_depth, near_values,
            left, right, edge, edge_courant, inner, inner_courant, depths, own, rim_y, rim_x,
        ],
        out_hbm=(0, 1),
        scalars=[source_cell],
        scratch=[
            pltpu.VMEM((2, 40, 24, 128), F32),
            pltpu.VMEM((2, 2, 4, 16, 128), F32),
            pltpu.VMEM((2, 32, 8, 128), F32),
            pltpu.VMEM((4, 2, 32, 128), F32),
            pltpu.VMEM(tile, F32),
            pltpu.VMEM(tile, F32),
            pltpu.SemaphoreType.DMA((2,)),
        ],
    )
    near_left, near_right = both_ways(up, down, "gx")
    (angles,) = call(
        angles_kernel, [((16, 8, 128), F32)], [near, near_left, near_right],
        scratch=[pltpu.VMEM((4, 64, 128), F32)],
    )
    angles = lax.all_to_all(angles, "gy", 0, 0, tiled=True)
    (image,) = call(arrange_kernel, [((2, 8, 1024), F32)], [angles])
    return source_field, receiver_field, image


def solution(mesh):
    return jax.shard_map(
        body,
        mesh=mesh,
        in_specs=(
            P("gx", "gy", None),
            P("gx", "gy", None),
            P("gx", "gy", None),
            P("gx", "gy", None),
            P("gx", "gy", None),
            P(),
            P(),
            P(("gx", "gy")),
            P(None, ("gx", "gy")),
            P("gy", "gx"),
            P(None, None, "gy", "gx"),
        ),
        out_specs=(P("gx", "gy", None), P("gx", "gy", None), P("gy", "gx", None)),
        check_vma=False,
    )
```

```python
import math

import jax
import jax.numpy as jnp
import numpy as np
from jax import lax
from jax.experimental import pallas as pl
from jax.experimental.pallas import tpu as pltpu
from jax.sharding import PartitionSpec as P

COEFS = (-205.0 / 72.0, 8.0 / 5.0, -1.0 / 5.0, 8.0 / 315.0, -1.0 / 560.0)
SLOPES = np.array(
    [math.tan(math.pi * (-60.0 + 120.0 * (angle + 0.5) / 32.0) / 180.0) for angle in range(32)],
    dtype=np.float32,
)
GX, GY = 8, 16
TX, TY, TZ = 32, 8, 128
DEVICES = GX * GY
RECEIVERS = 256
SLOTS = 16
F32, BF16, I32 = jnp.float32, jnp.bfloat16, jnp.int32
VMEM_LIMIT = 24 * 1024 * 1024


def iota(shape, dim):
    return lax.broadcasted_iota(I32, shape, dim)


def halves(value):
    high = value.astype(BF16)
    return high, (value - high.astype(F32)).astype(BF16)


def dot_nt(left, right):
    return lax.dot_general(left, right, (((1,), (1,)), ((), ())), preferred_element_type=F32)


def routed(cells, traces, first_slot):
    x, y, z = cells >> 14, (cells >> 7) & 127, cells & 127
    tile_x, tile_y, in_x, in_y = x >> 5, y >> 3, x & 31, y & 7
    beside_y = jnp.where(in_y < 4, tile_y - 1, tile_y + 1)
    beside_x = jnp.where(in_x < 4, tile_x - 1, jnp.where(in_x >= 28, tile_x + 1, -1))
    to_y = jnp.where((beside_y >= 0) & (beside_y < GY), tile_x * GY + beside_y, -1)
    to_x = jnp.where((beside_x >= 0) & (beside_x < GX), beside_x * GY + tile_y, -1)
    rim_x = jnp.where(in_x < 4, in_x + 4, in_x - 28)
    classes = (
        (tile_x * GY + tile_y, (in_x * 8 + in_y) * 128 + z, 2),
        (to_y, (in_x * 8 + (in_y ^ 4)) * 128 + z, 1),
        (to_x, (rim_x * 8 + in_y) * 128 + z, 1),
    )
    earlier = jnp.where(
        iota((RECEIVERS, RECEIVERS), 0) < iota((RECEIVERS, RECEIVERS), 1), 1.0, 0.0
    ).astype(BF16)
    device = iota((DEVICES, RECEIVERS), 0)
    slot = iota((SLOTS, RECEIVERS), 0).astype(F32) + first_slot.astype(F32)
    hits, kept, last_rank, row = [], [], None, 0
    for target, place, steps in classes:
        hit = jnp.where(device == target, 1.0, 0.0)
        before = jnp.dot(hit.astype(BF16), earlier, preferred_element_type=F32)
        rank = jnp.sum(hit * before, axis=0, keepdims=True)
        last_rank = rank if last_rank is None else jnp.maximum(last_rank, rank)
        mine = slot == rank
        rows = [jnp.where(mine, place.astype(F32), 0.0)]
        rows += [jnp.where(mine, traces[s : s + 1], 0.0) for s in range(steps)]
        size = SLOTS * len(rows)
        above = [jnp.zeros((row, RECEIVERS), F32)] if row else []
        below = [jnp.zeros((128 - row - size, RECEIVERS), F32)]
        kept.append(jnp.concatenate(above + rows + below, axis=0))
        hits.append(hit.astype(BF16))
        row += size
    hits = jnp.concatenate(hits, axis=1)
    high, low = halves(jnp.concatenate(kept, axis=1))
    sent = dot_nt(hits, high) + dot_nt(hits, low)
    rounds = (jnp.max(last_rank, axis=1, keepdims=True).astype(I32) // SLOTS + 1).astype(F32)
    return jnp.where(iota((DEVICES, 128), 1) >= row, rounds, sent)


def route_more_kernel(first_ref, cells, traces, sent_ref, cells_v, traces_v, sems):
    for copy in started([(cells, cells_v), (traces, traces_v)], sems):
        copy.wait()
    sent_ref[:, 0, :] = routed(cells_v[...], traces_v[...], first_ref[0])


def collected(got):
    rows = got.T
    sums, row = [], 0
    down = iota((TZ, DEVICES), 0).astype(F32).astype(BF16)
    unit, zero = jnp.ones((), BF16), jnp.zeros((), BF16)
    for columns, steps in ((TX * 8, 2), (TX * 8, 1), (64, 1)):
        cell = rows[row : row + SLOTS].astype(I32)
        column, depth = (cell >> 7).astype(F32), (cell & 127).astype(F32)
        at = iota((columns, DEVICES), 0).astype(F32).astype(BF16)
        one, parts = [], [[] for _ in range(2 * steps)]
        for k in range(SLOTS):
            one.append(jnp.where(at == column[k : k + 1].astype(BF16), unit, zero))
            same = down == depth[k : k + 1].astype(BF16)
            for s in range(steps):
                value = rows[row + (s + 1) * SLOTS + k : row + (s + 1) * SLOTS + k + 1]
                high, low = halves(value)
                parts[2 * s].append(jnp.where(same, high, zero))
                parts[2 * s + 1].append(jnp.where(same, low, zero))
        one = jnp.concatenate(one, axis=1)
        both = dot_nt(one, jnp.concatenate([jnp.concatenate(part, axis=1) for part in parts], axis=0))
        for s in range(steps):
            sums.append(both[:, 256 * s : 256 * s + 128] + both[:, 256 * s + 128 : 256 * s + 256])
        row += SLOTS * (steps + 1)
    return sums


def collect_kernel(got_ref, inner_courant, own_ref, rim_y_ref, rim_x_ref, rounds_ref):
    got = got_ref[...]
    own_0, own_1, rim_y, rim_x = collected(got)
    own_ref[0] = own_0.reshape(TX, 8, 128)
    own_ref[1] = own_1.reshape(TX, 8, 128)
    rim_y_ref[...] = rim_y.reshape(TX, 8, 128)
    rim_x_ref[...] = rim_x.reshape(8, 8, 128)
    rounds_ref[0] = jnp.max(got[:, 112:128]).astype(I32)


def collect_more_kernel(got_ref, own_in, rim_y_in, rim_x_in, own_ref, rim_y_ref, rim_x_ref):
    own_0, own_1, rim_y, rim_x = collected(got_ref[:, 0, :])
    own_ref[0] = own_in[0] + own_0.reshape(TX, 8, 128)
    own_ref[1] = own_in[1] + own_1.reshape(TX, 8, 128)
    rim_y_ref[...] = rim_y_in[...] + rim_y.reshape(TX, 8, 128)
    rim_x_ref[...] = rim_x_in[...] + rim_x.reshape(8, 8, 128)


def strip_values_tile(values, step, rows):
    return jnp.concatenate([values[step, layer][rows] for layer in range(4)], axis=1)


def wide(depth):
    return jnp.concatenate([depth, jnp.zeros((depth.shape[0], 96), depth.dtype)], axis=1)


def started(copies, sems):
    copies = [pltpu.make_async_copy(*ends, sems.at[k]) for k, ends in enumerate(copies)]
    for copy in copies:
        copy.start()
    return copies


def pack_kernel(
    cells, traces, wavelet, s0, r0, sm, rm, c, depth, values,
    first_y, second_y, wavelet_ref, sm_v, rm_v, c_v, depth_v, values_v, sent_ref,
    sent_v, cells_v, traces_v, sems,
):
    copies = started(
        [
            (cells, cells_v), (traces, traces_v), (depth, depth_v), (values, values_v), (wavelet, wavelet_ref),
            (sm, sm_v), (rm, rm_v), (c, c_v),
            (s0, first_y.at[0:32]), (r0, first_y.at[32:64]), (s0, second_y.at[0:32]), (r0, second_y.at[32:64]),
        ],
        sems,
    )
    for copy in copies[:2]:
        copy.wait()
    sent_v[:, 0, :] = routed(cells_v[...], traces_v[...], jnp.int32(0))
    out = pltpu.make_async_copy(sent_v, sent_ref, sems.at[12])
    out.start()
    for copy in copies[2:8]:
        copy.wait()
    even = lax.axis_index("gy") % 2 == 0
    strips, depths = strip_values_tile(values_v, 0, slice(0, 8)), wide(depth_v[...].astype(F32))
    for ref, high in ((first_y, even), (second_y, ~even)):

        def four(rows):
            return jnp.where(high, rows[..., 4:8, :], rows[..., 0:4, :])

        ref[64:96, 0:4] = four(sm_v[...])
        ref[64:96, 4:8] = four(rm_v[...])
        ref[96:112, 0:4] = four(c_v[0:16])
        ref[96:112, 4:8] = four(c_v[16:32])
        ref[112, 0:4] = four(strips)
        ref[112, 4:8] = four(depths)
    for copy in copies[8:]:
        copy.wait()
    out.wait()


def depth_matrix():
    apart = jnp.abs(iota((TZ, TZ), 0) - iota((TZ, TZ), 1))
    weights = jnp.zeros((TZ, TZ), F32)
    for reach in range(1, 5):
        weights = jnp.where(apart == reach, COEFS[reach], weights)
    high, low = halves(weights)
    top = jnp.concatenate([high, low], axis=1)
    return jnp.concatenate([top, jnp.concatenate([high, jnp.zeros_like(low)], axis=1)], axis=0)


def depth_sums(rows, matrix):
    both = jnp.dot(jnp.concatenate(halves(rows), axis=1), matrix, preferred_element_type=F32)
    return both[:, :128] + both[:, 128:]


def curvature(ref, f, x, row, depth_sum):
    tile = ref[f, x, row : row + 8]
    total = (3.0 * COEFS[0]) * tile + depth_sum
    for reach in range(1, 5):
        pairs = ref[f, x + reach, row : row + 8] + ref[f, x - reach, row : row + 8]
        pairs = pairs + ref[f, x, row + reach : row + reach + 8]
        pairs = pairs + ref[f, x, row - reach : row - reach + 8]
        total = total + COEFS[reach] * pairs
    return tile, total


def overwritten(tile, depths, values, lane_start):
    lane = iota((8, 128), 1)
    column = jnp.full((8, 128), lane_start, I32)
    relative = lane - jnp.take_along_axis(depths, column, axis=1)
    fill = jnp.take_along_axis(values, (relative & 3) * 32 + column, axis=1)
    return jnp.where((relative >= 0) & (relative < 4), fill, tile)


def keeps(axis, size):
    at = lax.axis_index(axis)
    return jnp.where(at > 0, 1.0, 0.0), jnp.where(at < size - 1, 1.0, 0.0)


def pulse(source_cell, wavelet, step, row):
    cell = source_cell[0]
    lane, sublane = iota((8, 128), 1), iota((8, 128), 0)
    at_row = sublane + (row + lax.axis_index("gy") * TY) == (cell >> 7) & 127
    return jnp.where((lane == cell & 127) & at_row, wavelet[0:1, step : step + 1], 0.0)


def source_layer(source_cell):
    return (source_cell[0] >> 14) - lax.axis_index("gx") * TX


def advanced(i, at, x, e_ref, z_ref, m_ref, courant_ref, depth_ref, v_ref, pulses, source_x, new_ref):
    for t in range(2):
        rows = slice(8 * t, 8 * t + 8)
        courant = courant_ref[i, rows]
        now, total = curvature(e_ref, 0, at, 8 + 8 * t, z_ref[0, i, rows])
        if pulses is not None:
            total = total - jnp.where(x == source_x, pulses[t], 0.0)
        new = 2.0 * now - m_ref[0, i, rows] + courant * total
        new_ref[0, i, rows] = overwritten(new, depth_ref[rows], v_ref[rows], x)
        now, total = curvature(e_ref, 1, at, 8 + 8 * t, z_ref[1, i, rows])
        new_ref[1, i, rows] = 2.0 * now - m_ref[1, i, rows] + courant * total


def in_order(beside, first, second):
    even = lax.axis_index("gy") % 2 == 0

    @pl.when(even)
    def _():
        beside(second, first)

    @pl.when(~even)
    def _():
        beside(first, second)


def edge_kernel(
    own_y, sm, rm, c, depth, values, first, second,
    new_ref, courant_ref, depth_ref, v_ref, up_ref, down_ref,
    e_ref, m_ref, z_ref,
):
    keep_before, keep_after = keeps("gy", GY)
    spans = ((4, 0), (12, 24))
    for f in range(2):
        e_ref[f, 0:4, 8:24] = jnp.zeros((4, 16, 128), F32)
        e_ref[f, 20:24, 8:24] = jnp.zeros((4, 16, 128), F32)
        for to, start in spans:
            e_ref[f, to : to + 8, 12:20] = own_y[32 * f + start : 32 * f + start + 8]
    v_ref[4:12] = strip_values_tile(values, 0, slice(0, 8))
    depth_ref[4:12] = wide(depth[...])
    for to, start in ((0, 0), (4, 28)):
        layers = slice(to, to + 4)
        m_ref[0, layers, 4:12] = sm[start : start + 4]
        m_ref[1, layers, 4:12] = rm[start : start + 4]
        courant_ref[layers, 4:12] = c[start : start + 4]

    def beside(before, after):
        for f in range(2):
            for to, start in spans:
                layers = slice(32 * f + start, 32 * f + start + 8)
                e_ref[f, to : to + 8, 4:12] = before[layers] * keep_before
                e_ref[f, to : to + 8, 20:28] = after[layers] * keep_after
        for ref, keep, rows in ((before, keep_before, slice(0, 4)), (after, keep_after, slice(12, 16))):
            for to, start in ((0, 0), (4, 28)):
                layers, half = slice(to, to + 4), start // 16
                m_ref[0, layers, rows] = ref[64 + start : 68 + start, 0:4] * keep
                m_ref[1, layers, rows] = ref[64 + start : 68 + start, 4:8] * keep
                at = 96 + start - 16 * half
                courant_ref[layers, rows] = ref[at : at + 4, 4 * half : 4 * half + 4] * keep
            v_ref[rows] = ref[112, 0:4] * keep
            depth_ref[rows] = (ref[112, 4:8] * keep).astype(I32)

    in_order(beside, first, second)
    matrix = depth_matrix()
    for f in range(2):
        for half in range(2):
            rows = e_ref[f, 4 + 12 * half : 8 + 12 * half, 8:24].reshape(64, 128)
            z_ref[f, 4 * half : 4 * half + 4] = depth_sums(rows, matrix).reshape(4, 16, 128)
    for i in range(8):
        at, x = (i + 4, i) if i < 4 else (i + 12, i + 24)
        advanced(
            i, at, x, e_ref, z_ref, m_ref, courant_ref, depth_ref, v_ref, None, None, new_ref
        )
    for ref, to, rim, at in ((up_ref, 4, 28, 16), (down_ref, 0, 0, 4)):
        for f in range(2):
            ref[4 * f : 4 * f + 4] = new_ref[f, to : to + 4, 4:12]
            ref[12 + 4 * f : 16 + 4 * f] = own_y[32 * f + rim : 32 * f + rim + 4]
            ref[20 + 4 * f : 24 + 4 * f, 0:4] = e_ref[f, at : at + 4, 8:12]
            ref[20 + 4 * f : 24 + 4 * f, 4:8] = e_ref[f, at : at + 4, 20:24]
        ref[8:12] = c[rim : rim + 4]
        ref[28] = depth_ref[4:12].astype(F32)


def inner_kernel(
    source_cell,
    wavelet, own_y, sm, rm, c, first, second, depths, values,
    new_ref, courant_ref,
    e_ref, m_ref, z_ref,
):
    keep_before, keep_after = keeps("gy", GY)
    for f in range(2):
        e_ref[f, :, 12:20] = own_y[32 * f : 32 * f + 32]
    m_ref[0, :, 4:12] = sm[4:28]
    m_ref[1, :, 4:12] = rm[4:28]
    courant_ref[:, 4:12] = c[4:28]

    def beside(before, after):
        for f in range(2):
            e_ref[f, :, 4:12] = before[32 * f : 32 * f + 32] * keep_before
            e_ref[f, :, 20:28] = after[32 * f : 32 * f + 32] * keep_after
        for ref, keep, rows in ((before, keep_before, slice(0, 4)), (after, keep_after, slice(12, 16))):
            m_ref[0, :, rows] = ref[68:92, 0:4] * keep
            m_ref[1, :, rows] = ref[68:92, 4:8] * keep
            courant_ref[0:12, rows] = ref[100:112, 0:4] * keep
            courant_ref[12:24, rows] = ref[96:108, 4:8] * keep

    in_order(beside, first, second)
    pulses = [pulse(source_cell, wavelet, 0, 8 * t - 4) for t in range(2)]
    source_x = source_layer(source_cell)
    matrix = depth_matrix()
    for f in range(2):
        rows = e_ref[f, 4:28, 8:24].reshape(384, 128)
        z_ref[f] = depth_sums(rows, matrix).reshape(24, 16, 128)

    def layer(i, carry):
        advanced(
            i, i + 4, i + 4, e_ref, z_ref, m_ref, courant_ref, depths, values, pulses, source_x, new_ref
        )
        return carry

    lax.fori_loop(0, 24, layer, 0, unroll=8)


def unless_strip(depths, column, amount):
    relative = iota((8, 128), 1) - depths[:, column : column + 1]
    return jnp.where((relative >= 0) & (relative < 4), 0.0, amount)


def steps_kernel(
    source_cell,
    wavelet, own_y, c, depth, values, left, right, edge, edge_courant, inner, inner_courant, depths,
    own, rim_y, rim_x,
    s_out, r_out, near_ref, up_ref, down_ref,
    o_ref, h_ref, z_ref, sub_ref, s_v, r_v, sems,
):
    keep_left, keep_right = keeps("gx", GX)
    s0, r0 = own_y.at[0:32], own_y.at[32:64]
    for new1, courant, start, first, size in (
        (edge, edge_courant, 0, 0, 4), (inner, inner_courant, 0, 4, 24), (edge, edge_courant, 4, 28, 4)
    ):
        to, part, x = slice(first + 4, first + 4 + size), slice(start, start + size), slice(first, first + size)
        o_ref[0, to, 4:20] = new1[0, part]
        o_ref[1, to, 8:16] = new1[1, part, 4:12] + courant[part, 4:12] * own[0, x]
        o_ref[1, to, 4:8] = new1[1, part, 0:4] + courant[part, 0:4] * rim_y[x, 0:4]
        o_ref[1, to, 16:20] = new1[1, part, 12:16] + courant[part, 12:16] * rim_y[x, 4:8]
    source_x = source_layer(source_cell)
    pulses = [pulse(source_cell, wavelet, 0, row) for row in (-4, 4, 0)]
    for side, ref, keep in ((0, left, keep_left), (1, right, keep_right)):
        beyond_depths = (ref[28] * keep).astype(I32)
        for f in range(2):
            h_ref[f, side, :, 4:12] = ref[12 + 4 * f : 16 + 4 * f] * keep
            h_ref[f, side, :, 0:4] = ref[20 + 4 * f : 24 + 4 * f, 0:4] * keep
            h_ref[f, side, :, 12:16] = ref[20 + 4 * f : 24 + 4 * f, 4:8] * keep
        for n in range(4):
            x = 31 - n if side else n
            for f in range(2):
                for t in range(2):
                    rows = slice(8 * t, 8 * t + 8)
                    amount = None
                    for reach in range(n + 1, 5):
                        away = reach - n
                        term = COEFS[reach] * h_ref[f, side, away - 1 if side else 4 - away, rows]
                        amount = term if amount is None else amount + term
                    if f == 0:
                        amount = amount - jnp.where(x == source_x, pulses[t], 0.0)
                    amount = edge_courant[x - 24 if side else x, rows] * amount
                    if f == 0:
                        amount = unless_strip(depths[rows], x, amount)
                    at = slice(4 + 8 * t, 12 + 8 * t)
                    o_ref[f, x + 4, at] = o_ref[f, x + 4, at] + amount
            k = n if side else 3 - n
            for f, field in ((0, s0), (1, r0)):
                amount = None
                for reach in range(n + 1, 5):
                    inward = reach - n - 1
                    term = COEFS[reach] * field[31 - inward if side else inward]
                    amount = term if amount is None else amount + term
                if f == 0:
                    beyond = 32 + n if side else -1 - n
                    amount = amount - jnp.where(beyond == source_x, pulses[2], 0.0)
                else:
                    amount = amount + rim_x[4 * side + k]
                amount = ref[8 + k] * amount
                if f == 0:
                    amount = unless_strip(beyond_depths, k if side else 28 + k, amount)
                o_ref[f, 36 + n if side else 3 - n, 8:16] = (ref[4 * f + k] + amount) * keep
    matrix = depth_matrix()
    for f in range(2):
        rows = o_ref[f, 4:36, 8:16].reshape(256, 128)
        z_ref[f] = depth_sums(rows, matrix).reshape(32, 8, 128)
    late_values = strip_values_tile(values, 1, slice(0, 8))
    near_depth = wide(depth[...])
    late_pulse = pulse(source_cell, wavelet, 1, 0)

    def second(x, carry):
        now, total = curvature(o_ref, 0, x + 4, 8, z_ref[0, x])
        total = total - jnp.where(x == source_x, late_pulse, 0.0)
        new = 2.0 * now - s0[x] + c[x] * total
        new = overwritten(new, near_depth, late_values, x)
        s_v[x] = new
        for j in range(2):
            sub_ref[0, j, pl.ds(x, 1)] = now[4 * j : 4 * j + 1]
            sub_ref[1, j, pl.ds(x, 1)] = new[4 * j : 4 * j + 1]
        now, total = curvature(o_ref, 1, x + 4, 8, z_ref[1, x])
        new = 2.0 * now - r0[x] + c[x] * (total + own[1, x])
        r_v[x] = new
        for j in range(2):
            sub_ref[2, j, pl.ds(x, 1)] = now[4 * j : 4 * j + 1]
            sub_ref[3, j, pl.ds(x, 1)] = new[4 * j : 4 * j + 1]
        return carry

    lax.fori_loop(0, 32, second, 0, unroll=16)
    copies = started([(s_v, s_out), (r_v, r_out)], sems)
    z, to = iota((TZ, 128), 0), iota((TZ, 128), 1)
    totals = []
    for k in range(4):
        total = None
        for j in range(2):
            pick = jnp.where((z & 3 == 0) & (to == (z >> 2) + (16 + 64 * j)), 1.0, 0.0)
            part = jnp.dot(
                sub_ref[k, j], pick, precision=lax.Precision.HIGHEST, preferred_element_type=F32
            )
            total = part if total is None else total + part
        near_ref[k] = total
        totals.append(total)
    for f in range(2):
        packed = totals[2 * f] + pltpu.roll(totals[2 * f + 1], 32, 1)
        up_ref[f] = packed[16:32]
        down_ref[f] = packed[0:16]
    for copy in copies:
        copy.wait()


def angles_kernel(near, left, right, out_ref, g_ref):
    keep_left, keep_right = keeps("gx", GX)
    lane = iota((16, 128), 1)
    held = ((lane >= 16) & (lane < 48)) | ((lane >= 80) & (lane < 112))
    for f in range(2):
        for ref, keep, rows in ((left, keep_left, slice(0, 16)), (right, keep_right, slice(48, 64))):
            packed = ref[f] * keep
            g_ref[2 * f, rows] = jnp.where(held, packed, 0.0)
            g_ref[2 * f + 1, rows] = jnp.where(held, pltpu.roll(packed, 96, 1), 0.0)
    for k in range(4):
        g_ref[k, 16:48] = near[k]
    sums = [None] * 32
    for lag in range(-16, 17):
        product = None
        for step in range(2):
            source = g_ref[step, pl.ds(16 - lag, 8, stride=4)]
            receiver = g_ref[2 + step, pl.ds(16 + lag, 8, stride=4)]
            part = source * receiver
            product = part if product is None else product + part
        shifted = {}

        def shift(amount):
            if amount not in shifted:
                shifted[amount] = product if amount == 0 else pltpu.roll(product, -amount % 128, 1)
            return shifted[amount]

        for a in range(32):
            move = np.float32(lag) * SLOPES[a] / np.float32(4.0)
            low = np.floor(move)
            frac = float(move - low)
            term = shift(int(low)) * (1.0 - frac)
            if frac != 0.0:
                term = term + shift(int(low) + 1) * frac
            sums[a] = term if sums[a] is None else sums[a] + term
    lane = iota((8, 128), 1)
    for b in range(16):
        first, second = sums[2 * b], sums[2 * b + 1]
        packed = jnp.where(lane < 32, pltpu.roll(first, 112, 1), pltpu.roll(first, 80, 1))
        other = jnp.where(lane < 96, pltpu.roll(second, 48, 1), pltpu.roll(second, 16, 1))
        out_ref[b] = jnp.where(lane < 64, packed, other)


def arrange_kernel(got, out_ref):
    lane = iota((8, 128), 1)
    for t in range(8):
        even, odd = got[2 * t], got[2 * t + 1]
        out_ref[0, :, 128 * t : 128 * t + 128] = jnp.where(lane < 64, even, pltpu.roll(odd, 64, 1))
        out_ref[1, :, 128 * t : 128 * t + 128] = jnp.where(lane < 64, pltpu.roll(even, 64, 1), odd)


def call(kernel, outs, arrays, scalars=(), hbm=(), out_scalars=0, out_hbm=(), scratch=(), weight=0):
    smem, vmem = pl.BlockSpec(memory_space=pltpu.SMEM), pl.BlockSpec(memory_space=pltpu.VMEM)
    far = pl.BlockSpec(memory_space=pltpu.HBM)
    hbm = [
        pltpu.with_memory_space_constraint(array, pltpu.HBM) for array in hbm
    ]
    return pl.pallas_call(
        kernel,
        out_shape=[jax.ShapeDtypeStruct(shape, kind) for shape, kind in outs],
        in_specs=[smem] * len(scalars) + [far] * len(hbm) + [vmem] * len(arrays),
        out_specs=[
            smem if k >= len(outs) - out_scalars else far if k in out_hbm else vmem for k in range(len(outs))
        ],
        scratch_shapes=list(scratch),
        compiler_params=pltpu.CompilerParams(vmem_limit_bytes=VMEM_LIMIT),
        cost_estimate=pl.CostEstimate(flops=0, bytes_accessed=weight, transcendentals=0) if weight else None,
    )(*scalars, *hbm, *arrays)


def both_ways(to_next, to_last, axis):
    size = lax.axis_size(axis)
    from_last = lax.ppermute(to_next, axis, [(i, (i + 1) % size) for i in range(size)])
    from_next = lax.ppermute(to_last, axis, [((i + 1) % size, i) for i in range(size)])
    return from_last, from_next


def body(
    source_now,
    source_next,
    receiver_now,
    receiver_next,
    courant,
    source_cell,
    wavelet,
    receiver_cells,
    receiver_traces,
    strip_depth,
    strip_values,
):
    cells = receiver_cells.reshape(1, RECEIVERS)
    tile, sent_shape = (TX, TY, TZ), ((DEVICES, 1, 128), F32)
    listed = [((1, RECEIVERS), I32), ((2, RECEIVERS), F32)]
    fields = (source_now, receiver_now, source_next, receiver_next, courant, strip_depth, strip_values)
    first_y, second_y, near_wavelet, near_sm, near_rm, near_c, near_depth, near_values, sent = call(
        pack_kernel,
        [((113, 8, 128), F32)] * 2
        + [((1, 2), F32), *[(tile, F32)] * 3, ((8, 32), I32), ((2, 4, 8, 32), F32), sent_shape],
        [],
        hbm=[cells, receiver_traces, wavelet.reshape(1, 2), *fields],
        out_hbm=(8,),
        scratch=[pltpu.VMEM(*shape) for shape in (sent_shape, *listed)] + [pltpu.SemaphoreType.DMA((13,))],
    )
    pairs = [(i, i ^ 1) for i in range(GY)]
    first = lax.ppermute(first_y, "gy", pairs)
    second = lax.ppermute(second_y, "gy", [(i, (i + 1 if i % 2 else i - 1) % GY) for i in range(GY)])
    got = lax.all_to_all(sent, ("gx", "gy"), 0, 0, tiled=True)
    got = jnp.maximum(got.reshape(DEVICES, 128), -jnp.finfo(F32).max)
    edge, edge_courant, depths, strips, up_x, down_x = call(
        edge_kernel,
        [((2, 8, 16, 128), F32), ((8, 16, 128), F32), ((16, 128), I32), ((16, 128), F32)]
        + [((29, 8, 128), F32)] * 2,
        [first_y, near_sm, near_rm, near_c, near_depth, near_values, first, second],
        scratch=[
            pltpu.VMEM((2, 24, 32, 128), F32),
            pltpu.VMEM((2, 8, 16, 128), F32),
            pltpu.VMEM((2, 8, 16, 128), F32),
        ],
    )
    left, right = both_ways(up_x, down_x, "gx")
    inner, inner_courant = call(
        inner_kernel,
        [((2, 24, 16, 128), F32), ((24, 16, 128), F32)],
        [near_wavelet, first_y, near_sm, near_rm, near_c, first, second, depths, strips],
        scalars=[source_cell],
        scratch=[
            pltpu.VMEM((2, 32, 32, 128), F32),
            pltpu.VMEM((2, 24, 16, 128), F32),
            pltpu.VMEM((2, 24, 16, 128), F32),
        ],
    )
    sums = [((2, *tile), F32), (tile, F32), ((8, 8, 128), F32)]
    own, rim_y, rim_x, rounds = call(collect_kernel, [*sums, ((1,), I32)], [got, inner_courant], out_scalars=1, weight=1000)

    def another(state):
        turn, *partial = state
        (more,) = call(
            route_more_kernel,
            [sent_shape],
            [],
            scalars=[(turn * SLOTS).reshape(1)],
            hbm=[cells, receiver_traces],
            scratch=[pltpu.VMEM(*shape) for shape in listed] + [pltpu.SemaphoreType.DMA((2,))],
        )
        more = lax.all_to_all(more, ("gx", "gy"), 0, 0, tiled=True)
        return (turn + 1, *call(collect_more_kernel, sums, [more, *partial]))

    _, own, rim_y, rim_x = lax.while_loop(
        lambda state: state[0] < rounds[0], another, (jnp.int32(1), own, rim_y, rim_x)
    )
    source_field, receiver_field, near, up, down = call(
        steps_kernel,
        [(tile, F32), (tile, F32), ((4, 32, 128), F32), ((2, 16, 128), F32), ((2, 16, 128), F32)],
        [
            near_wavelet, first_y, near_c, near_depth, near_values,
            left, right, edge, edge_courant, inner, inner_courant, depths, own, rim_y, rim_x,
        ],
        out_hbm=(0, 1),
        scalars=[source_cell],
        scratch=[
            pltpu.VMEM((2, 40, 24, 128), F32),
            pltpu.VMEM((2, 2, 4, 16, 128), F32),
            pltpu.VMEM((2, 32, 8, 128), F32),
            pltpu.VMEM((4, 2, 32, 128), F32),
            pltpu.VMEM(tile, F32),
            pltpu.VMEM(tile, F32),
            pltpu.SemaphoreType.DMA((2,)),
        ],
    )
    near_left, near_right = both_ways(up, down, "gx")
    (angles,) = call(
        angles_kernel, [((16, 8, 128), F32)], [near, near_left, near_right],
        scratch=[pltpu.VMEM((4, 64, 128), F32)],
    )
    angles = lax.all_to_all(angles, "gy", 0, 0, tiled=True)
    (image,) = call(arrange_kernel, [((2, 8, 1024), F32)], [angles])
    return source_field, receiver_field, image


def solution(mesh):
    return jax.shard_map(
        body,
        mesh=mesh,
        in_specs=(
            P("gx", "gy", None),
            P("gx", "gy", None),
            P("gx", "gy", None),
            P("gx", "gy", None),
            P("gx", "gy", None),
            P(),
            P(),
            P(("gx", "gy")),
            P(None, ("gx", "gy")),
            P("gy", "gx"),
            P(None, None, "gy", "gx"),
        ),
        out_specs=(P("gx", "gy", None), P("gx", "gy", None), P("gy", "gx", None)),
        check_vma=False,
    )
```

```python
import math

import jax
import jax.numpy as jnp
import numpy as np
from jax import lax
from jax.experimental import pallas as pl
from jax.experimental.pallas import tpu as pltpu
from jax.sharding import PartitionSpec as P

COEFS = (-205.0 / 72.0, 8.0 / 5.0, -1.0 / 5.0, 8.0 / 315.0, -1.0 / 560.0)
SLOPES = np.array(
    [math.tan(math.pi * (-60.0 + 120.0 * (angle + 0.5) / 32.0) / 180.0) for angle in range(32)],
    dtype=np.float32,
)
GX, GY = 8, 16
TX, TY, TZ = 32, 8, 128
DEVICES = GX * GY
RECEIVERS = 256
SLOTS = 16
F32, BF16, I32 = jnp.float32, jnp.bfloat16, jnp.int32
VMEM_LIMIT = 24 * 1024 * 1024


def iota(shape, dim):
    return lax.broadcasted_iota(I32, shape, dim)


def halves(value):
    high = value.astype(BF16)
    return high, (value - high.astype(F32)).astype(BF16)


def dot_nt(left, right):
    return lax.dot_general(left, right, (((1,), (1,)), ((), ())), preferred_element_type=F32)


def routed(cells, traces, first_slot):
    x, y, z = cells >> 14, (cells >> 7) & 127, cells & 127
    tile_x, tile_y, in_x, in_y = x >> 5, y >> 3, x & 31, y & 7
    beside_y = jnp.where(in_y < 4, tile_y - 1, tile_y + 1)
    beside_x = jnp.where(in_x < 4, tile_x - 1, jnp.where(in_x >= 28, tile_x + 1, -1))
    to_y = jnp.where((beside_y >= 0) & (beside_y < GY), tile_x * GY + beside_y, -1)
    to_x = jnp.where((beside_x >= 0) & (beside_x < GX), beside_x * GY + tile_y, -1)
    rim_x = jnp.where(in_x < 4, in_x + 4, in_x - 28)
    classes = (
        (tile_x * GY + tile_y, (in_x * 8 + in_y) * 128 + z, 2),
        (to_y, (in_x * 8 + (in_y ^ 4)) * 128 + z, 1),
        (to_x, (rim_x * 8 + in_y) * 128 + z, 1),
    )
    earlier = jnp.where(
        iota((RECEIVERS, RECEIVERS), 0) < iota((RECEIVERS, RECEIVERS), 1), 1.0, 0.0
    ).astype(BF16)
    device = iota((DEVICES, RECEIVERS), 0)
    slot = iota((SLOTS, RECEIVERS), 0).astype(F32) + first_slot.astype(F32)
    hits, kept, last_rank, row = [], [], None, 0
    for target, place, steps in classes:
        hit = jnp.where(device == target, 1.0, 0.0)
        before = jnp.dot(hit.astype(BF16), earlier, preferred_element_type=F32)
        rank = jnp.sum(hit * before, axis=0, keepdims=True)
        last_rank = rank if last_rank is None else jnp.maximum(last_rank, rank)
        mine = slot == rank
        rows = [jnp.where(mine, place.astype(F32), 0.0)]
        rows += [jnp.where(mine, traces[s : s + 1], 0.0) for s in range(steps)]
        size = SLOTS * len(rows)
        above = [jnp.zeros((row, RECEIVERS), F32)] if row else []
        below = [jnp.zeros((128 - row - size, RECEIVERS), F32)]
        kept.append(jnp.concatenate(above + rows + below, axis=0))
        hits.append(hit.astype(BF16))
        row += size
    hits = jnp.concatenate(hits, axis=1)
    high, low = halves(jnp.concatenate(kept, axis=1))
    sent = dot_nt(hits, high) + dot_nt(hits, low)
    rounds = (jnp.max(last_rank, axis=1, keepdims=True).astype(I32) // SLOTS + 1).astype(F32)
    return jnp.where(iota((DEVICES, 128), 1) >= row, rounds, sent)


def route_more_kernel(first_ref, cells, traces, sent_ref, cells_v, traces_v, sems):
    for copy in started([(cells, cells_v), (traces, traces_v)], sems):
        copy.wait()
    sent_ref[:, 0, :] = routed(cells_v[...], traces_v[...], first_ref[0])


def collected(got):
    rows = got.T
    sums, row = [], 0
    down = iota((TZ, DEVICES), 0).astype(F32).astype(BF16)
    unit, zero = jnp.ones((), BF16), jnp.zeros((), BF16)
    for columns, steps in ((TX * 8, 2), (TX * 8, 1), (64, 1)):
        cell = rows[row : row + SLOTS].astype(I32)
        column, depth = (cell >> 7).astype(F32), (cell & 127).astype(F32)
        at = iota((columns, DEVICES), 0).astype(F32).astype(BF16)
        one, parts = [], [[] for _ in range(2 * steps)]
        for k in range(SLOTS):
            one.append(jnp.where(at == column[k : k + 1].astype(BF16), unit, zero))
            same = down == depth[k : k + 1].astype(BF16)
            for s in range(steps):
                value = rows[row + (s + 1) * SLOTS + k : row + (s + 1) * SLOTS + k + 1]
                high, low = halves(value)
                parts[2 * s].append(jnp.where(same, high, zero))
                parts[2 * s + 1].append(jnp.where(same, low, zero))
        one = jnp.concatenate(one, axis=1)
        both = dot_nt(one, jnp.concatenate([jnp.concatenate(part, axis=1) for part in parts], axis=0))
        for s in range(steps):
            sums.append(both[:, 256 * s : 256 * s + 128] + both[:, 256 * s + 128 : 256 * s + 256])
        row += SLOTS * (steps + 1)
    return sums


def collect_kernel(got_ref, inner_courant, own_ref, rim_y_ref, rim_x_ref, rounds_ref):
    got = got_ref[...]
    own_0, own_1, rim_y, rim_x = collected(got)
    own_ref[0] = own_0.reshape(TX, 8, 128)
    own_ref[1] = own_1.reshape(TX, 8, 128)
    rim_y_ref[...] = rim_y.reshape(TX, 8, 128)
    rim_x_ref[...] = rim_x.reshape(8, 8, 128)
    rounds_ref[0] = jnp.max(got[:, 112:128]).astype(I32)


def collect_more_kernel(got_ref, own_in, rim_y_in, rim_x_in, own_ref, rim_y_ref, rim_x_ref):
    own_0, own_1, rim_y, rim_x = collected(got_ref[:, 0, :])
    own_ref[0] = own_in[0] + own_0.reshape(TX, 8, 128)
    own_ref[1] = own_in[1] + own_1.reshape(TX, 8, 128)
    rim_y_ref[...] = rim_y_in[...] + rim_y.reshape(TX, 8, 128)
    rim_x_ref[...] = rim_x_in[...] + rim_x.reshape(8, 8, 128)


def strip_values_tile(values, step, rows):
    return jnp.concatenate([values[step, layer][rows] for layer in range(4)], axis=1)


def wide(depth):
    return jnp.concatenate([depth, jnp.zeros((depth.shape[0], 96), depth.dtype)], axis=1)


def started(copies, sems):
    copies = [pltpu.make_async_copy(*ends, sems.at[k]) for k, ends in enumerate(copies)]
    for copy in copies:
        copy.start()
    return copies


def pack_kernel(
    cells, traces, wavelet, s0, r0, sm, rm, c, depth, values,
    first_y, second_y, wavelet_ref, sm_v, rm_v, c_v, depth_v, values_v, sent_ref,
    sent_v, cells_v, traces_v, sems,
):
    copies = started(
        [
            (cells, cells_v), (traces, traces_v), (depth, depth_v), (values, values_v), (wavelet, wavelet_ref),
            (sm, sm_v), (rm, rm_v), (c, c_v),
            (s0, first_y.at[0:32]), (r0, first_y.at[32:64]), (s0, second_y.at[0:32]), (r0, second_y.at[32:64]),
        ],
        sems,
    )
    for copy in copies[:2]:
        copy.wait()
    sent_v[:, 0, :] = routed(cells_v[...], traces_v[...], jnp.int32(0))
    out = pltpu.make_async_copy(sent_v, sent_ref, sems.at[12])
    out.start()
    for copy in copies[2:8]:
        copy.wait()
    even = lax.axis_index("gy") % 2 == 0
    strips, depths = strip_values_tile(values_v, 0, slice(0, 8)), wide(depth_v[...].astype(F32))
    for ref, high in ((first_y, even), (second_y, ~even)):

        def four(rows):
            return jnp.where(high, rows[..., 4:8, :], rows[..., 0:4, :])

        ref[64:96, 0:4] = four(sm_v[...])
        ref[64:96, 4:8] = four(rm_v[...])
        ref[96:112, 0:4] = four(c_v[0:16])
        ref[96:112, 4:8] = four(c_v[16:32])
        ref[112, 0:4] = four(strips)
        ref[112, 4:8] = four(depths)
    for copy in copies[8:]:
        copy.wait()
    out.wait()


def depth_matrix():
    apart = jnp.abs(iota((TZ, TZ), 0) - iota((TZ, TZ), 1))
    weights = jnp.zeros((TZ, TZ), F32)
    for reach in range(1, 5):
        weights = jnp.where(apart == reach, COEFS[reach], weights)
    high, low = halves(weights)
    top = jnp.concatenate([high, low], axis=1)
    return jnp.concatenate([top, jnp.concatenate([high, jnp.zeros_like(low)], axis=1)], axis=0)


def depth_sums(rows, matrix):
    both = jnp.dot(jnp.concatenate(halves(rows), axis=1), matrix, preferred_element_type=F32)
    return both[:, :128] + both[:, 128:]


def curvature(ref, f, x, row, depth_sum):
    tile = ref[f, x, row : row + 8]
    total = (3.0 * COEFS[0]) * tile + depth_sum
    for reach in range(1, 5):
        pairs = ref[f, x + reach, row : row + 8] + ref[f, x - reach, row : row + 8]
        pairs = pairs + ref[f, x, row + reach : row + reach + 8]
        pairs = pairs + ref[f, x, row - reach : row - reach + 8]
        total = total + COEFS[reach] * pairs
    return tile, total


def overwritten(tile, depths, values, lane_start):
    lane = iota((8, 128), 1)
    column = jnp.full((8, 128), lane_start, I32)
    relative = lane - jnp.take_along_axis(depths, column, axis=1)
    fill = jnp.take_along_axis(values, (relative & 3) * 32 + column, axis=1)
    return jnp.where((relative >= 0) & (relative < 4), fill, tile)


def keeps(axis, size):
    at = lax.axis_index(axis)
    return jnp.where(at > 0, 1.0, 0.0), jnp.where(at < size - 1, 1.0, 0.0)


def pulse(source_cell, wavelet, step, row):
    cell = source_cell[0]
    lane, sublane = iota((8, 128), 1), iota((8, 128), 0)
    at_row = sublane + (row + lax.axis_index("gy") * TY) == (cell >> 7) & 127
    return jnp.where((lane == cell & 127) & at_row, wavelet[0:1, step : step + 1], 0.0)


def source_layer(source_cell):
    return (source_cell[0] >> 14) - lax.axis_index("gx") * TX


def advanced(i, at, x, e_ref, z_ref, m_ref, courant_ref, depth_ref, v_ref, pulses, source_x, new_ref):
    for t in range(2):
        rows = slice(8 * t, 8 * t + 8)
        courant = courant_ref[i, rows]
        now, total = curvature(e_ref, 0, at, 8 + 8 * t, z_ref[0, i, rows])
        if pulses is not None:
            total = total - jnp.where(x == source_x, pulses[t], 0.0)
        new = 2.0 * now - m_ref[0, i, rows] + courant * total
        new_ref[0, i, rows] = overwritten(new, depth_ref[rows], v_ref[rows], x)
        now, total = curvature(e_ref, 1, at, 8 + 8 * t, z_ref[1, i, rows])
        new_ref[1, i, rows] = 2.0 * now - m_ref[1, i, rows] + courant * total


def in_order(beside, first, second):
    even = lax.axis_index("gy") % 2 == 0

    @pl.when(even)
    def _():
        beside(second, first)

    @pl.when(~even)
    def _():
        beside(first, second)


def edge_kernel(
    own_y, sm, rm, c, depth, values, first, second,
    new_ref, courant_ref, depth_ref, v_ref, up_ref, down_ref,
    e_ref, m_ref, z_ref,
):
    keep_before, keep_after = keeps("gy", GY)
    spans = ((4, 0), (12, 24))
    for f in range(2):
        e_ref[f, 0:4, 8:24] = jnp.zeros((4, 16, 128), F32)
        e_ref[f, 20:24, 8:24] = jnp.zeros((4, 16, 128), F32)
        for to, start in spans:
            e_ref[f, to : to + 8, 12:20] = own_y[32 * f + start : 32 * f + start + 8]
    v_ref[4:12] = strip_values_tile(values, 0, slice(0, 8))
    depth_ref[4:12] = wide(depth[...])
    for to, start in ((0, 0), (4, 28)):
        layers = slice(to, to + 4)
        m_ref[0, layers, 4:12] = sm[start : start + 4]
        m_ref[1, layers, 4:12] = rm[start : start + 4]
        courant_ref[layers, 4:12] = c[start : start + 4]

    def beside(before, after):
        for f in range(2):
            for to, start in spans:
                layers = slice(32 * f + start, 32 * f + start + 8)
                e_ref[f, to : to + 8, 4:12] = before[layers] * keep_before
                e_ref[f, to : to + 8, 20:28] = after[layers] * keep_after
        for ref, keep, rows in ((before, keep_before, slice(0, 4)), (after, keep_after, slice(12, 16))):
            for to, start in ((0, 0), (4, 28)):
                layers, half = slice(to, to + 4), start // 16
                m_ref[0, layers, rows] = ref[64 + start : 68 + start, 0:4] * keep
                m_ref[1, layers, rows] = ref[64 + start : 68 + start, 4:8] * keep
                at = 96 + start - 16 * half
                courant_ref[layers, rows] = ref[at : at + 4, 4 * half : 4 * half + 4] * keep
            v_ref[rows] = ref[112, 0:4] * keep
            depth_ref[rows] = (ref[112, 4:8] * keep).astype(I32)

    in_order(beside, first, second)
    matrix = depth_matrix()
    for f in range(2):
        for half in range(2):
            rows = e_ref[f, 4 + 12 * half : 8 + 12 * half, 8:24].reshape(64, 128)
            z_ref[f, 4 * half : 4 * half + 4] = depth_sums(rows, matrix).reshape(4, 16, 128)
    for i in range(8):
        at, x = (i + 4, i) if i < 4 else (i + 12, i + 24)
        advanced(
            i, at, x, e_ref, z_ref, m_ref, courant_ref, depth_ref, v_ref, None, None, new_ref
        )
    for ref, to, rim, at in ((up_ref, 4, 28, 16), (down_ref, 0, 0, 4)):
        for f in range(2):
            ref[4 * f : 4 * f + 4] = new_ref[f, to : to + 4, 4:12]
            ref[12 + 4 * f : 16 + 4 * f] = own_y[32 * f + rim : 32 * f + rim + 4]
            ref[20 + 4 * f : 24 + 4 * f, 0:4] = e_ref[f, at : at + 4, 8:12]
            ref[20 + 4 * f : 24 + 4 * f, 4:8] = e_ref[f, at : at + 4, 20:24]
        ref[8:12] = c[rim : rim + 4]
        ref[28] = depth_ref[4:12].astype(F32)


def inner_kernel(
    source_cell,
    wavelet, own_y, sm, rm, c, first, second, depths, values,
    new_ref, courant_ref,
    e_ref, m_ref, z_ref,
):
    keep_before, keep_after = keeps("gy", GY)
    for f in range(2):
        e_ref[f, :, 12:20] = own_y[32 * f : 32 * f + 32]
    m_ref[0, :, 4:12] = sm[4:28]
    m_ref[1, :, 4:12] = rm[4:28]
    courant_ref[:, 4:12] = c[4:28]

    def beside(before, after):
        for f in range(2):
            e_ref[f, :, 4:12] = before[32 * f : 32 * f + 32] * keep_before
            e_ref[f, :, 20:28] = after[32 * f : 32 * f + 32] * keep_after
        for ref, keep, rows in ((before, keep_before, slice(0, 4)), (after, keep_after, slice(12, 16))):
            m_ref[0, :, rows] = ref[68:92, 0:4] * keep
            m_ref[1, :, rows] = ref[68:92, 4:8] * keep
            courant_ref[0:12, rows] = ref[100:112, 0:4] * keep
            courant_ref[12:24, rows] = ref[96:108, 4:8] * keep

    in_order(beside, first, second)
    pulses = [pulse(source_cell, wavelet, 0, 8 * t - 4) for t in range(2)]
    source_x = source_layer(source_cell)
    matrix = depth_matrix()
    for f in range(2):
        rows = e_ref[f, 4:28, 8:24].reshape(384, 128)
        z_ref[f] = depth_sums(rows, matrix).reshape(24, 16, 128)

    def layer(i, carry):
        advanced(
            i, i + 4, i + 4, e_ref, z_ref, m_ref, courant_ref, depths, values, pulses, source_x, new_ref
        )
        return carry

    lax.fori_loop(0, 24, layer, 0, unroll=8)


def unless_strip(depths, column, amount):
    relative = iota((8, 128), 1) - depths[:, column : column + 1]
    return jnp.where((relative >= 0) & (relative < 4), 0.0, amount)


def late_layer(x, at, i, o_ref, z_ref, s0, r0, c, own, depths, values, late_pulse, source_x, s_v, r_v, sub_ref, to):
    now, total = curvature(o_ref, 0, at, 8, z_ref[0, i])
    total = total - jnp.where(x == source_x, late_pulse, 0.0)
    new = 2.0 * now - s0[x] + c[x] * total
    new = overwritten(new, depths, values, x)
    s_v[i] = new
    for j in range(2):
        sub_ref[0, j, pl.ds(to, 1)] = now[4 * j : 4 * j + 1]
        sub_ref[1, j, pl.ds(to, 1)] = new[4 * j : 4 * j + 1]
    now, total = curvature(o_ref, 1, at, 8, z_ref[1, i])
    new = 2.0 * now - r0[x] + c[x] * (total + own[1, x])
    r_v[i] = new
    for j in range(2):
        sub_ref[2, j, pl.ds(to, 1)] = now[4 * j : 4 * j + 1]
        sub_ref[3, j, pl.ds(to, 1)] = new[4 * j : 4 * j + 1]


def middle_kernel(
    source_cell,
    wavelet, own_y, c, depth, values, inner, inner_courant, own, rim_y,
    r1_ref, s_v, r_v, sub_ref,
    o_ref, z_ref,
):
    o_ref[0, :, 4:20] = inner[0]
    o_ref[1, :, 8:16] = inner[1, :, 4:12] + inner_courant[:, 4:12] * own[0, 4:28]
    o_ref[1, :, 4:8] = inner[1, :, 0:4] + inner_courant[:, 0:4] * rim_y[4:28, 0:4]
    o_ref[1, :, 16:20] = inner[1, :, 12:16] + inner_courant[:, 12:16] * rim_y[4:28, 4:8]
    for half in range(2):
        r1_ref[8 * half : 8 * half + 8] = o_ref[1, 16 * half : 16 * half + 8, 4:20]
    matrix = depth_matrix()
    for f in range(2):
        rows = o_ref[f, 4:20, 8:16].reshape(128, 128)
        z_ref[f] = depth_sums(rows, matrix).reshape(16, 8, 128)
    late_values = strip_values_tile(values, 1, slice(0, 8))
    near_depth = wide(depth[...])
    late_pulse, source_x = pulse(source_cell, wavelet, 1, 0), source_layer(source_cell)

    def layer(i, carry):
        late_layer(
            i + 8, i + 4, i, o_ref, z_ref, own_y.at[0:32], own_y.at[32:64], c, own,
            near_depth, late_values, late_pulse, source_x, s_v, r_v, sub_ref, i,
        )
        return carry

    lax.fori_loop(0, 16, layer, 0, unroll=16)


def steps_kernel(
    source_cell,
    wavelet, own_y, c, depth, values, left, right, edge, edge_courant, inner, depths,
    own, rim_y, rim_x, r1, sub_mid,
    s_v, r_v, near_ref, up_ref, down_ref,
    o_ref, h_ref, z_ref, sub_ref,
):
    keep_left, keep_right = keeps("gx", GX)
    s0, r0 = own_y.at[0:32], own_y.at[32:64]
    for start, first in ((0, 0), (4, 28)):
        to, part, x = slice(first + 4, first + 8), slice(start, start + 4), slice(first, first + 4)
        o_ref[0, to, 4:20] = edge[0, part]
        o_ref[1, to, 8:16] = edge[1, part, 4:12] + edge_courant[part, 4:12] * own[0, x]
        o_ref[1, to, 4:8] = edge[1, part, 0:4] + edge_courant[part, 0:4] * rim_y[x, 0:4]
        o_ref[1, to, 16:20] = edge[1, part, 12:16] + edge_courant[part, 12:16] * rim_y[x, 4:8]
    for half in range(2):
        to = slice(8 + 16 * half, 16 + 16 * half)
        o_ref[0, to, 4:20] = inner[0, 16 * half : 16 * half + 8]
        o_ref[1, to, 4:20] = r1[8 * half : 8 * half + 8]
    source_x = source_layer(source_cell)
    pulses = [pulse(source_cell, wavelet, 0, row) for row in (-4, 4, 0)]
    for side, ref, keep in ((0, left, keep_left), (1, right, keep_right)):
        beyond_depths = (ref[28] * keep).astype(I32)
        for f in range(2):
            h_ref[f, side, :, 4:12] = ref[12 + 4 * f : 16 + 4 * f] * keep
            h_ref[f, side, :, 0:4] = ref[20 + 4 * f : 24 + 4 * f, 0:4] * keep
            h_ref[f, side, :, 12:16] = ref[20 + 4 * f : 24 + 4 * f, 4:8] * keep
        for n in range(4):
            x = 31 - n if side else n
            for f in range(2):
                for t in range(2):
                    rows = slice(8 * t, 8 * t + 8)
                    amount = None
                    for reach in range(n + 1, 5):
                        away = reach - n
                        term = COEFS[reach] * h_ref[f, side, away - 1 if side else 4 - away, rows]
                        amount = term if amount is None else amount + term
                    if f == 0:
                        amount = amount - jnp.where(x == source_x, pulses[t], 0.0)
                    amount = edge_courant[x - 24 if side else x, rows] * amount
                    if f == 0:
                        amount = unless_strip(depths[rows], x, amount)
                    at = slice(4 + 8 * t, 12 + 8 * t)
                    o_ref[f, x + 4, at] = o_ref[f, x + 4, at] + amount
            k = n if side else 3 - n
            for f, field in ((0, s0), (1, r0)):
                amount = None
                for reach in range(n + 1, 5):
                    inward = reach - n - 1
                    term = COEFS[reach] * field[31 - inward if side else inward]
                    amount = term if amount is None else amount + term
                if f == 0:
                    beyond = 32 + n if side else -1 - n
                    amount = amount - jnp.where(beyond == source_x, pulses[2], 0.0)
                else:
                    amount = amount + rim_x[4 * side + k]
                amount = ref[8 + k] * amount
                if f == 0:
                    amount = unless_strip(beyond_depths, k if side else 28 + k, amount)
                o_ref[f, 36 + n if side else 3 - n, 8:16] = (ref[4 * f + k] + amount) * keep
    matrix = depth_matrix()
    for f in range(2):
        for half in range(2):
            rows = o_ref[f, 4 + 24 * half : 12 + 24 * half, 8:16].reshape(64, 128)
            z_ref[f, 8 * half : 8 * half + 8] = depth_sums(rows, matrix).reshape(8, 8, 128)
    late_values = strip_values_tile(values, 1, slice(0, 8))
    near_depth = wide(depth[...])
    late_pulse = pulse(source_cell, wavelet, 1, 0)
    for k in range(4):
        for j in range(2):
            sub_ref[k, j, 8:24] = sub_mid[k, j]
    for i in range(16):
        x = i if i < 8 else i + 16
        late_layer(
            x, x + 4, i, o_ref, z_ref, s0, r0, c, own,
            near_depth, late_values, late_pulse, source_x, s_v, r_v, sub_ref, x,
        )
    z, to = iota((TZ, 128), 0), iota((TZ, 128), 1)
    totals = []
    for k in range(4):
        total = None
        for j in range(2):
            pick = jnp.where((z & 3 == 0) & (to == (z >> 2) + (16 + 64 * j)), 1.0, 0.0)
            part = jnp.dot(
                sub_ref[k, j], pick, precision=lax.Precision.HIGHEST, preferred_element_type=F32
            )
            total = part if total is None else total + part
        near_ref[k] = total
        totals.append(total)
    for f in range(2):
        packed = totals[2 * f] + pltpu.roll(totals[2 * f + 1], 32, 1)
        up_ref[f] = packed[16:32]
        down_ref[f] = packed[0:16]


def store_kernel(s_mid, r_mid, s_edge, r_edge, s_out, r_out, sems):
    ends = [
        pair
        for mid, edge, to in ((s_mid, s_edge, s_out), (r_mid, r_edge, r_out))
        for pair in ((mid, to.at[8:24]), (edge.at[0:8], to.at[0:8]), (edge.at[8:16], to.at[24:32]))
    ]
    for copy in started(ends, sems):
        copy.wait()


def angles_kernel(stored, near, left, right, out_ref, g_ref):
    keep_left, keep_right = keeps("gx", GX)
    lane = iota((16, 128), 1)
    held = ((lane >= 16) & (lane < 48)) | ((lane >= 80) & (lane < 112))
    for f in range(2):
        for ref, keep, rows in ((left, keep_left, slice(0, 16)), (right, keep_right, slice(48, 64))):
            packed = ref[f] * keep
            g_ref[2 * f, rows] = jnp.where(held, packed, 0.0)
            g_ref[2 * f + 1, rows] = jnp.where(held, pltpu.roll(packed, 96, 1), 0.0)
    for k in range(4):
        g_ref[k, 16:48] = near[k]
    sums = [None] * 32
    for lag in range(-16, 17):
        product = None
        for step in range(2):
            source = g_ref[step, pl.ds(16 - lag, 8, stride=4)]
            receiver = g_ref[2 + step, pl.ds(16 + lag, 8, stride=4)]
            part = source * receiver
            product = part if product is None else product + part
        shifted = {}

        def shift(amount):
            if amount not in shifted:
                shifted[amount] = product if amount == 0 else pltpu.roll(product, -amount % 128, 1)
            return shifted[amount]

        for a in range(32):
            move = np.float32(lag) * SLOPES[a] / np.float32(4.0)
            low = np.floor(move)
            frac = float(move - low)
            term = shift(int(low)) * (1.0 - frac)
            if frac != 0.0:
                term = term + shift(int(low) + 1) * frac
            sums[a] = term if sums[a] is None else sums[a] + term
    lane = iota((8, 128), 1)
    for b in range(16):
        first, second = sums[2 * b], sums[2 * b + 1]
        packed = jnp.where(lane < 32, pltpu.roll(first, 112, 1), pltpu.roll(first, 80, 1))
        other = jnp.where(lane < 96, pltpu.roll(second, 48, 1), pltpu.roll(second, 16, 1))
        out_ref[b] = jnp.where(lane < 64, packed, other)


def arrange_kernel(got, out_ref):
    lane = iota((8, 128), 1)
    for t in range(8):
        even, odd = got[2 * t], got[2 * t + 1]
        out_ref[0, :, 128 * t : 128 * t + 128] = jnp.where(lane < 64, even, pltpu.roll(odd, 64, 1))
        out_ref[1, :, 128 * t : 128 * t + 128] = jnp.where(lane < 64, pltpu.roll(even, 64, 1), odd)


def call(kernel, outs, arrays, scalars=(), hbm=(), out_scalars=0, out_hbm=(), scratch=(), weight=0):
    smem, vmem = pl.BlockSpec(memory_space=pltpu.SMEM), pl.BlockSpec(memory_space=pltpu.VMEM)
    far = pl.BlockSpec(memory_space=pltpu.HBM)
    hbm = [
        pltpu.with_memory_space_constraint(array, pltpu.HBM) for array in hbm
    ]
    return pl.pallas_call(
        kernel,
        out_shape=[jax.ShapeDtypeStruct(shape, kind) for shape, kind in outs],
        in_specs=[smem] * len(scalars) + [far] * len(hbm) + [vmem] * len(arrays),
        out_specs=[
            smem if k >= len(outs) - out_scalars else far if k in out_hbm else vmem for k in range(len(outs))
        ],
        scratch_shapes=list(scratch),
        compiler_params=pltpu.CompilerParams(vmem_limit_bytes=VMEM_LIMIT),
        cost_estimate=pl.CostEstimate(flops=0, bytes_accessed=weight, transcendentals=0) if weight else None,
    )(*scalars, *hbm, *arrays)


def both_ways(to_next, to_last, axis):
    size = lax.axis_size(axis)
    from_last = lax.ppermute(to_next, axis, [(i, (i + 1) % size) for i in range(size)])
    from_next = lax.ppermute(to_last, axis, [((i + 1) % size, i) for i in range(size)])
    return from_last, from_next


def body(
    source_now,
    source_next,
    receiver_now,
    receiver_next,
    courant,
    source_cell,
    wavelet,
    receiver_cells,
    receiver_traces,
    strip_depth,
    strip_values,
):
    cells = receiver_cells.reshape(1, RECEIVERS)
    tile, sent_shape = (TX, TY, TZ), ((DEVICES, 1, 128), F32)
    listed = [((1, RECEIVERS), I32), ((2, RECEIVERS), F32)]
    fields = (source_now, receiver_now, source_next, receiver_next, courant, strip_depth, strip_values)
    first_y, second_y, near_wavelet, near_sm, near_rm, near_c, near_depth, near_values, sent = call(
        pack_kernel,
        [((113, 8, 128), F32)] * 2
        + [((1, 2), F32), *[(tile, F32)] * 3, ((8, 32), I32), ((2, 4, 8, 32), F32), sent_shape],
        [],
        hbm=[cells, receiver_traces, wavelet.reshape(1, 2), *fields],
        out_hbm=(8,),
        scratch=[pltpu.VMEM(*shape) for shape in (sent_shape, *listed)] + [pltpu.SemaphoreType.DMA((13,))],
    )
    pairs = [(i, i ^ 1) for i in range(GY)]
    first = lax.ppermute(first_y, "gy", pairs)
    second = lax.ppermute(second_y, "gy", [(i, (i + 1 if i % 2 else i - 1) % GY) for i in range(GY)])
    got = lax.all_to_all(sent, ("gx", "gy"), 0, 0, tiled=True)
    got = jnp.maximum(got.reshape(DEVICES, 128), -jnp.finfo(F32).max)
    edge, edge_courant, depths, strips, up_x, down_x = call(
        edge_kernel,
        [((2, 8, 16, 128), F32), ((8, 16, 128), F32), ((16, 128), I32), ((16, 128), F32)]
        + [((29, 8, 128), F32)] * 2,
        [first_y, near_sm, near_rm, near_c, near_depth, near_values, first, second],
        scratch=[
            pltpu.VMEM((2, 24, 32, 128), F32),
            pltpu.VMEM((2, 8, 16, 128), F32),
            pltpu.VMEM((2, 8, 16, 128), F32),
        ],
    )
    left, right = both_ways(up_x, down_x, "gx")
    inner, inner_courant = call(
        inner_kernel,
        [((2, 24, 16, 128), F32), ((24, 16, 128), F32)],
        [near_wavelet, first_y, near_sm, near_rm, near_c, first, second, depths, strips],
        scalars=[source_cell],
        scratch=[
            pltpu.VMEM((2, 32, 32, 128), F32),
            pltpu.VMEM((2, 24, 16, 128), F32),
            pltpu.VMEM((2, 24, 16, 128), F32),
        ],
    )
    sums = [((2, *tile), F32), (tile, F32), ((8, 8, 128), F32)]
    own, rim_y, rim_x, rounds = call(collect_kernel, [*sums, ((1,), I32)], [got, inner_courant], out_scalars=1, weight=1000)

    def another(state):
        turn, *partial = state
        (more,) = call(
            route_more_kernel,
            [sent_shape],
            [],
            scalars=[(turn * SLOTS).reshape(1)],
            hbm=[cells, receiver_traces],
            scratch=[pltpu.VMEM(*shape) for shape in listed] + [pltpu.SemaphoreType.DMA((2,))],
        )
        more = lax.all_to_all(more, ("gx", "gy"), 0, 0, tiled=True)
        return (turn + 1, *call(collect_more_kernel, sums, [more, *partial]))

    _, own, rim_y, rim_x = lax.while_loop(
        lambda state: state[0] < rounds[0], another, (jnp.int32(1), own, rim_y, rim_x)
    )
    part = (16, TY, TZ)
    r1, s_mid, r_mid, sub_mid = call(
        middle_kernel,
        [((16, 16, 128), F32), (part, F32), (part, F32), ((4, 2, 16, 128), F32)],
        [near_wavelet, first_y, near_c, near_depth, near_values, inner, inner_courant, own, rim_y],
        scalars=[source_cell],
        scratch=[pltpu.VMEM((2, 24, 24, 128), F32), pltpu.VMEM((2, 16, 8, 128), F32)],
    )
    s_edge, r_edge, near, up, down = call(
        steps_kernel,
        [(part, F32), (part, F32), ((4, 32, 128), F32), ((2, 16, 128), F32), ((2, 16, 128), F32)],
        [
            near_wavelet, first_y, near_c, near_depth, near_values, left, right, edge, edge_courant,
            inner, depths, own, rim_y, rim_x, r1, sub_mid,
        ],
        scalars=[source_cell],
        scratch=[
            pltpu.VMEM((2, 40, 24, 128), F32),
            pltpu.VMEM((2, 2, 4, 16, 128), F32),
            pltpu.VMEM((2, 16, 8, 128), F32),
            pltpu.VMEM((4, 2, 32, 128), F32),
        ],
    )
    near_left, near_right = both_ways(up, down, "gx")
    source_field, receiver_field = call(
        store_kernel,
        [(tile, F32), (tile, F32)],
        [s_mid, r_mid, s_edge, r_edge],
        out_hbm=(0, 1),
        scratch=[pltpu.SemaphoreType.DMA((6,))],
        weight=1_000_000,
    )
    (angles,) = call(
        angles_kernel, [((16, 8, 128), F32)], [near, near_left, near_right], hbm=[source_field],
        scratch=[pltpu.VMEM((4, 64, 128), F32)],
    )
    angles = lax.all_to_all(angles, "gy", 0, 0, tiled=True)
    (image,) = call(arrange_kernel, [((2, 8, 1024), F32)], [angles])
    return source_field, receiver_field, image


def solution(mesh):
    return jax.shard_map(
        body,
        mesh=mesh,
        in_specs=(
            P("gx", "gy", None),
            P("gx", "gy", None),
            P("gx", "gy", None),
            P("gx", "gy", None),
            P("gx", "gy", None),
            P(),
            P(),
            P(("gx", "gy")),
            P(None, ("gx", "gy")),
            P("gy", "gx"),
            P(None, None, "gy", "gx"),
        ),
        out_specs=(P("gx", "gy", None), P("gx", "gy", None), P("gy", "gx", None)),
        check_vma=False,
    )
```

```python
import math

import jax
import jax.numpy as jnp
import numpy as np
from jax import lax
from jax.experimental import pallas as pl
from jax.experimental.pallas import tpu as pltpu
from jax.sharding import PartitionSpec as P

COEFS = (-205.0 / 72.0, 8.0 / 5.0, -1.0 / 5.0, 8.0 / 315.0, -1.0 / 560.0)
SLOPES = np.array(
    [math.tan(math.pi * (-60.0 + 120.0 * (angle + 0.5) / 32.0) / 180.0) for angle in range(32)],
    dtype=np.float32,
)
GX, GY = 8, 16
TX, TY, TZ = 32, 8, 128
DEVICES = GX * GY
RECEIVERS = 256
SLOTS = 16
F32, BF16, I32 = jnp.float32, jnp.bfloat16, jnp.int32
VMEM_LIMIT = 24 * 1024 * 1024


def iota(shape, dim):
    return lax.broadcasted_iota(I32, shape, dim)


def halves(value):
    high = value.astype(BF16)
    return high, (value - high.astype(F32)).astype(BF16)


def dot_nt(left, right):
    return lax.dot_general(left, right, (((1,), (1,)), ((), ())), preferred_element_type=F32)


def routed(cells, traces, first_slot):
    x, y, z = cells >> 14, (cells >> 7) & 127, cells & 127
    tile_x, tile_y, in_x, in_y = x >> 5, y >> 3, x & 31, y & 7
    beside_y = jnp.where(in_y < 4, tile_y - 1, tile_y + 1)
    beside_x = jnp.where(in_x < 4, tile_x - 1, jnp.where(in_x >= 28, tile_x + 1, -1))
    to_y = jnp.where((beside_y >= 0) & (beside_y < GY), tile_x * GY + beside_y, -1)
    to_x = jnp.where((beside_x >= 0) & (beside_x < GX), beside_x * GY + tile_y, -1)
    rim_x = jnp.where(in_x < 4, in_x + 4, in_x - 28)
    classes = (
        (tile_x * GY + tile_y, (in_x * 8 + in_y) * 128 + z, 2),
        (to_y, (in_x * 8 + (in_y ^ 4)) * 128 + z, 1),
        (to_x, (rim_x * 8 + in_y) * 128 + z, 1),
    )
    earlier = jnp.where(
        iota((RECEIVERS, RECEIVERS), 0) < iota((RECEIVERS, RECEIVERS), 1), 1.0, 0.0
    ).astype(BF16)
    device = iota((DEVICES, RECEIVERS), 0)
    slot = iota((SLOTS, RECEIVERS), 0).astype(F32) + first_slot.astype(F32)
    hits, kept, last_rank, row = [], [], None, 0
    for target, place, steps in classes:
        hit = jnp.where(device == target, 1.0, 0.0)
        before = jnp.dot(hit.astype(BF16), earlier, preferred_element_type=F32)
        rank = jnp.sum(hit * before, axis=0, keepdims=True)
        last_rank = rank if last_rank is None else jnp.maximum(last_rank, rank)
        mine = slot == rank
        rows = [jnp.where(mine, place.astype(F32), 0.0)]
        rows += [jnp.where(mine, traces[s : s + 1], 0.0) for s in range(steps)]
        size = SLOTS * len(rows)
        above = [jnp.zeros((row, RECEIVERS), F32)] if row else []
        below = [jnp.zeros((128 - row - size, RECEIVERS), F32)]
        kept.append(jnp.concatenate(above + rows + below, axis=0))
        hits.append(hit.astype(BF16))
        row += size
    hits = jnp.concatenate(hits, axis=1)
    high, low = halves(jnp.concatenate(kept, axis=1))
    sent = dot_nt(hits, high) + dot_nt(hits, low)
    rounds = (jnp.max(last_rank, axis=1, keepdims=True).astype(I32) // SLOTS + 1).astype(F32)
    return jnp.where(iota((DEVICES, 128), 1) >= row, rounds, sent)


def route_more_kernel(first_ref, cells, traces, sent_ref, cells_v, traces_v, sems):
    for copy in started([(cells, cells_v), (traces, traces_v)], sems):
        copy.wait()
    sent_ref[:, 0, :] = routed(cells_v[...], traces_v[...], first_ref[0])


def collected(got):
    rows = got.T
    sums, row = [], 0
    down = iota((TZ, DEVICES), 0).astype(F32).astype(BF16)
    unit, zero = jnp.ones((), BF16), jnp.zeros((), BF16)
    for columns, steps in ((TX * 8, 2), (TX * 8, 1), (64, 1)):
        cell = rows[row : row + SLOTS].astype(I32)
        column, depth = (cell >> 7).astype(F32), (cell & 127).astype(F32)
        at = iota((columns, DEVICES), 0).astype(F32).astype(BF16)
        one, parts = [], [[] for _ in range(2 * steps)]
        for k in range(SLOTS):
            one.append(jnp.where(at == column[k : k + 1].astype(BF16), unit, zero))
            same = down == depth[k : k + 1].astype(BF16)
            for s in range(steps):
                value = rows[row + (s + 1) * SLOTS + k : row + (s + 1) * SLOTS + k + 1]
                high, low = halves(value)
                parts[2 * s].append(jnp.where(same, high, zero))
                parts[2 * s + 1].append(jnp.where(same, low, zero))
        one = jnp.concatenate(one, axis=1)
        both = dot_nt(one, jnp.concatenate([jnp.concatenate(part, axis=1) for part in parts], axis=0))
        for s in range(steps):
            sums.append(both[:, 256 * s : 256 * s + 128] + both[:, 256 * s + 128 : 256 * s + 256])
        row += SLOTS * (steps + 1)
    return sums


def collect_kernel(got_ref, inner_courant, own_ref, rim_y_ref, rim_x_ref, rounds_ref):
    got = got_ref[...]
    own_0, own_1, rim_y, rim_x = collected(got)
    own_ref[0] = own_0.reshape(TX, 8, 128)
    own_ref[1] = own_1.reshape(TX, 8, 128)
    rim_y_ref[...] = rim_y.reshape(TX, 8, 128)
    rim_x_ref[...] = rim_x.reshape(8, 8, 128)
    rounds_ref[0] = jnp.max(got[:, 112:128]).astype(I32)


def collect_more_kernel(got_ref, own_in, rim_y_in, rim_x_in, own_ref, rim_y_ref, rim_x_ref):
    own_0, own_1, rim_y, rim_x = collected(got_ref[:, 0, :])
    own_ref[0] = own_in[0] + own_0.reshape(TX, 8, 128)
    own_ref[1] = own_in[1] + own_1.reshape(TX, 8, 128)
    rim_y_ref[...] = rim_y_in[...] + rim_y.reshape(TX, 8, 128)
    rim_x_ref[...] = rim_x_in[...] + rim_x.reshape(8, 8, 128)


def strip_values_tile(values, step, rows):
    return jnp.concatenate([values[step, layer][rows] for layer in range(4)], axis=1)


def wide(depth):
    return jnp.concatenate([depth, jnp.zeros((depth.shape[0], 96), depth.dtype)], axis=1)


def started(copies, sems):
    copies = [pltpu.make_async_copy(*ends, sems.at[k]) for k, ends in enumerate(copies)]
    for copy in copies:
        copy.start()
    return copies


def pack_kernel(
    cells, traces, wavelet, s0, r0, sm, rm, c, depth, values,
    first_y, second_y, wavelet_ref, sm_v, rm_v, c_v, depth_v, values_v, sent_ref,
    sent_v, cells_v, traces_v, sems,
):
    copies = started(
        [
            (cells, cells_v), (traces, traces_v), (depth, depth_v), (values, values_v), (wavelet, wavelet_ref),
            (sm, sm_v), (rm, rm_v), (c, c_v),
            (s0, first_y.at[0:32]), (r0, first_y.at[32:64]), (s0, second_y.at[0:32]), (r0, second_y.at[32:64]),
        ],
        sems,
    )
    for copy in copies[:2]:
        copy.wait()
    sent_v[:, 0, :] = routed(cells_v[...], traces_v[...], jnp.int32(0))
    out = pltpu.make_async_copy(sent_v, sent_ref, sems.at[12])
    out.start()
    for copy in copies[2:8]:
        copy.wait()
    even = lax.axis_index("gy") % 2 == 0
    strips, depths = strip_values_tile(values_v, 0, slice(0, 8)), wide(depth_v[...].astype(F32))
    for ref, high in ((first_y, even), (second_y, ~even)):

        def four(rows):
            return jnp.where(high, rows[..., 4:8, :], rows[..., 0:4, :])

        ref[64:96, 0:4] = four(sm_v[...])
        ref[64:96, 4:8] = four(rm_v[...])
        ref[96:112, 0:4] = four(c_v[0:16])
        ref[96:112, 4:8] = four(c_v[16:32])
        ref[112, 0:4] = four(strips)
        ref[112, 4:8] = four(depths)
    for copy in copies[8:]:
        copy.wait()
    out.wait()


def depth_matrix():
    apart = jnp.abs(iota((TZ, TZ), 0) - iota((TZ, TZ), 1))
    weights = jnp.zeros((TZ, TZ), F32)
    for reach in range(1, 5):
        weights = jnp.where(apart == reach, COEFS[reach], weights)
    high, low = halves(weights)
    top = jnp.concatenate([high, low], axis=1)
    return jnp.concatenate([top, jnp.concatenate([high, jnp.zeros_like(low)], axis=1)], axis=0)


def depth_sums(rows, matrix):
    both = jnp.dot(jnp.concatenate(halves(rows), axis=1), matrix, preferred_element_type=F32)
    return both[:, :128] + both[:, 128:]


def curvature(ref, f, x, row, depth_sum):
    tile = ref[f, x, row : row + 8]
    total = (3.0 * COEFS[0]) * tile + depth_sum
    for reach in range(1, 5):
        pairs = ref[f, x + reach, row : row + 8] + ref[f, x - reach, row : row + 8]
        pairs = pairs + ref[f, x, row + reach : row + reach + 8]
        pairs = pairs + ref[f, x, row - reach : row - reach + 8]
        total = total + COEFS[reach] * pairs
    return tile, total


def overwritten(tile, depths, values, lane_start):
    lane = iota((8, 128), 1)
    column = jnp.full((8, 128), lane_start, I32)
    relative = lane - jnp.take_along_axis(depths, column, axis=1)
    fill = jnp.take_along_axis(values, (relative & 3) * 32 + column, axis=1)
    return jnp.where((relative >= 0) & (relative < 4), fill, tile)


def keeps(axis, size):
    at = lax.axis_index(axis)
    return jnp.where(at > 0, 1.0, 0.0), jnp.where(at < size - 1, 1.0, 0.0)


def pulse(source_cell, wavelet, step, row):
    cell = source_cell[0, 0]
    lane, sublane = iota((8, 128), 1), iota((8, 128), 0)
    at_row = sublane + (row + lax.axis_index("gy") * TY) == (cell >> 7) & 127
    return jnp.where((lane == cell & 127) & at_row, wavelet[0:1, step : step + 1], 0.0)


def source_layer(source_cell):
    return (source_cell[0, 0] >> 14) - lax.axis_index("gx") * TX


def advanced(i, at, x, e_ref, z_ref, m_ref, courant_ref, depth_ref, v_ref, new_ref):
    for t in range(2):
        rows = slice(8 * t, 8 * t + 8)
        courant = courant_ref[i, rows]
        now, total = curvature(e_ref, 0, at, 8 + 8 * t, z_ref[0, i, rows])
        new = 2.0 * now - m_ref[0, i, rows] + courant * total
        new_ref[0, i, rows] = overwritten(new, depth_ref[rows], v_ref[rows], x)
        now, total = curvature(e_ref, 1, at, 8 + 8 * t, z_ref[1, i, rows])
        new_ref[1, i, rows] = 2.0 * now - m_ref[1, i, rows] + courant * total


def in_order(beside, first, second):
    even = lax.axis_index("gy") % 2 == 0

    @pl.when(even)
    def _():
        beside(second, first)

    @pl.when(~even)
    def _():
        beside(first, second)


def edge_kernel(
    own_y, sm, rm, c, depth, values, first, second,
    new_ref, courant_ref, depth_ref, v_ref, up_ref, down_ref,
    e_ref, m_ref, z_ref,
):
    keep_before, keep_after = keeps("gy", GY)
    spans = ((4, 0), (12, 24))
    for f in range(2):
        e_ref[f, 0:4, 8:24] = jnp.zeros((4, 16, 128), F32)
        e_ref[f, 20:24, 8:24] = jnp.zeros((4, 16, 128), F32)
        for to, start in spans:
            e_ref[f, to : to + 8, 12:20] = own_y[32 * f + start : 32 * f + start + 8]
    v_ref[4:12] = strip_values_tile(values, 0, slice(0, 8))
    depth_ref[4:12] = wide(depth[...])
    for to, start in ((0, 0), (4, 28)):
        layers = slice(to, to + 4)
        m_ref[0, layers, 4:12] = sm[start : start + 4]
        m_ref[1, layers, 4:12] = rm[start : start + 4]
        courant_ref[layers, 4:12] = c[start : start + 4]

    def beside(before, after):
        for f in range(2):
            for to, start in spans:
                layers = slice(32 * f + start, 32 * f + start + 8)
                e_ref[f, to : to + 8, 4:12] = before[layers] * keep_before
                e_ref[f, to : to + 8, 20:28] = after[layers] * keep_after
        for ref, keep, rows in ((before, keep_before, slice(0, 4)), (after, keep_after, slice(12, 16))):
            for to, start in ((0, 0), (4, 28)):
                layers, half = slice(to, to + 4), start // 16
                m_ref[0, layers, rows] = ref[64 + start : 68 + start, 0:4] * keep
                m_ref[1, layers, rows] = ref[64 + start : 68 + start, 4:8] * keep
                at = 96 + start - 16 * half
                courant_ref[layers, rows] = ref[at : at + 4, 4 * half : 4 * half + 4] * keep
            v_ref[rows] = ref[112, 0:4] * keep
            depth_ref[rows] = (ref[112, 4:8] * keep).astype(I32)

    in_order(beside, first, second)
    matrix = depth_matrix()
    for f in range(2):
        for half in range(2):
            rows = e_ref[f, 4 + 12 * half : 8 + 12 * half, 8:24].reshape(64, 128)
            z_ref[f, 4 * half : 4 * half + 4] = depth_sums(rows, matrix).reshape(4, 16, 128)
    for i in range(8):
        at, x = (i + 4, i) if i < 4 else (i + 12, i + 24)
        advanced(
            i, at, x, e_ref, z_ref, m_ref, courant_ref, depth_ref, v_ref, new_ref
        )
    for ref, to, rim, at in ((up_ref, 4, 28, 16), (down_ref, 0, 0, 4)):
        for f in range(2):
            ref[4 * f : 4 * f + 4] = new_ref[f, to : to + 4, 4:12]
            ref[12 + 4 * f : 16 + 4 * f] = own_y[32 * f + rim : 32 * f + rim + 4]
            ref[20 + 4 * f : 24 + 4 * f, 0:4] = e_ref[f, at : at + 4, 8:12]
            ref[20 + 4 * f : 24 + 4 * f, 4:8] = e_ref[f, at : at + 4, 20:24]
        ref[8:12] = c[rim : rim + 4]
        ref[28] = depth_ref[4:12].astype(F32)


def inner_kernel(
    own_y, sm, rm, c, first, second, depths, values,
    new_ref, courant_ref,
    e_ref, m_ref, z_ref,
):
    keep_before, keep_after = keeps("gy", GY)
    for f in range(2):
        e_ref[f, :, 12:20] = own_y[32 * f : 32 * f + 32]
    m_ref[0, :, 4:12] = sm[4:28]
    m_ref[1, :, 4:12] = rm[4:28]
    courant_ref[:, 4:12] = c[4:28]

    def beside(before, after):
        for f in range(2):
            e_ref[f, :, 4:12] = before[32 * f : 32 * f + 32] * keep_before
            e_ref[f, :, 20:28] = after[32 * f : 32 * f + 32] * keep_after
        for ref, keep, rows in ((before, keep_before, slice(0, 4)), (after, keep_after, slice(12, 16))):
            m_ref[0, :, rows] = ref[68:92, 0:4] * keep
            m_ref[1, :, rows] = ref[68:92, 4:8] * keep
            courant_ref[0:12, rows] = ref[100:112, 0:4] * keep
            courant_ref[12:24, rows] = ref[96:108, 4:8] * keep

    in_order(beside, first, second)
    matrix = depth_matrix()
    for f in range(2):
        rows = e_ref[f, 4:28, 8:24].reshape(384, 128)
        z_ref[f] = depth_sums(rows, matrix).reshape(24, 16, 128)

    def layer(i, carry):
        advanced(
            i, i + 4, i + 4, e_ref, z_ref, m_ref, courant_ref, depths, values, new_ref
        )
        return carry

    lax.fori_loop(0, 24, layer, 0, unroll=8)


def unless_strip(depths, column, amount):
    relative = iota((8, 128), 1) - depths[:, column : column + 1]
    return jnp.where((relative >= 0) & (relative < 4), 0.0, amount)


def late_layer(x, at, i, o_ref, z_ref, s0, r0, c, own, depths, values, late_pulse, source_x, s_v, r_v, sub_ref, to):
    now, total = curvature(o_ref, 0, at, 8, z_ref[0, i])
    total = total - jnp.where(x == source_x, late_pulse, 0.0)
    new = 2.0 * now - s0[x] + c[x] * total
    new = overwritten(new, depths, values, x)
    s_v[i] = new
    for j in range(2):
        sub_ref[0, j, pl.ds(to, 1)] = now[4 * j : 4 * j + 1]
        sub_ref[1, j, pl.ds(to, 1)] = new[4 * j : 4 * j + 1]
    now, total = curvature(o_ref, 1, at, 8, z_ref[1, i])
    new = 2.0 * now - r0[x] + c[x] * (total + own[1, x])
    r_v[i] = new
    for j in range(2):
        sub_ref[2, j, pl.ds(to, 1)] = now[4 * j : 4 * j + 1]
        sub_ref[3, j, pl.ds(to, 1)] = new[4 * j : 4 * j + 1]


def middle_kernel(
    source_cell,
    wavelet, own_y, c, depth, values, inner, inner_courant, depths, own, rim_y,
    new_ref, s_v, r_v, sub_ref,
    o_ref, z_ref,
):
    o_ref[0, :, 4:20] = inner[0]
    o_ref[1, :, 8:16] = inner[1, :, 4:12] + inner_courant[:, 4:12] * own[0, 4:28]
    o_ref[1, :, 4:8] = inner[1, :, 0:4] + inner_courant[:, 0:4] * rim_y[4:28, 0:4]
    o_ref[1, :, 16:20] = inner[1, :, 12:16] + inner_courant[:, 12:16] * rim_y[4:28, 4:8]
    k = (source_cell[0, 0] >> 14) - lax.axis_index("gx") * TX - 4

    @pl.when((k >= 0) & (k < 24))
    def _():
        for t in range(2):
            rows, at = slice(8 * t, 8 * t + 8), slice(4 + 8 * t, 12 + 8 * t)
            column = jnp.full((8, 128), k + 4, I32)
            relative = iota((8, 128), 1) - jnp.take_along_axis(depths[rows], column, axis=1)
            amount = inner_courant[k, rows] * pulse(source_cell, wavelet, 0, 8 * t - 4)
            free = (relative < 0) | (relative >= 4)
            o_ref[0, k, at] = o_ref[0, k, at] - jnp.where(free, amount, 0.0)

    for f in range(2):
        for half in range(2):
            new_ref[f, 8 * half : 8 * half + 8] = o_ref[f, 16 * half : 16 * half + 8, 4:20]
    matrix = depth_matrix()
    for f in range(2):
        rows = o_ref[f, 4:20, 8:16].reshape(128, 128)
        z_ref[f] = depth_sums(rows, matrix).reshape(16, 8, 128)
    late_values = strip_values_tile(values, 1, slice(0, 8))
    near_depth = wide(depth[...])
    late_pulse, source_x = pulse(source_cell, wavelet, 1, 0), source_layer(source_cell)

    def layer(i, carry):
        late_layer(
            i + 8, i + 4, i, o_ref, z_ref, own_y.at[0:32], own_y.at[32:64], c, own,
            near_depth, late_values, late_pulse, source_x, s_v, r_v, sub_ref, i,
        )
        return carry

    lax.fori_loop(0, 16, layer, 0, unroll=16)


def steps_kernel(
    source_cell,
    wavelet, own_y, c, depth, values, left, right, edge, edge_courant, depths,
    own, rim_y, rim_x, inner, sub_mid,
    s_v, r_v, near_ref, up_ref, down_ref,
    o_ref, h_ref, z_ref, sub_ref,
):
    keep_left, keep_right = keeps("gx", GX)
    s0, r0 = own_y.at[0:32], own_y.at[32:64]
    for start, first in ((0, 0), (4, 28)):
        to, part, x = slice(first + 4, first + 8), slice(start, start + 4), slice(first, first + 4)
        o_ref[0, to, 4:20] = edge[0, part]
        o_ref[1, to, 8:16] = edge[1, part, 4:12] + edge_courant[part, 4:12] * own[0, x]
        o_ref[1, to, 4:8] = edge[1, part, 0:4] + edge_courant[part, 0:4] * rim_y[x, 0:4]
        o_ref[1, to, 16:20] = edge[1, part, 12:16] + edge_courant[part, 12:16] * rim_y[x, 4:8]
    for half in range(2):
        to = slice(8 + 16 * half, 16 + 16 * half)
        for f in range(2):
            o_ref[f, to, 4:20] = inner[f, 8 * half : 8 * half + 8]
    source_x = source_layer(source_cell)
    pulses = [pulse(source_cell, wavelet, 0, row) for row in (-4, 4, 0)]
    for side, ref, keep in ((0, left, keep_left), (1, right, keep_right)):
        beyond_depths = (ref[28] * keep).astype(I32)
        for f in range(2):
            h_ref[f, side, :, 4:12] = ref[12 + 4 * f : 16 + 4 * f] * keep
            h_ref[f, side, :, 0:4] = ref[20 + 4 * f : 24 + 4 * f, 0:4] * keep
            h_ref[f, side, :, 12:16] = ref[20 + 4 * f : 24 + 4 * f, 4:8] * keep
        for n in range(4):
            x = 31 - n if side else n
            for f in range(2):
                for t in range(2):
                    rows = slice(8 * t, 8 * t + 8)
                    amount = None
                    for reach in range(n + 1, 5):
                        away = reach - n
                        term = COEFS[reach] * h_ref[f, side, away - 1 if side else 4 - away, rows]
                        amount = term if amount is None else amount + term
                    if f == 0:
                        amount = amount - jnp.where(x == source_x, pulses[t], 0.0)
                    amount = edge_courant[x - 24 if side else x, rows] * amount
                    if f == 0:
                        amount = unless_strip(depths[rows], x, amount)
                    at = slice(4 + 8 * t, 12 + 8 * t)
                    o_ref[f, x + 4, at] = o_ref[f, x + 4, at] + amount
            k = n if side else 3 - n
            for f, field in ((0, s0), (1, r0)):
                amount = None
                for reach in range(n + 1, 5):
                    inward = reach - n - 1
                    term = COEFS[reach] * field[31 - inward if side else inward]
                    amount = term if amount is None else amount + term
                if f == 0:
                    beyond = 32 + n if side else -1 - n
                    amount = amount - jnp.where(beyond == source_x, pulses[2], 0.0)
                else:
                    amount = amount + rim_x[4 * side + k]
                amount = ref[8 + k] * amount
                if f == 0:
                    amount = unless_strip(beyond_depths, k if side else 28 + k, amount)
                o_ref[f, 36 + n if side else 3 - n, 8:16] = (ref[4 * f + k] + amount) * keep
    matrix = depth_matrix()
    for f in range(2):
        for half in range(2):
            rows = o_ref[f, 4 + 24 * half : 12 + 24 * half, 8:16].reshape(64, 128)
            z_ref[f, 8 * half : 8 * half + 8] = depth_sums(rows, matrix).reshape(8, 8, 128)
    late_values = strip_values_tile(values, 1, slice(0, 8))
    near_depth = wide(depth[...])
    late_pulse = pulse(source_cell, wavelet, 1, 0)
    for k in range(4):
        for j in range(2):
            sub_ref[k, j, 8:24] = sub_mid[k, j]
    for i in range(16):
        x = i if i < 8 else i + 16
        late_layer(
            x, x + 4, i, o_ref, z_ref, s0, r0, c, own,
            near_depth, late_values, late_pulse, source_x, s_v, r_v, sub_ref, x,
        )
    z, to = iota((TZ, 128), 0), iota((TZ, 128), 1)
    totals = []
    for k in range(4):
        total = None
        for j in range(2):
            pick = jnp.where((z & 3 == 0) & (to == (z >> 2) + (16 + 64 * j)), 1.0, 0.0)
            part = jnp.dot(
                sub_ref[k, j], pick, precision=lax.Precision.HIGHEST, preferred_element_type=F32
            )
            total = part if total is None else total + part
        near_ref[k] = total
        totals.append(total)
    for f in range(2):
        packed = totals[2 * f] + pltpu.roll(totals[2 * f + 1], 32, 1)
        up_ref[f] = packed[16:32]
        down_ref[f] = packed[0:16]


def store_kernel(s_mid, r_mid, s_edge, r_edge, s_out, r_out, sems):
    ends = [
        pair
        for mid, edge, to in ((s_mid, s_edge, s_out), (r_mid, r_edge, r_out))
        for pair in ((mid, to.at[8:24]), (edge.at[0:8], to.at[0:8]), (edge.at[8:16], to.at[24:32]))
    ]
    for copy in started(ends, sems):
        copy.wait()


def angles_kernel(stored, near, left, right, out_ref, g_ref):
    keep_left, keep_right = keeps("gx", GX)
    lane = iota((16, 128), 1)
    held = ((lane >= 16) & (lane < 48)) | ((lane >= 80) & (lane < 112))
    for f in range(2):
        for ref, keep, rows in ((left, keep_left, slice(0, 16)), (right, keep_right, slice(48, 64))):
            packed = ref[f] * keep
            g_ref[2 * f, rows] = jnp.where(held, packed, 0.0)
            g_ref[2 * f + 1, rows] = jnp.where(held, pltpu.roll(packed, 96, 1), 0.0)
    for k in range(4):
        g_ref[k, 16:48] = near[k]
    sums = [None] * 32
    for lag in range(-16, 17):
        product = None
        for step in range(2):
            source = g_ref[step, pl.ds(16 - lag, 8, stride=4)]
            receiver = g_ref[2 + step, pl.ds(16 + lag, 8, stride=4)]
            part = source * receiver
            product = part if product is None else product + part
        shifted = {}

        def shift(amount):
            if amount not in shifted:
                shifted[amount] = product if amount == 0 else pltpu.roll(product, -amount % 128, 1)
            return shifted[amount]

        for a in range(32):
            move = np.float32(lag) * SLOPES[a] / np.float32(4.0)
            low = np.floor(move)
            frac = float(move - low)
            term = shift(int(low)) * (1.0 - frac)
            if frac != 0.0:
                term = term + shift(int(low) + 1) * frac
            sums[a] = term if sums[a] is None else sums[a] + term
    lane = iota((8, 128), 1)
    for b in range(16):
        first, second = sums[2 * b], sums[2 * b + 1]
        packed = jnp.where(lane < 32, pltpu.roll(first, 112, 1), pltpu.roll(first, 80, 1))
        other = jnp.where(lane < 96, pltpu.roll(second, 48, 1), pltpu.roll(second, 16, 1))
        out_ref[b] = jnp.where(lane < 64, packed, other)


def arrange_kernel(got, out_ref):
    lane = iota((8, 128), 1)
    for t in range(8):
        even, odd = got[2 * t], got[2 * t + 1]
        out_ref[0, :, 128 * t : 128 * t + 128] = jnp.where(lane < 64, even, pltpu.roll(odd, 64, 1))
        out_ref[1, :, 128 * t : 128 * t + 128] = jnp.where(lane < 64, pltpu.roll(even, 64, 1), odd)


def call(kernel, outs, arrays, scalars=(), hbm=(), out_scalars=0, out_hbm=(), scratch=(), weight=0):
    smem, vmem = pl.BlockSpec(memory_space=pltpu.SMEM), pl.BlockSpec(memory_space=pltpu.VMEM)
    far = pl.BlockSpec(memory_space=pltpu.HBM)
    hbm = [
        pltpu.with_memory_space_constraint(array, pltpu.HBM) for array in hbm
    ]
    return pl.pallas_call(
        kernel,
        out_shape=[jax.ShapeDtypeStruct(shape, kind) for shape, kind in outs],
        in_specs=[smem] * len(scalars) + [far] * len(hbm) + [vmem] * len(arrays),
        out_specs=[
            smem if k >= len(outs) - out_scalars else far if k in out_hbm else vmem for k in range(len(outs))
        ],
        scratch_shapes=list(scratch),
        compiler_params=pltpu.CompilerParams(vmem_limit_bytes=VMEM_LIMIT),
        cost_estimate=pl.CostEstimate(flops=0, bytes_accessed=weight, transcendentals=0) if weight else None,
    )(*scalars, *hbm, *arrays)


def both_ways(to_next, to_last, axis):
    size = lax.axis_size(axis)
    from_last = lax.ppermute(to_next, axis, [(i, (i + 1) % size) for i in range(size)])
    from_next = lax.ppermute(to_last, axis, [((i + 1) % size, i) for i in range(size)])
    return from_last, from_next


def body(
    source_now,
    source_next,
    receiver_now,
    receiver_next,
    courant,
    source_cell,
    wavelet,
    receiver_cells,
    receiver_traces,
    strip_depth,
    strip_values,
):
    cells = receiver_cells.reshape(1, RECEIVERS)
    near_cell = source_cell.reshape(1, 1)
    tile, sent_shape = (TX, TY, TZ), ((DEVICES, 1, 128), F32)
    listed = [((1, RECEIVERS), I32), ((2, RECEIVERS), F32)]
    fields = (source_now, receiver_now, source_next, receiver_next, courant, strip_depth, strip_values)
    first_y, second_y, near_wavelet, near_sm, near_rm, near_c, near_depth, near_values, sent = call(
        pack_kernel,
        [((113, 8, 128), F32)] * 2
        + [((1, 2), F32), *[(tile, F32)] * 3, ((8, 32), I32), ((2, 4, 8, 32), F32), sent_shape],
        [],
        hbm=[cells, receiver_traces, wavelet.reshape(1, 2), *fields],
        out_hbm=(8,),
        scratch=[pltpu.VMEM(*shape) for shape in (sent_shape, *listed)] + [pltpu.SemaphoreType.DMA((13,))],
    )
    pairs = [(i, i ^ 1) for i in range(GY)]
    first = lax.ppermute(first_y, "gy", pairs)
    second = lax.ppermute(second_y, "gy", [(i, (i + 1 if i % 2 else i - 1) % GY) for i in range(GY)])
    got = lax.all_to_all(sent, ("gx", "gy"), 0, 0, tiled=True)
    got = jnp.maximum(got.reshape(DEVICES, 128), -jnp.finfo(F32).max)
    edge, edge_courant, depths, strips, up_x, down_x = call(
        edge_kernel,
        [((2, 8, 16, 128), F32), ((8, 16, 128), F32), ((16, 128), I32), ((16, 128), F32)]
        + [((29, 8, 128), F32)] * 2,
        [first_y, near_sm, near_rm, near_c, near_depth, near_values, first, second],
        scratch=[
            pltpu.VMEM((2, 24, 32, 128), F32),
            pltpu.VMEM((2, 8, 16, 128), F32),
            pltpu.VMEM((2, 8, 16, 128), F32),
        ],
    )
    left, right = both_ways(up_x, down_x, "gx")
    inner, inner_courant = call(
        inner_kernel,
        [((2, 24, 16, 128), F32), ((24, 16, 128), F32)],
        [first_y, near_sm, near_rm, near_c, first, second, depths, strips],
        scratch=[
            pltpu.VMEM((2, 32, 32, 128), F32),
            pltpu.VMEM((2, 24, 16, 128), F32),
            pltpu.VMEM((2, 24, 16, 128), F32),
        ],
    )
    sums = [((2, *tile), F32), (tile, F32), ((8, 8, 128), F32)]
    own, rim_y, rim_x, rounds = call(collect_kernel, [*sums, ((1,), I32)], [got, inner_courant], out_scalars=1, weight=1000)

    def another(state):
        left_over, *partial = state
        (more,) = call(
            route_more_kernel,
            [sent_shape],
            [],
            scalars=[(left_over - 1) * SLOTS],
            hbm=[cells, receiver_traces],
            scratch=[pltpu.VMEM(*shape) for shape in listed] + [pltpu.SemaphoreType.DMA((2,))],
        )
        more = lax.all_to_all(more, ("gx", "gy"), 0, 0, tiled=True)
        return (left_over - 1, *call(collect_more_kernel, sums, [more, *partial]))

    _, own, rim_y, rim_x = lax.while_loop(
        lambda state: state[0][0] > 1, another, (rounds, own, rim_y, rim_x)
    )
    part = (16, TY, TZ)
    new1, s_mid, r_mid, sub_mid = call(
        middle_kernel,
        [((2, 16, 16, 128), F32), (part, F32), (part, F32), ((4, 2, 16, 128), F32)],
        [
            near_cell, near_wavelet, first_y, near_c, near_depth, near_values, inner, inner_courant, depths, own, rim_y,
        ],
        scratch=[pltpu.VMEM((2, 24, 24, 128), F32), pltpu.VMEM((2, 16, 8, 128), F32)],
    )
    s_edge, r_edge, near, up, down = call(
        steps_kernel,
        [(part, F32), (part, F32), ((4, 32, 128), F32), ((2, 16, 128), F32), ((2, 16, 128), F32)],
        [
            near_cell, near_wavelet, first_y, near_c, near_depth, near_values, left, right, edge, edge_courant,
            depths, own, rim_y, rim_x, new1, sub_mid,
        ],
        scratch=[
            pltpu.VMEM((2, 40, 24, 128), F32),
            pltpu.VMEM((2, 2, 4, 16, 128), F32),
            pltpu.VMEM((2, 16, 8, 128), F32),
            pltpu.VMEM((4, 2, 32, 128), F32),
        ],
    )
    near_left, near_right = both_ways(up, down, "gx")
    source_field, receiver_field = call(
        store_kernel,
        [(tile, F32), (tile, F32)],
        [s_mid, r_mid, s_edge, r_edge],
        out_hbm=(0, 1),
        scratch=[pltpu.SemaphoreType.DMA((6,))],
        weight=1_000_000,
    )
    (angles,) = call(
        angles_kernel, [((16, 8, 128), F32)], [near, near_left, near_right], hbm=[source_field],
        scratch=[pltpu.VMEM((4, 64, 128), F32)],
    )
    angles = lax.all_to_all(angles, "gy", 0, 0, tiled=True)
    (image,) = call(arrange_kernel, [((2, 8, 1024), F32)], [angles])
    return source_field, receiver_field, image


def solution(mesh):
    return jax.shard_map(
        body,
        mesh=mesh,
        in_specs=(
            P("gx", "gy", None),
            P("gx", "gy", None),
            P("gx", "gy", None),
            P("gx", "gy", None),
            P("gx", "gy", None),
            P(),
            P(),
            P(("gx", "gy")),
            P(None, ("gx", "gy")),
            P("gy", "gx"),
            P(None, None, "gy", "gx"),
        ),
        out_specs=(P("gx", "gy", None), P("gx", "gy", None), P("gy", "gx", None)),
        check_vma=False,
    )
```

```python
import math

import jax
import jax.numpy as jnp
import numpy as np
from jax import lax
from jax.experimental import pallas as pl
from jax.experimental.pallas import tpu as pltpu
from jax.sharding import PartitionSpec as P

COEFS = (-205.0 / 72.0, 8.0 / 5.0, -1.0 / 5.0, 8.0 / 315.0, -1.0 / 560.0)
SLOPES = np.array(
    [math.tan(math.pi * (-60.0 + 120.0 * (angle + 0.5) / 32.0) / 180.0) for angle in range(32)],
    dtype=np.float32,
)
GX, GY = 8, 16
TX, TY, TZ = 32, 8, 128
DEVICES = GX * GY
RECEIVERS = 256
SLOTS = 16
F32, BF16, I32 = jnp.float32, jnp.bfloat16, jnp.int32
VMEM_LIMIT = 24 * 1024 * 1024


def iota(shape, dim):
    return lax.broadcasted_iota(I32, shape, dim)


def halves(value):
    high = value.astype(BF16)
    return high, (value - high.astype(F32)).astype(BF16)


def dot_nt(left, right):
    return lax.dot_general(left, right, (((1,), (1,)), ((), ())), preferred_element_type=F32)


def routed(cells, traces, first_slot):
    x, y, z = cells >> 14, (cells >> 7) & 127, cells & 127
    tile_x, tile_y, in_x, in_y = x >> 5, y >> 3, x & 31, y & 7
    beside_y = jnp.where(in_y < 4, tile_y - 1, tile_y + 1)
    beside_x = jnp.where(in_x < 4, tile_x - 1, jnp.where(in_x >= 28, tile_x + 1, -1))
    to_y = jnp.where((beside_y >= 0) & (beside_y < GY), tile_x * GY + beside_y, -1)
    to_x = jnp.where((beside_x >= 0) & (beside_x < GX), beside_x * GY + tile_y, -1)
    rim_x = jnp.where(in_x < 4, in_x + 4, in_x - 28)
    classes = (
        (tile_x * GY + tile_y, (in_x * 8 + in_y) * 128 + z, 2),
        (to_y, (in_x * 8 + (in_y ^ 4)) * 128 + z, 1),
        (to_x, (rim_x * 8 + in_y) * 128 + z, 1),
    )
    earlier = jnp.where(
        iota((RECEIVERS, RECEIVERS), 0) < iota((RECEIVERS, RECEIVERS), 1), 1.0, 0.0
    ).astype(BF16)
    device = iota((DEVICES, RECEIVERS), 0)
    slot = iota((SLOTS, RECEIVERS), 0).astype(F32) + first_slot.astype(F32)
    hits, kept, last_rank, row = [], [], None, 0
    for target, place, steps in classes:
        hit = jnp.where(device == target, 1.0, 0.0)
        before = jnp.dot(hit.astype(BF16), earlier, preferred_element_type=F32)
        rank = jnp.sum(hit * before, axis=0, keepdims=True)
        last_rank = rank if last_rank is None else jnp.maximum(last_rank, rank)
        mine = slot == rank
        rows = [jnp.where(mine, place.astype(F32), 0.0)]
        rows += [jnp.where(mine, traces[s : s + 1], 0.0) for s in range(steps)]
        size = SLOTS * len(rows)
        above = [jnp.zeros((row, RECEIVERS), F32)] if row else []
        below = [jnp.zeros((128 - row - size, RECEIVERS), F32)]
        kept.append(jnp.concatenate(above + rows + below, axis=0))
        hits.append(hit.astype(BF16))
        row += size
    hits = jnp.concatenate(hits, axis=1)
    high, low = halves(jnp.concatenate(kept, axis=1))
    sent = dot_nt(hits, high) + dot_nt(hits, low)
    rounds = (jnp.max(last_rank, axis=1, keepdims=True).astype(I32) // SLOTS + 1).astype(F32)
    return jnp.where(iota((DEVICES, 128), 1) >= row, rounds, sent)


def route_more_kernel(first_ref, cells, traces, sent_ref, cells_v, traces_v, sems):
    for copy in started([(cells, cells_v), (traces, traces_v)], sems):
        copy.wait()
    sent_ref[:, 0, :] = routed(cells_v[...], traces_v[...], first_ref[0])


def collected(got):
    rows = got.T
    sums, row = [], 0
    down = iota((TZ, DEVICES), 0).astype(F32).astype(BF16)
    unit, zero = jnp.ones((), BF16), jnp.zeros((), BF16)
    for columns, steps in ((TX * 8, 2), (TX * 8, 1), (64, 1)):
        cell = rows[row : row + SLOTS].astype(I32)
        column, depth = (cell >> 7).astype(F32), (cell & 127).astype(F32)
        at = iota((columns, DEVICES), 0).astype(F32).astype(BF16)
        one, parts = [], [[] for _ in range(2 * steps)]
        for k in range(SLOTS):
            one.append(jnp.where(at == column[k : k + 1].astype(BF16), unit, zero))
            same = down == depth[k : k + 1].astype(BF16)
            for s in range(steps):
                value = rows[row + (s + 1) * SLOTS + k : row + (s + 1) * SLOTS + k + 1]
                high, low = halves(value)
                parts[2 * s].append(jnp.where(same, high, zero))
                parts[2 * s + 1].append(jnp.where(same, low, zero))
        one = jnp.concatenate(one, axis=1)
        both = dot_nt(one, jnp.concatenate([jnp.concatenate(part, axis=1) for part in parts], axis=0))
        for s in range(steps):
            sums.append(both[:, 256 * s : 256 * s + 128] + both[:, 256 * s + 128 : 256 * s + 256])
        row += SLOTS * (steps + 1)
    return sums


def collect_kernel(got_ref, inner_courant, own_ref, rim_y_ref, rim_x_ref, rounds_ref):
    got = got_ref[...]
    own_0, own_1, rim_y, rim_x = collected(got)
    own_ref[0] = own_0.reshape(TX, 8, 128)
    own_ref[1] = own_1.reshape(TX, 8, 128)
    rim_y_ref[...] = rim_y.reshape(TX, 8, 128)
    rim_x_ref[...] = rim_x.reshape(8, 8, 128)
    rounds_ref[0] = jnp.max(got[:, 112:128]).astype(I32)


def collect_more_kernel(got_ref, own_in, rim_y_in, rim_x_in, own_ref, rim_y_ref, rim_x_ref):
    own_0, own_1, rim_y, rim_x = collected(got_ref[:, 0, :])
    own_ref[0] = own_in[0] + own_0.reshape(TX, 8, 128)
    own_ref[1] = own_in[1] + own_1.reshape(TX, 8, 128)
    rim_y_ref[...] = rim_y_in[...] + rim_y.reshape(TX, 8, 128)
    rim_x_ref[...] = rim_x_in[...] + rim_x.reshape(8, 8, 128)


def strip_values_tile(values, step, rows):
    return jnp.concatenate([values[step, layer][rows] for layer in range(4)], axis=1)


def wide(depth):
    return jnp.concatenate([depth, jnp.zeros((depth.shape[0], 96), depth.dtype)], axis=1)


def started(copies, sems):
    copies = [pltpu.make_async_copy(*ends, sems.at[k]) for k, ends in enumerate(copies)]
    for copy in copies:
        copy.start()
    return copies


def pack_kernel(
    cells, traces, wavelet, s0, r0, sm, rm, c, depth, values,
    first_y, second_y, wavelet_ref, sm_v, rm_v, c_v, depth_v, values_v, sent_ref,
    sent_v, cells_v, traces_v, sems,
):
    copies = started(
        [
            (cells, cells_v), (traces, traces_v), (depth, depth_v), (values, values_v), (wavelet, wavelet_ref),
            (sm, sm_v), (rm, rm_v), (c, c_v),
            (s0, first_y.at[0:32]), (r0, first_y.at[32:64]), (s0, second_y.at[0:32]), (r0, second_y.at[32:64]),
        ],
        sems,
    )
    for copy in copies[:2]:
        copy.wait()
    sent_v[:, 0, :] = routed(cells_v[...], traces_v[...], jnp.int32(0))
    out = pltpu.make_async_copy(sent_v, sent_ref, sems.at[12])
    out.start()
    for copy in copies[2:8]:
        copy.wait()
    even = lax.axis_index("gy") % 2 == 0
    strips, depths = strip_values_tile(values_v, 0, slice(0, 8)), wide(depth_v[...].astype(F32))
    for ref, high in ((first_y, even), (second_y, ~even)):

        def four(rows):
            return jnp.where(high, rows[..., 4:8, :], rows[..., 0:4, :])

        ref[64:96, 0:4] = four(sm_v[...])
        ref[64:96, 4:8] = four(rm_v[...])
        ref[96:112, 0:4] = four(c_v[0:16])
        ref[96:112, 4:8] = four(c_v[16:32])
        ref[112, 0:4] = four(strips)
        ref[112, 4:8] = four(depths)
    for copy in copies[8:]:
        copy.wait()
    out.wait()


def depth_matrix():
    apart = jnp.abs(iota((TZ, TZ), 0) - iota((TZ, TZ), 1))
    weights = jnp.zeros((TZ, TZ), F32)
    for reach in range(1, 5):
        weights = jnp.where(apart == reach, COEFS[reach], weights)
    high, low = halves(weights)
    top = jnp.concatenate([high, low], axis=1)
    return jnp.concatenate([top, jnp.concatenate([high, jnp.zeros_like(low)], axis=1)], axis=0)


def depth_sums(rows, matrix):
    both = jnp.dot(jnp.concatenate(halves(rows), axis=1), matrix, preferred_element_type=F32)
    return both[:, :128] + both[:, 128:]


def curvature(ref, f, x, row, depth_sum):
    tile = ref[f, x, row : row + 8]
    total = (3.0 * COEFS[0]) * tile + depth_sum
    for reach in range(1, 5):
        pairs = ref[f, x + reach, row : row + 8] + ref[f, x - reach, row : row + 8]
        pairs = pairs + ref[f, x, row + reach : row + reach + 8]
        pairs = pairs + ref[f, x, row - reach : row - reach + 8]
        total = total + COEFS[reach] * pairs
    return tile, total


def overwritten(tile, depths, values, lane_start):
    lane = iota((8, 128), 1)
    column = jnp.full((8, 128), lane_start, I32)
    relative = lane - jnp.take_along_axis(depths, column, axis=1)
    fill = jnp.take_along_axis(values, (relative & 3) * 32 + column, axis=1)
    return jnp.where((relative >= 0) & (relative < 4), fill, tile)


def keeps(axis, size):
    at = lax.axis_index(axis)
    return jnp.where(at > 0, 1.0, 0.0), jnp.where(at < size - 1, 1.0, 0.0)


def pulse(source_cell, wavelet, step, row):
    cell = source_cell[0]
    lane, sublane = iota((8, 128), 1), iota((8, 128), 0)
    at_row = sublane + (row + lax.axis_index("gy") * TY) == (cell >> 7) & 127
    return jnp.where((lane == cell & 127) & at_row, wavelet[0:1, step : step + 1], 0.0)


def source_layer(source_cell):
    return (source_cell[0] >> 14) - lax.axis_index("gx") * TX


def advanced(i, at, x, e_ref, z_ref, m_ref, courant_ref, depth_ref, v_ref, pulses, source_x, new_ref):
    for t in range(2):
        rows = slice(8 * t, 8 * t + 8)
        courant = courant_ref[i, rows]
        now, total = curvature(e_ref, 0, at, 8 + 8 * t, z_ref[0, i, rows])
        if pulses is not None:
            total = total - jnp.where(x == source_x, pulses[t], 0.0)
        new = 2.0 * now - m_ref[0, i, rows] + courant * total
        new_ref[0, i, rows] = overwritten(new, depth_ref[rows], v_ref[rows], x)
        now, total = curvature(e_ref, 1, at, 8 + 8 * t, z_ref[1, i, rows])
        new_ref[1, i, rows] = 2.0 * now - m_ref[1, i, rows] + courant * total


def in_order(beside, first, second):
    even = lax.axis_index("gy") % 2 == 0

    @pl.when(even)
    def _():
        beside(second, first)

    @pl.when(~even)
    def _():
        beside(first, second)


def edge_kernel(
    own_y, sm, rm, c, depth, values, first, second,
    new_ref, courant_ref, depth_ref, v_ref, up_ref, down_ref,
    e_ref, m_ref, z_ref,
):
    keep_before, keep_after = keeps("gy", GY)
    spans = ((4, 0), (12, 24))
    for f in range(2):
        e_ref[f, 0:4, 8:24] = jnp.zeros((4, 16, 128), F32)
        e_ref[f, 20:24, 8:24] = jnp.zeros((4, 16, 128), F32)
        for to, start in spans:
            e_ref[f, to : to + 8, 12:20] = own_y[32 * f + start : 32 * f + start + 8]
    v_ref[4:12] = strip_values_tile(values, 0, slice(0, 8))
    depth_ref[4:12] = wide(depth[...])
    for to, start in ((0, 0), (4, 28)):
        layers = slice(to, to + 4)
        m_ref[0, layers, 4:12] = sm[start : start + 4]
        m_ref[1, layers, 4:12] = rm[start : start + 4]
        courant_ref[layers, 4:12] = c[start : start + 4]

    def beside(before, after):
        for f in range(2):
            for to, start in spans:
                layers = slice(32 * f + start, 32 * f + start + 8)
                e_ref[f, to : to + 8, 4:12] = before[layers] * keep_before
                e_ref[f, to : to + 8, 20:28] = after[layers] * keep_after
        for ref, keep, rows in ((before, keep_before, slice(0, 4)), (after, keep_after, slice(12, 16))):
            for to, start in ((0, 0), (4, 28)):
                layers, half = slice(to, to + 4), start // 16
                m_ref[0, layers, rows] = ref[64 + start : 68 + start, 0:4] * keep
                m_ref[1, layers, rows] = ref[64 + start : 68 + start, 4:8] * keep
                at = 96 + start - 16 * half
                courant_ref[layers, rows] = ref[at : at + 4, 4 * half : 4 * half + 4] * keep
            v_ref[rows] = ref[112, 0:4] * keep
            depth_ref[rows] = (ref[112, 4:8] * keep).astype(I32)

    in_order(beside, first, second)
    matrix = depth_matrix()
    for f in range(2):
        for half in range(2):
            rows = e_ref[f, 4 + 12 * half : 8 + 12 * half, 8:24].reshape(64, 128)
            z_ref[f, 4 * half : 4 * half + 4] = depth_sums(rows, matrix).reshape(4, 16, 128)
    for i in range(8):
        at, x = (i + 4, i) if i < 4 else (i + 12, i + 24)
        advanced(
            i, at, x, e_ref, z_ref, m_ref, courant_ref, depth_ref, v_ref, None, None, new_ref
        )
    for ref, to, rim, at in ((up_ref, 4, 28, 16), (down_ref, 0, 0, 4)):
        for f in range(2):
            ref[4 * f : 4 * f + 4] = new_ref[f, to : to + 4, 4:12]
            ref[12 + 4 * f : 16 + 4 * f] = own_y[32 * f + rim : 32 * f + rim + 4]
            ref[20 + 4 * f : 24 + 4 * f, 0:4] = e_ref[f, at : at + 4, 8:12]
            ref[20 + 4 * f : 24 + 4 * f, 4:8] = e_ref[f, at : at + 4, 20:24]
        ref[8:12] = c[rim : rim + 4]
        ref[28] = depth_ref[4:12].astype(F32)


def inner_kernel(
    source_cell,
    wavelet, own_y, sm, rm, c, first, second, depths, values,
    new_ref, courant_ref,
    e_ref, m_ref, z_ref,
):
    keep_before, keep_after = keeps("gy", GY)
    for f in range(2):
        e_ref[f, :, 12:20] = own_y[32 * f : 32 * f + 32]
    m_ref[0, :, 4:12] = sm[4:28]
    m_ref[1, :, 4:12] = rm[4:28]
    courant_ref[:, 4:12] = c[4:28]

    def beside(before, after):
        for f in range(2):
            e_ref[f, :, 4:12] = before[32 * f : 32 * f + 32] * keep_before
            e_ref[f, :, 20:28] = after[32 * f : 32 * f + 32] * keep_after
        for ref, keep, rows in ((before, keep_before, slice(0, 4)), (after, keep_after, slice(12, 16))):
            m_ref[0, :, rows] = ref[68:92, 0:4] * keep
            m_ref[1, :, rows] = ref[68:92, 4:8] * keep
            courant_ref[0:12, rows] = ref[100:112, 0:4] * keep
            courant_ref[12:24, rows] = ref[96:108, 4:8] * keep

    in_order(beside, first, second)
    pulses = [pulse(source_cell, wavelet, 0, 8 * t - 4) for t in range(2)]
    source_x = source_layer(source_cell)
    matrix = depth_matrix()
    for f in range(2):
        rows = e_ref[f, 4:28, 8:24].reshape(384, 128)
        z_ref[f] = depth_sums(rows, matrix).reshape(24, 16, 128)

    def layer(i, carry):
        advanced(
            i, i + 4, i + 4, e_ref, z_ref, m_ref, courant_ref, depths, values, pulses, source_x, new_ref
        )
        return carry

    lax.fori_loop(0, 24, layer, 0, unroll=8)


def unless_strip(depths, column, amount):
    relative = iota((8, 128), 1) - depths[:, column : column + 1]
    return jnp.where((relative >= 0) & (relative < 4), 0.0, amount)


def late_layer(x, at, i, o_ref, z_ref, s0, r0, c, own, depths, values, late_pulse, source_x, s_v, r_v, sub_ref, to):
    now, total = curvature(o_ref, 0, at, 8, z_ref[0, i])
    total = total - jnp.where(x == source_x, late_pulse, 0.0)
    new = 2.0 * now - s0[x] + c[x] * total
    new = overwritten(new, depths, values, x)
    s_v[i] = new
    for j in range(2):
        sub_ref[0, j, pl.ds(to, 1)] = now[4 * j : 4 * j + 1]
        sub_ref[1, j, pl.ds(to, 1)] = new[4 * j : 4 * j + 1]
    now, total = curvature(o_ref, 1, at, 8, z_ref[1, i])
    new = 2.0 * now - r0[x] + c[x] * (total + own[1, x])
    r_v[i] = new
    for j in range(2):
        sub_ref[2, j, pl.ds(to, 1)] = now[4 * j : 4 * j + 1]
        sub_ref[3, j, pl.ds(to, 1)] = new[4 * j : 4 * j + 1]


def middle_kernel(
    source_cell,
    wavelet, own_y, c, depth, values, inner, inner_courant, own, rim_y,
    r1_ref, s_v, r_v, sub_ref,
    o_ref, z_ref,
):
    o_ref[0, :, 4:20] = inner[0]
    o_ref[1, :, 8:16] = inner[1, :, 4:12] + inner_courant[:, 4:12] * own[0, 4:28]
    o_ref[1, :, 4:8] = inner[1, :, 0:4] + inner_courant[:, 0:4] * rim_y[4:28, 0:4]
    o_ref[1, :, 16:20] = inner[1, :, 12:16] + inner_courant[:, 12:16] * rim_y[4:28, 4:8]
    for half in range(2):
        r1_ref[8 * half : 8 * half + 8] = o_ref[1, 16 * half : 16 * half + 8, 4:20]
    matrix = depth_matrix()
    for f in range(2):
        rows = o_ref[f, 4:20, 8:16].reshape(128, 128)
        z_ref[f] = depth_sums(rows, matrix).reshape(16, 8, 128)
    late_values = strip_values_tile(values, 1, slice(0, 8))
    near_depth = wide(depth[...])
    late_pulse, source_x = pulse(source_cell, wavelet, 1, 0), source_layer(source_cell)

    def layer(i, carry):
        late_layer(
            i + 8, i + 4, i, o_ref, z_ref, own_y.at[0:32], own_y.at[32:64], c, own,
            near_depth, late_values, late_pulse, source_x, s_v, r_v, sub_ref, i,
        )
        return carry

    lax.fori_loop(0, 16, layer, 0, unroll=16)


def steps_kernel(
    source_cell,
    wavelet, own_y, c, depth, values, left, right, edge, edge_courant, inner, depths,
    own, rim_y, rim_x, r1, sub_mid,
    s_v, r_v, near_ref, up_ref, down_ref,
    o_ref, h_ref, z_ref, sub_ref,
):
    keep_left, keep_right = keeps("gx", GX)
    s0, r0 = own_y.at[0:32], own_y.at[32:64]
    for start, first in ((0, 0), (4, 28)):
        to, part, x = slice(first + 4, first + 8), slice(start, start + 4), slice(first, first + 4)
        o_ref[0, to, 4:20] = edge[0, part]
        o_ref[1, to, 8:16] = edge[1, part, 4:12] + edge_courant[part, 4:12] * own[0, x]
        o_ref[1, to, 4:8] = edge[1, part, 0:4] + edge_courant[part, 0:4] * rim_y[x, 0:4]
        o_ref[1, to, 16:20] = edge[1, part, 12:16] + edge_courant[part, 12:16] * rim_y[x, 4:8]
    for half in range(2):
        to = slice(8 + 16 * half, 16 + 16 * half)
        o_ref[0, to, 4:20] = inner[0, 16 * half : 16 * half + 8]
        o_ref[1, to, 4:20] = r1[8 * half : 8 * half + 8]
    source_x = source_layer(source_cell)
    pulses = [pulse(source_cell, wavelet, 0, row) for row in (-4, 4, 0)]
    for side, ref, keep in ((0, left, keep_left), (1, right, keep_right)):
        beyond_depths = (ref[28] * keep).astype(I32)
        for f in range(2):
            h_ref[f, side, :, 4:12] = ref[12 + 4 * f : 16 + 4 * f] * keep
            h_ref[f, side, :, 0:4] = ref[20 + 4 * f : 24 + 4 * f, 0:4] * keep
            h_ref[f, side, :, 12:16] = ref[20 + 4 * f : 24 + 4 * f, 4:8] * keep
        for n in range(4):
            x = 31 - n if side else n
            for f in range(2):
                for t in range(2):
                    rows = slice(8 * t, 8 * t + 8)
                    amount = None
                    for reach in range(n + 1, 5):
                        away = reach - n
                        term = COEFS[reach] * h_ref[f, side, away - 1 if side else 4 - away, rows]
                        amount = term if amount is None else amount + term
                    if f == 0:
                        amount = amount - jnp.where(x == source_x, pulses[t], 0.0)
                    amount = edge_courant[x - 24 if side else x, rows] * amount
                    if f == 0:
                        amount = unless_strip(depths[rows], x, amount)
                    at = slice(4 + 8 * t, 12 + 8 * t)
                    o_ref[f, x + 4, at] = o_ref[f, x + 4, at] + amount
            k = n if side else 3 - n
            for f, field in ((0, s0), (1, r0)):
                amount = None
                for reach in range(n + 1, 5):
                    inward = reach - n - 1
                    term = COEFS[reach] * field[31 - inward if side else inward]
                    amount = term if amount is None else amount + term
                if f == 0:
                    beyond = 32 + n if side else -1 - n
                    amount = amount - jnp.where(beyond == source_x, pulses[2], 0.0)
                else:
                    amount = amount + rim_x[4 * side + k]
                amount = ref[8 + k] * amount
                if f == 0:
                    amount = unless_strip(beyond_depths, k if side else 28 + k, amount)
                o_ref[f, 36 + n if side else 3 - n, 8:16] = (ref[4 * f + k] + amount) * keep
    matrix = depth_matrix()
    for f in range(2):
        for half in range(2):
            rows = o_ref[f, 4 + 24 * half : 12 + 24 * half, 8:16].reshape(64, 128)
            z_ref[f, 8 * half : 8 * half + 8] = depth_sums(rows, matrix).reshape(8, 8, 128)
    late_values = strip_values_tile(values, 1, slice(0, 8))
    near_depth = wide(depth[...])
    late_pulse = pulse(source_cell, wavelet, 1, 0)
    for k in range(4):
        for j in range(2):
            sub_ref[k, j, 8:24] = sub_mid[k, j]
    for i in range(16):
        x = i if i < 8 else i + 16
        late_layer(
            x, x + 4, i, o_ref, z_ref, s0, r0, c, own,
            near_depth, late_values, late_pulse, source_x, s_v, r_v, sub_ref, x,
        )
    z, to = iota((TZ, 128), 0), iota((TZ, 128), 1)
    totals = []
    for k in range(4):
        total = None
        for j in range(2):
            pick = jnp.where((z & 3 == 0) & (to == (z >> 2) + (16 + 64 * j)), 1.0, 0.0)
            part = jnp.dot(
                sub_ref[k, j], pick, precision=lax.Precision.HIGHEST, preferred_element_type=F32
            )
            total = part if total is None else total + part
        near_ref[k] = total
        totals.append(total)
    for f in range(2):
        packed = totals[2 * f] + pltpu.roll(totals[2 * f + 1], 32, 1)
        up_ref[f] = packed[16:32]
        down_ref[f] = packed[0:16]


def store_kernel(s_mid, r_mid, s_edge, r_edge, s_out, r_out, sems):
    ends = [
        pair
        for mid, edge, to in ((s_mid, s_edge, s_out), (r_mid, r_edge, r_out))
        for pair in ((mid, to.at[8:24]), (edge.at[0:8], to.at[0:8]), (edge.at[8:16], to.at[24:32]))
    ]
    for copy in started(ends, sems):
        copy.wait()


def angles_kernel(stored, near, left, right, out_ref, g_ref):
    keep_left, keep_right = keeps("gx", GX)
    lane = iota((16, 128), 1)
    held = ((lane >= 16) & (lane < 48)) | ((lane >= 80) & (lane < 112))
    for f in range(2):
        for ref, keep, rows in ((left, keep_left, slice(0, 16)), (right, keep_right, slice(48, 64))):
            packed = ref[f] * keep
            g_ref[2 * f, rows] = jnp.where(held, packed, 0.0)
            g_ref[2 * f + 1, rows] = jnp.where(held, pltpu.roll(packed, 96, 1), 0.0)
    for k in range(4):
        g_ref[k, 16:48] = near[k]
    sums = [None] * 32
    for lag in range(-16, 17):
        product = None
        for step in range(2):
            source = g_ref[step, pl.ds(16 - lag, 8, stride=4)]
            receiver = g_ref[2 + step, pl.ds(16 + lag, 8, stride=4)]
            part = source * receiver
            product = part if product is None else product + part
        shifted = {}

        def shift(amount):
            if amount not in shifted:
                shifted[amount] = product if amount == 0 else pltpu.roll(product, -amount % 128, 1)
            return shifted[amount]

        for a in range(32):
            move = np.float32(lag) * SLOPES[a] / np.float32(4.0)
            low = np.floor(move)
            frac = float(move - low)
            term = shift(int(low)) * (1.0 - frac)
            if frac != 0.0:
                term = term + shift(int(low) + 1) * frac
            sums[a] = term if sums[a] is None else sums[a] + term
    lane = iota((8, 128), 1)
    for b in range(16):
        first, second = sums[2 * b], sums[2 * b + 1]
        packed = jnp.where(lane < 32, pltpu.roll(first, 112, 1), pltpu.roll(first, 80, 1))
        other = jnp.where(lane < 96, pltpu.roll(second, 48, 1), pltpu.roll(second, 16, 1))
        out_ref[b] = jnp.where(lane < 64, packed, other)


def arrange_kernel(got, image, out_v, sems):
    lane = iota((8, 128), 1)
    copies = []
    for a in range(2):
        for t in range(8):
            even, odd = got[2 * t], got[2 * t + 1]
            if a == 0:
                odd = pltpu.roll(odd, 64, 1)
            else:
                even = pltpu.roll(even, 64, 1)
            out_v[a, :, 128 * t : 128 * t + 128] = jnp.where(lane < 64, even, odd)
        copies.append(pltpu.make_async_copy(out_v.at[a], image.at[a], sems.at[a]))
        copies[a].start()
    for copy in copies:
        copy.wait()


def call(kernel, outs, arrays, scalars=(), hbm=(), out_scalars=0, out_hbm=(), scratch=(), weight=0):
    smem, vmem = pl.BlockSpec(memory_space=pltpu.SMEM), pl.BlockSpec(memory_space=pltpu.VMEM)
    far = pl.BlockSpec(memory_space=pltpu.HBM)
    hbm = [
        pltpu.with_memory_space_constraint(array, pltpu.HBM) for array in hbm
    ]
    return pl.pallas_call(
        kernel,
        out_shape=[jax.ShapeDtypeStruct(shape, kind) for shape, kind in outs],
        in_specs=[smem] * len(scalars) + [far] * len(hbm) + [vmem] * len(arrays),
        out_specs=[
            smem if k >= len(outs) - out_scalars else far if k in out_hbm else vmem for k in range(len(outs))
        ],
        scratch_shapes=list(scratch),
        compiler_params=pltpu.CompilerParams(vmem_limit_bytes=VMEM_LIMIT),
        cost_estimate=pl.CostEstimate(flops=0, bytes_accessed=weight, transcendentals=0) if weight else None,
    )(*scalars, *hbm, *arrays)


def both_ways(to_next, to_last, axis):
    size = lax.axis_size(axis)
    from_last = lax.ppermute(to_next, axis, [(i, (i + 1) % size) for i in range(size)])
    from_next = lax.ppermute(to_last, axis, [((i + 1) % size, i) for i in range(size)])
    return from_last, from_next


def body(
    source_now,
    source_next,
    receiver_now,
    receiver_next,
    courant,
    source_cell,
    wavelet,
    receiver_cells,
    receiver_traces,
    strip_depth,
    strip_values,
):
    cells = receiver_cells.reshape(1, RECEIVERS)
    tile, sent_shape = (TX, TY, TZ), ((DEVICES, 1, 128), F32)
    listed = [((1, RECEIVERS), I32), ((2, RECEIVERS), F32)]
    fields = (source_now, receiver_now, source_next, receiver_next, courant, strip_depth, strip_values)
    first_y, second_y, near_wavelet, near_sm, near_rm, near_c, near_depth, near_values, sent = call(
        pack_kernel,
        [((113, 8, 128), F32)] * 2
        + [((1, 2), F32), *[(tile, F32)] * 3, ((8, 32), I32), ((2, 4, 8, 32), F32), sent_shape],
        [],
        hbm=[cells, receiver_traces, wavelet.reshape(1, 2), *fields],
        out_hbm=(8,),
        scratch=[pltpu.VMEM(*shape) for shape in (sent_shape, *listed)] + [pltpu.SemaphoreType.DMA((13,))],
    )
    pairs = [(i, i ^ 1) for i in range(GY)]
    first = lax.ppermute(first_y, "gy", pairs)
    second = lax.ppermute(second_y, "gy", [(i, (i + 1 if i % 2 else i - 1) % GY) for i in range(GY)])
    got = lax.all_to_all(sent, ("gx", "gy"), 0, 0, tiled=True)
    got = jnp.maximum(got.reshape(DEVICES, 128), -jnp.finfo(F32).max)
    edge, edge_courant, depths, strips, up_x, down_x = call(
        edge_kernel,
        [((2, 8, 16, 128), F32), ((8, 16, 128), F32), ((16, 128), I32), ((16, 128), F32)]
        + [((29, 8, 128), F32)] * 2,
        [first_y, near_sm, near_rm, near_c, near_depth, near_values, first, second],
        scratch=[
            pltpu.VMEM((2, 24, 32, 128), F32),
            pltpu.VMEM((2, 8, 16, 128), F32),
            pltpu.VMEM((2, 8, 16, 128), F32),
        ],
    )
    left, right = both_ways(up_x, down_x, "gx")
    inner, inner_courant = call(
        inner_kernel,
        [((2, 24, 16, 128), F32), ((24, 16, 128), F32)],
        [near_wavelet, first_y, near_sm, near_rm, near_c, first, second, depths, strips],
        scalars=[source_cell],
        scratch=[
            pltpu.VMEM((2, 32, 32, 128), F32),
            pltpu.VMEM((2, 24, 16, 128), F32),
            pltpu.VMEM((2, 24, 16, 128), F32),
        ],
    )
    sums = [((2, *tile), F32), (tile, F32), ((8, 8, 128), F32)]
    own, rim_y, rim_x, rounds = call(collect_kernel, [*sums, ((1,), I32)], [got, inner_courant], out_scalars=1, weight=1000)

    def another(state):
        turn, *partial = state
        (more,) = call(
            route_more_kernel,
            [sent_shape],
            [],
            scalars=[(turn * SLOTS).reshape(1)],
            hbm=[cells, receiver_traces],
            scratch=[pltpu.VMEM(*shape) for shape in listed] + [pltpu.SemaphoreType.DMA((2,))],
        )
        more = lax.all_to_all(more, ("gx", "gy"), 0, 0, tiled=True)
        return (turn + 1, *call(collect_more_kernel, sums, [more, *partial]))

    _, own, rim_y, rim_x = lax.while_loop(
        lambda state: state[0] < rounds[0], another, (jnp.int32(1), own, rim_y, rim_x)
    )
    part = (16, TY, TZ)
    r1, s_mid, r_mid, sub_mid = call(
        middle_kernel,
        [((16, 16, 128), F32), (part, F32), (part, F32), ((4, 2, 16, 128), F32)],
        [near_wavelet, first_y, near_c, near_depth, near_values, inner, inner_courant, own, rim_y],
        scalars=[source_cell],
        scratch=[pltpu.VMEM((2, 24, 24, 128), F32), pltpu.VMEM((2, 16, 8, 128), F32)],
    )
    s_edge, r_edge, near, up, down = call(
        steps_kernel,
        [(part, F32), (part, F32), ((4, 32, 128), F32), ((2, 16, 128), F32), ((2, 16, 128), F32)],
        [
            near_wavelet, first_y, near_c, near_depth, near_values, left, right, edge, edge_courant,
            inner, depths, own, rim_y, rim_x, r1, sub_mid,
        ],
        scalars=[source_cell],
        scratch=[
            pltpu.VMEM((2, 40, 24, 128), F32),
            pltpu.VMEM((2, 2, 4, 16, 128), F32),
            pltpu.VMEM((2, 16, 8, 128), F32),
            pltpu.VMEM((4, 2, 32, 128), F32),
        ],
    )
    near_left, near_right = both_ways(up, down, "gx")
    source_field, receiver_field = call(
        store_kernel,
        [(tile, F32), (tile, F32)],
        [s_mid, r_mid, s_edge, r_edge],
        out_hbm=(0, 1),
        scratch=[pltpu.SemaphoreType.DMA((6,))],
        weight=1_000_000,
    )
    (angles,) = call(
        angles_kernel, [((16, 8, 128), F32)], [near, near_left, near_right], hbm=[source_field],
        scratch=[pltpu.VMEM((4, 64, 128), F32)],
    )
    angles = lax.all_to_all(angles, "gy", 0, 0, tiled=True)
    image_shape = ((2, 8, 1024), F32)
    (image,) = call(
        arrange_kernel,
        [image_shape],
        [angles],
        out_hbm=(0,),
        scratch=[pltpu.VMEM(*image_shape), pltpu.SemaphoreType.DMA((2,))],
    )
    return source_field, receiver_field, image


def solution(mesh):
    return jax.shard_map(
        body,
        mesh=mesh,
        in_specs=(
            P("gx", "gy", None),
            P("gx", "gy", None),
            P("gx", "gy", None),
            P("gx", "gy", None),
            P("gx", "gy", None),
            P(),
            P(),
            P(("gx", "gy")),
            P(None, ("gx", "gy")),
            P("gy", "gx"),
            P(None, None, "gy", "gx"),
        ),
        out_specs=(P("gx", "gy", None), P("gx", "gy", None), P("gy", "gx", None)),
        check_vma=False,
    )
```

```python
import math

import jax
import jax.numpy as jnp
import numpy as np
from jax import lax
from jax.experimental import pallas as pl
from jax.experimental.pallas import tpu as pltpu
from jax.sharding import PartitionSpec as P

COEFS = (-205.0 / 72.0, 8.0 / 5.0, -1.0 / 5.0, 8.0 / 315.0, -1.0 / 560.0)
SLOPES = np.array(
    [math.tan(math.pi * (-60.0 + 120.0 * (angle + 0.5) / 32.0) / 180.0) for angle in range(32)],
    dtype=np.float32,
)
GX, GY = 8, 16
TX, TY, TZ = 32, 8, 128
DEVICES = GX * GY
RECEIVERS = 256
SLOTS = 16
F32, BF16, I32 = jnp.float32, jnp.bfloat16, jnp.int32
VMEM_LIMIT = 24 * 1024 * 1024


def iota(shape, dim):
    return lax.broadcasted_iota(I32, shape, dim)


def halves(value):
    high = value.astype(BF16)
    return high, (value - high.astype(F32)).astype(BF16)


def dot_nt(left, right):
    return lax.dot_general(left, right, (((1,), (1,)), ((), ())), preferred_element_type=F32)


def routed(cells, traces, first_slot):
    x, y, z = cells >> 14, (cells >> 7) & 127, cells & 127
    tile_x, tile_y, in_x, in_y = x >> 5, y >> 3, x & 31, y & 7
    beside_y = jnp.where(in_y < 4, tile_y - 1, tile_y + 1)
    beside_x = jnp.where(in_x < 4, tile_x - 1, jnp.where(in_x >= 28, tile_x + 1, -1))
    to_y = jnp.where((beside_y >= 0) & (beside_y < GY), tile_x * GY + beside_y, -1)
    to_x = jnp.where((beside_x >= 0) & (beside_x < GX), beside_x * GY + tile_y, -1)
    rim_x = jnp.where(in_x < 4, in_x + 4, in_x - 28)
    classes = (
        (tile_x * GY + tile_y, (in_x * 8 + in_y) * 128 + z, 2),
        (to_y, (in_x * 8 + (in_y ^ 4)) * 128 + z, 1),
        (to_x, (rim_x * 8 + in_y) * 128 + z, 1),
    )
    earlier = jnp.where(
        iota((RECEIVERS, RECEIVERS), 0) < iota((RECEIVERS, RECEIVERS), 1), 1.0, 0.0
    ).astype(BF16)
    device = iota((DEVICES, RECEIVERS), 0)
    slot = iota((SLOTS, RECEIVERS), 0).astype(F32) + first_slot.astype(F32)
    hits, kept, last_rank, row = [], [], None, 0
    for target, place, steps in classes:
        hit = jnp.where(device == target, 1.0, 0.0)
        before = jnp.dot(hit.astype(BF16), earlier, preferred_element_type=F32)
        rank = jnp.sum(hit * before, axis=0, keepdims=True)
        last_rank = rank if last_rank is None else jnp.maximum(last_rank, rank)
        mine = slot == rank
        rows = [jnp.where(mine, place.astype(F32), 0.0)]
        rows += [jnp.where(mine, traces[s : s + 1], 0.0) for s in range(steps)]
        size = SLOTS * len(rows)
        above = [jnp.zeros((row, RECEIVERS), F32)] if row else []
        below = [jnp.zeros((128 - row - size, RECEIVERS), F32)]
        kept.append(jnp.concatenate(above + rows + below, axis=0))
        hits.append(hit.astype(BF16))
        row += size
    hits = jnp.concatenate(hits, axis=1)
    high, low = halves(jnp.concatenate(kept, axis=1))
    sent = dot_nt(hits, high) + dot_nt(hits, low)
    rounds = (jnp.max(last_rank, axis=1, keepdims=True).astype(I32) // SLOTS + 1).astype(F32)
    return jnp.where(iota((DEVICES, 128), 1) >= row, rounds, sent)


def route_more_kernel(first_ref, cells, traces, sent_ref, cells_v, traces_v, sems):
    for copy in started([(cells, cells_v), (traces, traces_v)], sems):
        copy.wait()
    sent_ref[:, 0, :] = routed(cells_v[...], traces_v[...], first_ref[0])


def collected(got):
    rows = got.T
    sums, row = [], 0
    down = iota((TZ, DEVICES), 0).astype(F32).astype(BF16)
    unit, zero = jnp.ones((), BF16), jnp.zeros((), BF16)
    for columns, steps in ((TX * 8, 2), (TX * 8, 1), (64, 1)):
        cell = rows[row : row + SLOTS].astype(I32)
        column, depth = (cell >> 7).astype(F32), (cell & 127).astype(F32)
        at = iota((columns, DEVICES), 0).astype(F32).astype(BF16)
        one, parts = [], [[] for _ in range(2 * steps)]
        for k in range(SLOTS):
            one.append(jnp.where(at == column[k : k + 1].astype(BF16), unit, zero))
            same = down == depth[k : k + 1].astype(BF16)
            for s in range(steps):
                value = rows[row + (s + 1) * SLOTS + k : row + (s + 1) * SLOTS + k + 1]
                high, low = halves(value)
                parts[2 * s].append(jnp.where(same, high, zero))
                parts[2 * s + 1].append(jnp.where(same, low, zero))
        one = jnp.concatenate(one, axis=1)
        both = dot_nt(one, jnp.concatenate([jnp.concatenate(part, axis=1) for part in parts], axis=0))
        for s in range(steps):
            sums.append(both[:, 256 * s : 256 * s + 128] + both[:, 256 * s + 128 : 256 * s + 256])
        row += SLOTS * (steps + 1)
    return sums


def collect_kernel(got_ref, inner_courant, own_ref, rim_y_ref, rim_x_ref, rounds_ref):
    got = got_ref[...]
    own_0, own_1, rim_y, rim_x = collected(got)
    own_ref[0] = own_0.reshape(TX, 8, 128)
    own_ref[1] = own_1.reshape(TX, 8, 128)
    rim_y_ref[...] = rim_y.reshape(TX, 8, 128)
    rim_x_ref[...] = rim_x.reshape(8, 8, 128)
    rounds_ref[0] = jnp.max(got[:, 112:128]).astype(I32)


def collect_more_kernel(got_ref, own_in, rim_y_in, rim_x_in, own_ref, rim_y_ref, rim_x_ref):
    own_0, own_1, rim_y, rim_x = collected(got_ref[:, 0, :])
    own_ref[0] = own_in[0] + own_0.reshape(TX, 8, 128)
    own_ref[1] = own_in[1] + own_1.reshape(TX, 8, 128)
    rim_y_ref[...] = rim_y_in[...] + rim_y.reshape(TX, 8, 128)
    rim_x_ref[...] = rim_x_in[...] + rim_x.reshape(8, 8, 128)


def strip_values_tile(values, step, rows):
    return jnp.concatenate([values[step, layer][rows] for layer in range(4)], axis=1)


def wide(depth):
    return jnp.concatenate([depth, jnp.zeros((depth.shape[0], 96), depth.dtype)], axis=1)


def started(copies, sems):
    copies = [pltpu.make_async_copy(*ends, sems.at[k]) for k, ends in enumerate(copies)]
    for copy in copies:
        copy.start()
    return copies


def pack_kernel(
    cells, traces, wavelet, s0, r0, sm, rm, c, depth, values,
    first_y, second_y, wavelet_ref, sm_v, rm_v, c_v, depth_v, values_v, sent_ref,
    sent_v, cells_v, traces_v, sems,
):
    copies = started(
        [
            (cells, cells_v), (traces, traces_v), (depth, depth_v), (values, values_v), (wavelet, wavelet_ref),
            (sm, sm_v), (rm, rm_v), (c, c_v),
            (s0, first_y.at[0:32]), (r0, first_y.at[32:64]), (s0, second_y.at[0:32]), (r0, second_y.at[32:64]),
        ],
        sems,
    )
    for copy in copies[:2]:
        copy.wait()
    sent_v[:, 0, :] = routed(cells_v[...], traces_v[...], jnp.int32(0))
    out = pltpu.make_async_copy(sent_v, sent_ref, sems.at[12])
    out.start()
    for copy in copies[2:8]:
        copy.wait()
    even = lax.axis_index("gy") % 2 == 0
    strips, depths = strip_values_tile(values_v, 0, slice(0, 8)), wide(depth_v[...].astype(F32))
    for ref, high in ((first_y, even), (second_y, ~even)):

        def four(rows):
            return jnp.where(high, rows[..., 4:8, :], rows[..., 0:4, :])

        ref[64:96, 0:4] = four(sm_v[...])
        ref[64:96, 4:8] = four(rm_v[...])
        ref[96:112, 0:4] = four(c_v[0:16])
        ref[96:112, 4:8] = four(c_v[16:32])
        ref[112, 0:4] = four(strips)
        ref[112, 4:8] = four(depths)
    for copy in copies[8:]:
        copy.wait()
    out.wait()


def depth_matrix():
    apart = jnp.abs(iota((TZ, TZ), 0) - iota((TZ, TZ), 1))
    weights = jnp.zeros((TZ, TZ), F32)
    for reach in range(1, 5):
        weights = jnp.where(apart == reach, COEFS[reach], weights)
    high, low = halves(weights)
    top = jnp.concatenate([high, low], axis=1)
    return jnp.concatenate([top, jnp.concatenate([high, jnp.zeros_like(low)], axis=1)], axis=0)


def depth_sums(rows, matrix):
    both = jnp.dot(jnp.concatenate(halves(rows), axis=1), matrix, preferred_element_type=F32)
    return both[:, :128] + both[:, 128:]


def curvature(ref, f, x, row, depth_sum):
    tile = ref[f, x, row : row + 8]
    total = (3.0 * COEFS[0]) * tile + depth_sum
    for reach in range(1, 5):
        pairs = ref[f, x + reach, row : row + 8] + ref[f, x - reach, row : row + 8]
        pairs = pairs + ref[f, x, row + reach : row + reach + 8]
        pairs = pairs + ref[f, x, row - reach : row - reach + 8]
        total = total + COEFS[reach] * pairs
    return tile, total


def overwritten(tile, depths, values, lane_start):
    lane = iota((8, 128), 1)
    column = jnp.full((8, 128), lane_start, I32)
    relative = lane - jnp.take_along_axis(depths, column, axis=1)
    fill = jnp.take_along_axis(values, (relative & 3) * 32 + column, axis=1)
    return jnp.where((relative >= 0) & (relative < 4), fill, tile)


def keeps(axis, size):
    at = lax.axis_index(axis)
    return jnp.where(at > 0, 1.0, 0.0), jnp.where(at < size - 1, 1.0, 0.0)


def pulse(source_cell, wavelet, step, row):
    cell = source_cell[0, 0]
    lane, sublane = iota((8, 128), 1), iota((8, 128), 0)
    at_row = sublane + (row + lax.axis_index("gy") * TY) == (cell >> 7) & 127
    return jnp.where((lane == cell & 127) & at_row, wavelet[0:1, step : step + 1], 0.0)


def source_layer(source_cell):
    return (source_cell[0, 0] >> 14) - lax.axis_index("gx") * TX


def advanced(i, at, x, e_ref, z_ref, m_ref, courant_ref, depth_ref, v_ref, new_ref):
    for t in range(2):
        rows = slice(8 * t, 8 * t + 8)
        courant = courant_ref[i, rows]
        now, total = curvature(e_ref, 0, at, 8 + 8 * t, z_ref[0, i, rows])
        new = 2.0 * now - m_ref[0, i, rows] + courant * total
        new_ref[0, i, rows] = overwritten(new, depth_ref[rows], v_ref[rows], x)
        now, total = curvature(e_ref, 1, at, 8 + 8 * t, z_ref[1, i, rows])
        new_ref[1, i, rows] = 2.0 * now - m_ref[1, i, rows] + courant * total


def in_order(beside, first, second):
    even = lax.axis_index("gy") % 2 == 0

    @pl.when(even)
    def _():
        beside(second, first)

    @pl.when(~even)
    def _():
        beside(first, second)


def edge_kernel(
    own_y, sm, rm, c, depth, values, first, second,
    new_ref, courant_ref, depth_ref, v_ref, up_ref, down_ref,
    e_ref, m_ref, z_ref,
):
    keep_before, keep_after = keeps("gy", GY)
    spans = ((4, 0), (12, 24))
    for f in range(2):
        e_ref[f, 0:4, 8:24] = jnp.zeros((4, 16, 128), F32)
        e_ref[f, 20:24, 8:24] = jnp.zeros((4, 16, 128), F32)
        for to, start in spans:
            e_ref[f, to : to + 8, 12:20] = own_y[32 * f + start : 32 * f + start + 8]
    v_ref[4:12] = strip_values_tile(values, 0, slice(0, 8))
    depth_ref[4:12] = wide(depth[...])
    for to, start in ((0, 0), (4, 28)):
        layers = slice(to, to + 4)
        m_ref[0, layers, 4:12] = sm[start : start + 4]
        m_ref[1, layers, 4:12] = rm[start : start + 4]
        courant_ref[layers, 4:12] = c[start : start + 4]

    def beside(before, after):
        for f in range(2):
            for to, start in spans:
                layers = slice(32 * f + start, 32 * f + start + 8)
                e_ref[f, to : to + 8, 4:12] = before[layers] * keep_before
                e_ref[f, to : to + 8, 20:28] = after[layers] * keep_after
        for ref, keep, rows in ((before, keep_before, slice(0, 4)), (after, keep_after, slice(12, 16))):
            for to, start in ((0, 0), (4, 28)):
                layers, half = slice(to, to + 4), start // 16
                m_ref[0, layers, rows] = ref[64 + start : 68 + start, 0:4] * keep
                m_ref[1, layers, rows] = ref[64 + start : 68 + start, 4:8] * keep
                at = 96 + start - 16 * half
                courant_ref[layers, rows] = ref[at : at + 4, 4 * half : 4 * half + 4] * keep
            v_ref[rows] = ref[112, 0:4] * keep
            depth_ref[rows] = (ref[112, 4:8] * keep).astype(I32)

    in_order(beside, first, second)
    matrix = depth_matrix()
    for f in range(2):
        for half in range(2):
            rows = e_ref[f, 4 + 12 * half : 8 + 12 * half, 8:24].reshape(64, 128)
            z_ref[f, 4 * half : 4 * half + 4] = depth_sums(rows, matrix).reshape(4, 16, 128)
    for i in range(8):
        at, x = (i + 4, i) if i < 4 else (i + 12, i + 24)
        advanced(
            i, at, x, e_ref, z_ref, m_ref, courant_ref, depth_ref, v_ref, new_ref
        )
    for ref, to, rim, at in ((up_ref, 4, 28, 16), (down_ref, 0, 0, 4)):
        for f in range(2):
            ref[4 * f : 4 * f + 4] = new_ref[f, to : to + 4, 4:12]
            ref[12 + 4 * f : 16 + 4 * f] = own_y[32 * f + rim : 32 * f + rim + 4]
            ref[20 + 4 * f : 24 + 4 * f, 0:4] = e_ref[f, at : at + 4, 8:12]
            ref[20 + 4 * f : 24 + 4 * f, 4:8] = e_ref[f, at : at + 4, 20:24]
        ref[8:12] = c[rim : rim + 4]
        ref[28] = depth_ref[4:12].astype(F32)


def inner_kernel(
    own_y, sm, rm, c, first, second, depths, values,
    new_ref, courant_ref,
    e_ref, m_ref, z_ref,
):
    keep_before, keep_after = keeps("gy", GY)
    for f in range(2):
        e_ref[f, :, 12:20] = own_y[32 * f : 32 * f + 32]
    m_ref[0, :, 4:12] = sm[4:28]
    m_ref[1, :, 4:12] = rm[4:28]
    courant_ref[:, 4:12] = c[4:28]

    def beside(before, after):
        for f in range(2):
            e_ref[f, :, 4:12] = before[32 * f : 32 * f + 32] * keep_before
            e_ref[f, :, 20:28] = after[32 * f : 32 * f + 32] * keep_after
        for ref, keep, rows in ((before, keep_before, slice(0, 4)), (after, keep_after, slice(12, 16))):
            m_ref[0, :, rows] = ref[68:92, 0:4] * keep
            m_ref[1, :, rows] = ref[68:92, 4:8] * keep
            courant_ref[0:12, rows] = ref[100:112, 0:4] * keep
            courant_ref[12:24, rows] = ref[96:108, 4:8] * keep

    in_order(beside, first, second)
    matrix = depth_matrix()
    for f in range(2):
        rows = e_ref[f, 4:28, 8:24].reshape(384, 128)
        z_ref[f] = depth_sums(rows, matrix).reshape(24, 16, 128)

    def layer(i, carry):
        advanced(
            i, i + 4, i + 4, e_ref, z_ref, m_ref, courant_ref, depths, values, new_ref
        )
        return carry

    lax.fori_loop(0, 24, layer, 0, unroll=8)


def unless_strip(depths, column, amount):
    relative = iota((8, 128), 1) - depths[:, column : column + 1]
    return jnp.where((relative >= 0) & (relative < 4), 0.0, amount)


def late_layer(x, at, i, o_ref, z_ref, s0, r0, c, own, depths, values, late_pulse, source_x, s_v, r_v, sub_ref, to):
    now, total = curvature(o_ref, 0, at, 8, z_ref[0, i])
    total = total - jnp.where(x == source_x, late_pulse, 0.0)
    new = 2.0 * now - s0[x] + c[x] * total
    new = overwritten(new, depths, values, x)
    s_v[i] = new
    for j in range(2):
        sub_ref[0, j, pl.ds(to, 1)] = now[4 * j : 4 * j + 1]
        sub_ref[1, j, pl.ds(to, 1)] = new[4 * j : 4 * j + 1]
    now, total = curvature(o_ref, 1, at, 8, z_ref[1, i])
    new = 2.0 * now - r0[x] + c[x] * (total + own[1, x])
    r_v[i] = new
    for j in range(2):
        sub_ref[2, j, pl.ds(to, 1)] = now[4 * j : 4 * j + 1]
        sub_ref[3, j, pl.ds(to, 1)] = new[4 * j : 4 * j + 1]


def middle_kernel(
    source_cell,
    wavelet, own_y, c, depth, values, inner, inner_courant, depths, own, rim_y,
    new_ref, s_v, r_v, sub_ref,
    o_ref, z_ref,
):
    o_ref[0, :, 4:20] = inner[0]
    o_ref[1, :, 8:16] = inner[1, :, 4:12] + inner_courant[:, 4:12] * own[0, 4:28]
    o_ref[1, :, 4:8] = inner[1, :, 0:4] + inner_courant[:, 0:4] * rim_y[4:28, 0:4]
    o_ref[1, :, 16:20] = inner[1, :, 12:16] + inner_courant[:, 12:16] * rim_y[4:28, 4:8]
    k = (source_cell[0, 0] >> 14) - lax.axis_index("gx") * TX - 4

    @pl.when((k >= 0) & (k < 24))
    def _():
        for t in range(2):
            rows, at = slice(8 * t, 8 * t + 8), slice(4 + 8 * t, 12 + 8 * t)
            column = jnp.full((8, 128), k + 4, I32)
            relative = iota((8, 128), 1) - jnp.take_along_axis(depths[rows], column, axis=1)
            amount = inner_courant[k, rows] * pulse(source_cell, wavelet, 0, 8 * t - 4)
            free = (relative < 0) | (relative >= 4)
            o_ref[0, k, at] = o_ref[0, k, at] - jnp.where(free, amount, 0.0)

    for f in range(2):
        for half in range(2):
            new_ref[f, 8 * half : 8 * half + 8] = o_ref[f, 16 * half : 16 * half + 8, 4:20]
    matrix = depth_matrix()
    for f in range(2):
        rows = o_ref[f, 4:20, 8:16].reshape(128, 128)
        z_ref[f] = depth_sums(rows, matrix).reshape(16, 8, 128)
    late_values = strip_values_tile(values, 1, slice(0, 8))
    near_depth = wide(depth[...])
    late_pulse, source_x = pulse(source_cell, wavelet, 1, 0), source_layer(source_cell)

    def layer(i, carry):
        late_layer(
            i + 8, i + 4, i, o_ref, z_ref, own_y.at[0:32], own_y.at[32:64], c, own,
            near_depth, late_values, late_pulse, source_x, s_v, r_v, sub_ref, i,
        )
        return carry

    lax.fori_loop(0, 16, layer, 0, unroll=16)


def steps_kernel(
    source_cell,
    wavelet, own_y, c, depth, values, left, right, edge, edge_courant, depths,
    own, rim_y, rim_x, inner, sub_mid,
    s_v, r_v, near_ref, up_ref, down_ref,
    o_ref, h_ref, z_ref, sub_ref,
):
    keep_left, keep_right = keeps("gx", GX)
    s0, r0 = own_y.at[0:32], own_y.at[32:64]
    for start, first in ((0, 0), (4, 28)):
        to, part, x = slice(first + 4, first + 8), slice(start, start + 4), slice(first, first + 4)
        o_ref[0, to, 4:20] = edge[0, part]
        o_ref[1, to, 8:16] = edge[1, part, 4:12] + edge_courant[part, 4:12] * own[0, x]
        o_ref[1, to, 4:8] = edge[1, part, 0:4] + edge_courant[part, 0:4] * rim_y[x, 0:4]
        o_ref[1, to, 16:20] = edge[1, part, 12:16] + edge_courant[part, 12:16] * rim_y[x, 4:8]
    for half in range(2):
        to = slice(8 + 16 * half, 16 + 16 * half)
        for f in range(2):
            o_ref[f, to, 4:20] = inner[f, 8 * half : 8 * half + 8]
    source_x = source_layer(source_cell)
    pulses = [pulse(source_cell, wavelet, 0, row) for row in (-4, 4, 0)]
    for side, ref, keep in ((0, left, keep_left), (1, right, keep_right)):
        beyond_depths = (ref[28] * keep).astype(I32)
        for f in range(2):
            h_ref[f, side, :, 4:12] = ref[12 + 4 * f : 16 + 4 * f] * keep
            h_ref[f, side, :, 0:4] = ref[20 + 4 * f : 24 + 4 * f, 0:4] * keep
            h_ref[f, side, :, 12:16] = ref[20 + 4 * f : 24 + 4 * f, 4:8] * keep
        for n in range(4):
            x = 31 - n if side else n
            for f in range(2):
                for t in range(2):
                    rows = slice(8 * t, 8 * t + 8)
                    amount = None
                    for reach in range(n + 1, 5):
                        away = reach - n
                        term = COEFS[reach] * h_ref[f, side, away - 1 if side else 4 - away, rows]
                        amount = term if amount is None else amount + term
                    if f == 0:
                        amount = amount - jnp.where(x == source_x, pulses[t], 0.0)
                    amount = edge_courant[x - 24 if side else x, rows] * amount
                    if f == 0:
                        amount = unless_strip(depths[rows], x, amount)
                    at = slice(4 + 8 * t, 12 + 8 * t)
                    o_ref[f, x + 4, at] = o_ref[f, x + 4, at] + amount
            k = n if side else 3 - n
            for f, field in ((0, s0), (1, r0)):
                amount = None
                for reach in range(n + 1, 5):
                    inward = reach - n - 1
                    term = COEFS[reach] * field[31 - inward if side else inward]
                    amount = term if amount is None else amount + term
                if f == 0:
                    beyond = 32 + n if side else -1 - n
                    amount = amount - jnp.where(beyond == source_x, pulses[2], 0.0)
                else:
                    amount = amount + rim_x[4 * side + k]
                amount = ref[8 + k] * amount
                if f == 0:
                    amount = unless_strip(beyond_depths, k if side else 28 + k, amount)
                o_ref[f, 36 + n if side else 3 - n, 8:16] = (ref[4 * f + k] + amount) * keep
    matrix = depth_matrix()
    for f in range(2):
        for half in range(2):
            rows = o_ref[f, 4 + 24 * half : 12 + 24 * half, 8:16].reshape(64, 128)
            z_ref[f, 8 * half : 8 * half + 8] = depth_sums(rows, matrix).reshape(8, 8, 128)
    late_values = strip_values_tile(values, 1, slice(0, 8))
    near_depth = wide(depth[...])
    late_pulse = pulse(source_cell, wavelet, 1, 0)
    for k in range(4):
        for j in range(2):
            sub_ref[k, j, 8:24] = sub_mid[k, j]
    for i in range(16):
        x = i if i < 8 else i + 16
        late_layer(
            x, x + 4, i, o_ref, z_ref, s0, r0, c, own,
            near_depth, late_values, late_pulse, source_x, s_v, r_v, sub_ref, x,
        )
    z, to = iota((TZ, 128), 0), iota((TZ, 128), 1)
    totals = []
    for k in range(4):
        total = None
        for j in range(2):
            pick = jnp.where((z & 3 == 0) & (to == (z >> 2) + (16 + 64 * j)), 1.0, 0.0)
            part = jnp.dot(
                sub_ref[k, j], pick, precision=lax.Precision.HIGHEST, preferred_element_type=F32
            )
            total = part if total is None else total + part
        near_ref[k] = total
        totals.append(total)
    for f in range(2):
        packed = totals[2 * f] + pltpu.roll(totals[2 * f + 1], 32, 1)
        up_ref[f] = packed[16:32]
        down_ref[f] = packed[0:16]


def store_kernel(s_mid, r_mid, s_edge, r_edge, s_out, r_out, sems):
    ends = [
        pair
        for mid, edge, to in ((s_mid, s_edge, s_out), (r_mid, r_edge, r_out))
        for pair in ((mid, to.at[8:24]), (edge.at[0:8], to.at[0:8]), (edge.at[8:16], to.at[24:32]))
    ]
    for copy in started(ends, sems):
        copy.wait()


def angles_kernel(stored, near, left, right, out_ref, g_ref):
    keep_left, keep_right = keeps("gx", GX)
    lane = iota((16, 128), 1)
    held = ((lane >= 16) & (lane < 48)) | ((lane >= 80) & (lane < 112))
    for f in range(2):
        for ref, keep, rows in ((left, keep_left, slice(0, 16)), (right, keep_right, slice(48, 64))):
            packed = ref[f] * keep
            g_ref[2 * f, rows] = jnp.where(held, packed, 0.0)
            g_ref[2 * f + 1, rows] = jnp.where(held, pltpu.roll(packed, 96, 1), 0.0)
    for k in range(4):
        g_ref[k, 16:48] = near[k]
    sums = [None] * 32
    for lag in range(-16, 17):
        product = None
        for step in range(2):
            source = g_ref[step, pl.ds(16 - lag, 8, stride=4)]
            receiver = g_ref[2 + step, pl.ds(16 + lag, 8, stride=4)]
            part = source * receiver
            product = part if product is None else product + part
        shifted = {}

        def shift(amount):
            if amount not in shifted:
                shifted[amount] = product if amount == 0 else pltpu.roll(product, -amount % 128, 1)
            return shifted[amount]

        for a in range(32):
            move = np.float32(lag) * SLOPES[a] / np.float32(4.0)
            low = np.floor(move)
            frac = float(move - low)
            term = shift(int(low)) * (1.0 - frac)
            if frac != 0.0:
                term = term + shift(int(low) + 1) * frac
            sums[a] = term if sums[a] is None else sums[a] + term
    lane = iota((8, 128), 1)
    for b in range(16):
        first, second = sums[2 * b], sums[2 * b + 1]
        packed = jnp.where(lane < 32, pltpu.roll(first, 112, 1), pltpu.roll(first, 80, 1))
        other = jnp.where(lane < 96, pltpu.roll(second, 48, 1), pltpu.roll(second, 16, 1))
        out_ref[b] = jnp.where(lane < 64, packed, other)


def arrange_kernel(got, image, out_v, sems):
    lane = iota((8, 128), 1)
    copies = []
    for a in range(2):
        for t in range(8):
            even, odd = got[2 * t], got[2 * t + 1]
            if a == 0:
                odd = pltpu.roll(odd, 64, 1)
            else:
                even = pltpu.roll(even, 64, 1)
            out_v[a, :, 128 * t : 128 * t + 128] = jnp.where(lane < 64, even, odd)
        copies.append(pltpu.make_async_copy(out_v.at[a], image.at[a], sems.at[a]))
        copies[a].start()
    for copy in copies:
        copy.wait()


def call(kernel, outs, arrays, scalars=(), hbm=(), out_scalars=0, out_hbm=(), scratch=(), weight=0):
    smem, vmem = pl.BlockSpec(memory_space=pltpu.SMEM), pl.BlockSpec(memory_space=pltpu.VMEM)
    far = pl.BlockSpec(memory_space=pltpu.HBM)
    hbm = [
        pltpu.with_memory_space_constraint(array, pltpu.HBM) for array in hbm
    ]
    return pl.pallas_call(
        kernel,
        out_shape=[jax.ShapeDtypeStruct(shape, kind) for shape, kind in outs],
        in_specs=[smem] * len(scalars) + [far] * len(hbm) + [vmem] * len(arrays),
        out_specs=[
            smem if k >= len(outs) - out_scalars else far if k in out_hbm else vmem for k in range(len(outs))
        ],
        scratch_shapes=list(scratch),
        compiler_params=pltpu.CompilerParams(vmem_limit_bytes=VMEM_LIMIT),
        cost_estimate=pl.CostEstimate(flops=0, bytes_accessed=weight, transcendentals=0) if weight else None,
    )(*scalars, *hbm, *arrays)


def both_ways(to_next, to_last, axis):
    size = lax.axis_size(axis)
    from_last = lax.ppermute(to_next, axis, [(i, (i + 1) % size) for i in range(size)])
    from_next = lax.ppermute(to_last, axis, [((i + 1) % size, i) for i in range(size)])
    return from_last, from_next


def body(
    source_now,
    source_next,
    receiver_now,
    receiver_next,
    courant,
    source_cell,
    wavelet,
    receiver_cells,
    receiver_traces,
    strip_depth,
    strip_values,
):
    cells = receiver_cells.reshape(1, RECEIVERS)
    near_cell = source_cell.reshape(1, 1)
    tile, sent_shape = (TX, TY, TZ), ((DEVICES, 1, 128), F32)
    listed = [((1, RECEIVERS), I32), ((2, RECEIVERS), F32)]
    fields = (source_now, receiver_now, source_next, receiver_next, courant, strip_depth, strip_values)
    first_y, second_y, near_wavelet, near_sm, near_rm, near_c, near_depth, near_values, sent = call(
        pack_kernel,
        [((113, 8, 128), F32)] * 2
        + [((1, 2), F32), *[(tile, F32)] * 3, ((8, 32), I32), ((2, 4, 8, 32), F32), sent_shape],
        [],
        hbm=[cells, receiver_traces, wavelet.reshape(1, 2), *fields],
        out_hbm=(8,),
        scratch=[pltpu.VMEM(*shape) for shape in (sent_shape, *listed)] + [pltpu.SemaphoreType.DMA((13,))],
    )
    pairs = [(i, i ^ 1) for i in range(GY)]
    first = lax.ppermute(first_y, "gy", pairs)
    second = lax.ppermute(second_y, "gy", [(i, (i + 1 if i % 2 else i - 1) % GY) for i in range(GY)])
    got = lax.all_to_all(sent, ("gx", "gy"), 0, 0, tiled=True)
    got = jnp.maximum(got.reshape(DEVICES, 128), -jnp.finfo(F32).max)
    edge, edge_courant, depths, strips, up_x, down_x = call(
        edge_kernel,
        [((2, 8, 16, 128), F32), ((8, 16, 128), F32), ((16, 128), I32), ((16, 128), F32)]
        + [((29, 8, 128), F32)] * 2,
        [first_y, near_sm, near_rm, near_c, near_depth, near_values, first, second],
        scratch=[
            pltpu.VMEM((2, 24, 32, 128), F32),
            pltpu.VMEM((2, 8, 16, 128), F32),
            pltpu.VMEM((2, 8, 16, 128), F32),
        ],
    )
    left, right = both_ways(up_x, down_x, "gx")
    inner, inner_courant = call(
        inner_kernel,
        [((2, 24, 16, 128), F32), ((24, 16, 128), F32)],
        [first_y, near_sm, near_rm, near_c, first, second, depths, strips],
        scratch=[
            pltpu.VMEM((2, 32, 32, 128), F32),
            pltpu.VMEM((2, 24, 16, 128), F32),
            pltpu.VMEM((2, 24, 16, 128), F32),
        ],
    )
    sums = [((2, *tile), F32), (tile, F32), ((8, 8, 128), F32)]
    own, rim_y, rim_x, rounds = call(collect_kernel, [*sums, ((1,), I32)], [got, inner_courant], out_scalars=1, weight=1000)

    def another(state):
        left_over, *partial = state
        (more,) = call(
            route_more_kernel,
            [sent_shape],
            [],
            scalars=[(left_over - 1) * SLOTS],
            hbm=[cells, receiver_traces],
            scratch=[pltpu.VMEM(*shape) for shape in listed] + [pltpu.SemaphoreType.DMA((2,))],
        )
        more = lax.all_to_all(more, ("gx", "gy"), 0, 0, tiled=True)
        return (left_over - 1, *call(collect_more_kernel, sums, [more, *partial]))

    _, own, rim_y, rim_x = lax.while_loop(
        lambda state: state[0][0] > 1, another, (rounds, own, rim_y, rim_x)
    )
    part = (16, TY, TZ)
    new1, s_mid, r_mid, sub_mid = call(
        middle_kernel,
        [((2, 16, 16, 128), F32), (part, F32), (part, F32), ((4, 2, 16, 128), F32)],
        [
            near_cell, near_wavelet, first_y, near_c, near_depth, near_values, inner, inner_courant, depths, own, rim_y,
        ],
        scratch=[pltpu.VMEM((2, 24, 24, 128), F32), pltpu.VMEM((2, 16, 8, 128), F32)],
    )
    s_edge, r_edge, near, up, down = call(
        steps_kernel,
        [(part, F32), (part, F32), ((4, 32, 128), F32), ((2, 16, 128), F32), ((2, 16, 128), F32)],
        [
            near_cell, near_wavelet, first_y, near_c, near_depth, near_values, left, right, edge, edge_courant,
            depths, own, rim_y, rim_x, new1, sub_mid,
        ],
        scratch=[
            pltpu.VMEM((2, 40, 24, 128), F32),
            pltpu.VMEM((2, 2, 4, 16, 128), F32),
            pltpu.VMEM((2, 16, 8, 128), F32),
            pltpu.VMEM((4, 2, 32, 128), F32),
        ],
    )
    near_left, near_right = both_ways(up, down, "gx")
    source_field, receiver_field = call(
        store_kernel,
        [(tile, F32), (tile, F32)],
        [s_mid, r_mid, s_edge, r_edge],
        out_hbm=(0, 1),
        scratch=[pltpu.SemaphoreType.DMA((6,))],
        weight=1_000_000,
    )
    (angles,) = call(
        angles_kernel, [((16, 8, 128), F32)], [near, near_left, near_right], hbm=[source_field],
        scratch=[pltpu.VMEM((4, 64, 128), F32)],
    )
    angles = lax.all_to_all(angles, "gy", 0, 0, tiled=True)
    image_shape = ((2, 8, 1024), F32)
    (image,) = call(
        arrange_kernel,
        [image_shape],
        [angles],
        out_hbm=(0,),
        scratch=[pltpu.VMEM(*image_shape), pltpu.SemaphoreType.DMA((2,))],
    )
    return source_field, receiver_field, image


def solution(mesh):
    return jax.shard_map(
        body,
        mesh=mesh,
        in_specs=(
            P("gx", "gy", None),
            P("gx", "gy", None),
            P("gx", "gy", None),
            P("gx", "gy", None),
            P("gx", "gy", None),
            P(),
            P(),
            P(("gx", "gy")),
            P(None, ("gx", "gy")),
            P("gy", "gx"),
            P(None, None, "gy", "gx"),
        ),
        out_specs=(P("gx", "gy", None), P("gx", "gy", None), P("gy", "gx", None)),
        check_vma=False,
    )
```
